32 devices in a mesh: wide: 16 (over z, y, core), pair: 2 (over x).
Axes of the slice: x: 2, y: 2, z: 4, core: 2. Of those that a mesh axis runs over, the one named last changes fastest.
Arguments:
- queries: bfloat16 [2, 16, 2, 8192], P('pair', 'wide'), may hold values from -200 to 200
- cache: bfloat16 [2, 16, 512, 2, 1024], P('pair', 'wide'), may hold values from -10 to 10
- fresh_key_value: bfloat16 [2, 16, 2, 2, 1024], P('pair', 'wide'), may hold values from -15 to 15
- lengths: int32 [2, 16], P('pair', 'wide'), may hold values from 64 to 510, as said below
- residual: bfloat16 [2, 16, 2, 8192], P('pair', 'wide'), may hold values from -10 to 10
- norm_gain: float32 [8192], replicated, may hold values from 0.5 to 1.5
- vocab_weight: bfloat16 [8192, 4096], P('pair', 'wide'), may hold values from -0.5 to 0.5
- guidance: float32 [16], replicated, may hold values from 2 to 5
- allowed_blocks: int32 [2, 16, 128], P(None, 'pair', 'wide'), may hold values from 0 to 1, as said below
- sampled: int32 [2, 16], P(None, 'pair'), may hold values from 0 to 4095
Outputs:
- guided_logprobs: float32 [2, 16, 4096], P(None, 'pair', 'wide')
- token_logprobs: float32 [2, 16], P(None, 'pair')
The draws below stay inside these ranges and needn't reach their ends.
Inputs may be any that keep to these rules, and one draw needn't show every extreme that they name: `lengths`: the longest row holds exactly 510 live slots. `allowed_blocks`: the block of each sampled id is allowed.
All inputs are finite; a program needn't handle non-finite values.
Results may differ from the reference program's by a relative error of at most 0.0022.
Values may be sent and summed in bfloat16 or wider, within the bound.
No kernel may reach another device: no remote copies, remote signals or barrier semaphores. Data moves between devices by JAX's collectives and lax.ppermute only.
A program may use at most 64 MiB of HBM per device.

```python
import math
import jax
import jax.numpy as jnp
from jax import lax

D = 8192
QUERY_HEADS = 64
KEY_VALUE_HEADS = 8
HEAD_SIZE = 128
BLK = 32
DECODE_STEPS = 2
CACHE_SLOTS = 512
GUIDED_PAIRS = 16
VOCAB = 4096
NBLK = 128


def shared_keys(key):
    return jax.random.normal(jax.random.fold_in(key, 101), (2, GUIDED_PAIRS, KEY_VALUE_HEADS * HEAD_SIZE), jnp.float32)


def grammar_state(key):
    base_offset = jax.random.fold_in(key, 303)
    chosen = jax.random.randint(base_offset, (DECODE_STEPS, GUIDED_PAIRS), 0, VOCAB)
    bits = jax.random.randint(jax.random.fold_in(base_offset, 1), (DECODE_STEPS, GUIDED_PAIRS, NBLK), 0, 2)
    block_ids = jnp.arange(NBLK)
    hit = (block_ids[None, None, :] == (chosen // BLK)[:, :, None]).astype(jnp.int32)
    return (chosen, jnp.maximum(bits, hit))


def draw_cache(key, part):
    base_offset = shared_keys(key)
    key = jax.random.fold_in(key, 1)
    field_list = jax.random.normal(key, (2, GUIDED_PAIRS, CACHE_SLOTS, 2, KEY_VALUE_HEADS * HEAD_SIZE), jnp.float32)
    second = field_list[:, :, 1, 0]
    key_rows = jnp.concatenate([base_offset[:, :, None], second[:, :, None], field_list[:, :, 2:, 0]], axis=2)
    stacked = jnp.stack([key_rows, field_list[:, :, :, 1]], axis=3)
    return jnp.clip(stacked, -10.0, 10.0).astype(jnp.bfloat16)


def draw_queries(key, part):
    key = jax.random.fold_in(key, 2)
    value_rows = jax.random.normal(key, (2, GUIDED_PAIRS, DECODE_STEPS, QUERY_HEADS * HEAD_SIZE), jnp.float32)
    return jnp.clip(value_rows, -200.0, 200.0).astype(jnp.bfloat16)


def draw_lengths(key, part):
    key = jax.random.fold_in(key, 11)
    lowest = CACHE_SLOTS // 8
    highest = CACHE_SLOTS - 2
    ticks = jax.random.randint(key, (2 * GUIDED_PAIRS,), 0, 64)
    spread = lowest + (highest - lowest) * (ticks * ticks * ticks) // (63 * 63 * 63)
    spot = jax.random.randint(jax.random.fold_in(key, 12), (), 0, 2 * GUIDED_PAIRS)
    spread = jnp.where(jnp.arange(2 * GUIDED_PAIRS) == spot, highest, spread)
    return spread.reshape(2, GUIDED_PAIRS).astype(jnp.int32)


def draw_residual(key, part):
    key = jax.random.fold_in(key, 6)
    value_rows = 0.1 * jax.random.normal(key, (2, GUIDED_PAIRS, DECODE_STEPS, D), jnp.float32)
    return jnp.clip(value_rows, -10.0, 10.0).astype(jnp.bfloat16)


def draw_vocab_weight(key, part):
    key = jax.random.fold_in(key, 9)
    columns = jnp.arange(VOCAB).astype(jnp.float32)
    jitter = jax.random.uniform(jax.random.fold_in(key, 10), (VOCAB,), jnp.float32, -0.6, 0.6)
    ramp = jnp.power(3.0, columns / VOCAB) * jnp.exp(jitter)
    value_rows = jax.random.normal(key, (D, VOCAB), jnp.float32) * D ** (-0.5) * ramp[None, :]
    return jnp.clip(value_rows, -0.5, 0.5).astype(jnp.bfloat16)


def draw_allowed_blocks(key, part):
    chosen, bits = grammar_state(key)
    return bits.astype(jnp.int32)


def draw_sampled(key, part):
    chosen, bits = grammar_state(key)
    return chosen.astype(jnp.int32)


def levels(stream_key, dims, shards, low, top_value):
    gain, own = 1.0, jax.random.fold_in(stream_key, 6)
    for position, parts in shards:
        heights = jnp.exp(jax.random.uniform(jax.random.fold_in(own, position), (parts,), jnp.float32, low / len(shards), top_value / len(shards)))
        gain = gain * jnp.repeat(heights, dims[position] // parts).reshape([-1 if axis == position else 1 for axis in range(len(dims))])
    return gain


def centred(stream_key, dims, scale, limit, cuts=(), kind=jnp.bfloat16):
    values = jax.random.normal(stream_key, dims, jnp.float32) * scale
    if len(cuts) > 0:
        values = levels(stream_key, dims, cuts, -0.22, 0.18) * values
    return jnp.clip(values, min=-limit, max=limit).astype(kind)


def setup_inputs(seed: int = 0) -> dict:
    streams_of = jax.random.split(jax.random.key(seed), 11)
    queries = draw_queries(jax.random.fold_in(streams_of[10], 71), 0)
    cache = draw_cache(jax.random.fold_in(streams_of[10], 71), 0)
    fresh_key_value = centred(streams_of[2], (2, GUIDED_PAIRS, DECODE_STEPS, 2, KEY_VALUE_HEADS * HEAD_SIZE), 2.5, 15.0, ((0, 2), (1, 16)))
    lengths = draw_lengths(jax.random.fold_in(streams_of[10], 71), 0)
    residual = draw_residual(jax.random.fold_in(streams_of[10], 71), 0)
    norm_gain = jnp.clip(1.0 + 0.1 * jax.random.normal(streams_of[5], (D,), jnp.float32), 0.5, 1.5)
    vocab_weight = draw_vocab_weight(jax.random.fold_in(streams_of[10], 71), 0)
    guidance = jnp.clip(jax.random.uniform(streams_of[7], (GUIDED_PAIRS,), jnp.float32, 2.0, 5.0), 2.0, 5.0)
    allowed_blocks = draw_allowed_blocks(jax.random.fold_in(streams_of[10], 71), 0)
    sampled = draw_sampled(jax.random.fold_in(streams_of[10], 71), 0)
    return {"queries": queries, "cache": cache, "fresh_key_value": fresh_key_value, "lengths": lengths, "residual": residual, "norm_gain": norm_gain, "vocab_weight": vocab_weight, "guidance": guidance, "allowed_blocks": allowed_blocks, "sampled": sampled}


def attend_row(row_of_query, row_of_cache, row_of_fresh, length):
    query_group = QUERY_HEADS // KEY_VALUE_HEADS
    factor = 1.0 / math.sqrt(HEAD_SIZE)
    key_rows = row_of_cache[:, 0].reshape(CACHE_SLOTS, KEY_VALUE_HEADS, HEAD_SIZE).astype(jnp.float32)
    value_rows = row_of_cache[:, 1].reshape(CACHE_SLOTS, KEY_VALUE_HEADS, HEAD_SIZE).astype(jnp.float32)
    appended_keys = row_of_fresh[:, 0].reshape(DECODE_STEPS, KEY_VALUE_HEADS, HEAD_SIZE).astype(jnp.float32)
    appended_values = row_of_fresh[:, 1].reshape(DECODE_STEPS, KEY_VALUE_HEADS, HEAD_SIZE).astype(jnp.float32)
    live = jnp.arange(CACHE_SLOTS).astype(jnp.int32) < length
    outputs = []
    for index_of_step in range(DECODE_STEPS):
        query_vector = row_of_query[index_of_step].reshape(KEY_VALUE_HEADS, query_group, HEAD_SIZE).astype(jnp.float32)
        old = jnp.einsum('kgd,ckd->kgc', query_vector, key_rows) * factor
        old = jnp.where(live[None, None, :], old, -jnp.inf)
        new = jnp.einsum('kgd,skd->kgs', query_vector, appended_keys[:index_of_step + 1]) * factor
        top = jnp.maximum(lax.optimization_barrier(jnp.max(old, axis=-1)), lax.optimization_barrier(jnp.max(new, axis=-1)))
        old_weight = jnp.exp(old - top[..., None])
        new_weight = jnp.exp(new - top[..., None])
        total = lax.optimization_barrier(jnp.sum(old_weight, axis=-1)) + lax.optimization_barrier(jnp.sum(new_weight, axis=-1))
        old_weight = lax.optimization_barrier((old_weight / total[..., None]).astype(jnp.bfloat16))
        new_weight = lax.optimization_barrier((new_weight / total[..., None]).astype(jnp.bfloat16))
        mixed = jnp.einsum('kgc,ckd->kgd', old_weight.astype(jnp.float32), value_rows)
        mixed = mixed + jnp.einsum('kgs,skd->kgd', new_weight.astype(jnp.float32), appended_values[:index_of_step + 1])
        outputs.append(mixed.reshape(QUERY_HEADS * HEAD_SIZE))
    return jnp.stack(outputs)

def reference(queries, cache, fresh_key_value, lengths, residual, norm_gain, vocab_weight, guidance, allowed_blocks, sampled):
    count_of_rows = 2 * GUIDED_PAIRS
    flat_queries = queries.reshape(count_of_rows, DECODE_STEPS, QUERY_HEADS * HEAD_SIZE)
    flattened_cache = cache.reshape(count_of_rows, CACHE_SLOTS, 2, KEY_VALUE_HEADS * HEAD_SIZE)
    flattened_fresh = fresh_key_value.reshape(count_of_rows, DECODE_STEPS, 2, KEY_VALUE_HEADS * HEAD_SIZE)
    flat_lengths = lengths.reshape(count_of_rows).astype(jnp.int32)
    attended = lax.map(lambda packed: attend_row(packed[0], packed[1], packed[2], packed[3]), (flat_queries, flattened_cache, flattened_fresh, flat_lengths))
    hidden = residual.reshape(count_of_rows, DECODE_STEPS, D).astype(jnp.float32) + attended
    power = lax.optimization_barrier(jnp.mean(hidden * hidden, axis=-1, keepdims=True))
    normed = (hidden * lax.rsqrt(power + 1e-05) * norm_gain).astype(jnp.bfloat16)
    logprob_list = []
    token_list = []
    for index_of_step in range(DECODE_STEPS):
        logits = jnp.dot(normed[:, index_of_step], vocab_weight, preferred_element_type=jnp.float32)
        logits = logits.reshape(2, GUIDED_PAIRS, VOCAB)
        guided = logits[1] + guidance[:, None] * (logits[0] - logits[1])
        blocks = allowed_blocks[index_of_step]
        allowed = jnp.broadcast_to(blocks[:, :, None] > 0, (GUIDED_PAIRS, NBLK, BLK)).reshape(GUIDED_PAIRS, VOCAB)
        top = lax.optimization_barrier(jnp.max(jnp.where(allowed, guided, -jnp.inf), axis=-1))
        total = lax.optimization_barrier(jnp.sum(jnp.where(allowed, jnp.exp(guided - top[:, None]), 0.0), axis=-1))
        normalizer = top + jnp.log(total)
        logprob_list.append(jnp.where(allowed, guided - normalizer[:, None], 0.0))
        chosen = jnp.take_along_axis(guided, sampled[index_of_step][:, None].astype(jnp.int32), axis=1)[:, 0]
        token_list.append(chosen - normalizer)
    return (jnp.stack(logprob_list), jnp.stack(token_list))
```

```python
import functools
import math

import jax
import jax.numpy as jnp
from jax import lax
from jax.experimental import pallas as pl
from jax.experimental.pallas import tpu as pltpu
from jax.sharding import PartitionSpec as P

QUERY_HEADS = 64
KEY_VALUE_HEADS = 8
HEAD_SIZE = 128
BLK = 32
DECODE_STEPS = 2
HEAD_ROWS = DECODE_STEPS * (QUERY_HEADS // KEY_VALUE_HEADS)
NEG_FILL = -1e30
BLOCKS = 4


def in_vmem():
    return pl.BlockSpec(memory_space=pltpu.VMEM)


def in_smem():
    return pl.BlockSpec(memory_space=pltpu.SMEM)


def call(kernel, out_shape, in_specs, scratch=(), limit=16 << 20, cost=None):
    return pl.pallas_call(
        kernel,
        out_shape=out_shape,
        in_specs=in_specs,
        out_specs=jax.tree.map(lambda _: in_vmem(), out_shape),
        scratch_shapes=list(scratch),
        compiler_params=pltpu.CompilerParams(vmem_limit_bytes=limit),
        cost_estimate=cost,
    )


def attend_kernel(
    lengths, queries_in, cache, fresh_in, residual_in, gain_in, mine, theirs,
    slots, gain_rows, queries, residual, gain, arrived,
):
    count = cache.shape[0]
    first_fresh = count - DECODE_STEPS
    small = [
        pltpu.make_async_copy(source, target, arrived.at[index])
        for index, (source, target) in enumerate(((queries_in, queries), (residual_in, residual), (gain_in, gain)))
    ]
    block = count // BLOCKS
    pieces = [
        [
            pltpu.make_async_copy(
                cache.at[pl.ds(part * block, size), head],
                slots.at[head, pl.ds(part * block, size)],
                arrived.at[len(small) + part * KEY_VALUE_HEADS + head],
            )
            for head in range(KEY_VALUE_HEADS)
        ]
        for part, size in enumerate([block] * (BLOCKS - 1) + [block - DECODE_STEPS])
    ]
    pieces[-1] += [
        pltpu.make_async_copy(
            fresh_in.at[:, head],
            slots.at[head, pl.ds(first_fresh, DECODE_STEPS)],
            arrived.at[len(small) + BLOCKS * KEY_VALUE_HEADS + head],
        )
        for head in range(KEY_VALUE_HEADS)
    ]
    small[0].start()
    for part in pieces:
        for copy in part:
            copy.start()
    small[1].start()
    small[2].start()
    small[0].wait()

    query_rows = queries.shape[0]
    head_of_row = lax.broadcasted_iota(jnp.int32, queries.shape, 0) // HEAD_ROWS
    wide_queries = queries[...].astype(jnp.float32)
    of_head = [
        jnp.where(head_of_row == head, wide_queries, 0.0).astype(jnp.bfloat16) for head in range(KEY_VALUE_HEADS)
    ]
    of_two = [jnp.concatenate(of_head[head : head + 2], axis=1) for head in range(0, KEY_VALUE_HEADS, 2)]
    interleaved = [slots.at[head].reshape(2 * count, HEAD_SIZE) for head in range(KEY_VALUE_HEADS)]
    parts = []
    for part, copies in enumerate(pieces):
        for copy in copies:
            copy.wait()
        rows = pl.ds(part * 2 * block, 2 * block)
        total = jnp.zeros((2 * block, query_rows), jnp.float32)
        for two, heads in enumerate(of_two):
            keys = jnp.concatenate([interleaved[2 * two][rows, :], interleaved[2 * two + 1][rows, :]], axis=1)
            total = total + lax.dot_general(
                keys, heads, (((1,), (1,)), ((), ())), preferred_element_type=jnp.float32
            )
        parts.append(total)
    score = jnp.concatenate(parts, axis=0)
    row = lax.broadcasted_iota(jnp.int32, score.shape, 0)
    step_of_query = lax.rem(lax.broadcasted_iota(jnp.int32, score.shape, 1), DECODE_STEPS)
    live = (row < 2 * lengths[0, 0]) | ((row >= 2 * first_fresh) & (row - 2 * first_fresh <= 2 * step_of_query))
    live = live & (lax.rem(row, 2) == 0)
    score = jnp.where(live, score * (1.0 / math.sqrt(HEAD_SIZE)), NEG_FILL)
    weight = jnp.exp(score - jnp.max(score, axis=0, keepdims=True))
    weight = weight * (1.0 / jnp.sum(weight, axis=0, keepdims=True))
    weight = pltpu.roll(weight, 1, 0).T.astype(jnp.bfloat16)
    mixed = [
        jnp.dot(
            weight[head * HEAD_ROWS : (head + 1) * HEAD_ROWS],
            interleaved[head][...],
            preferred_element_type=jnp.float32,
        )
        for head in range(KEY_VALUE_HEADS)
    ]
    for copy in small[1:]:
        copy.wait()
    gain_rows[pl.ds(0, QUERY_HEADS, stride=2), :] = gain[...]
    gain_rows[pl.ds(1, QUERY_HEADS, stride=2), :] = gain[...]
    hidden = jnp.concatenate(mixed, axis=0) + residual[...].astype(jnp.float32)
    row_power = jnp.sum(hidden * hidden, axis=1, keepdims=True)
    step_of_row = lax.rem(lax.broadcasted_iota(jnp.int32, row_power.shape, 0), DECODE_STEPS)
    scale = jnp.zeros_like(row_power)
    for step in range(DECODE_STEPS):
        power = jnp.sum(jnp.where(step_of_row == step, row_power, 0.0), axis=0, keepdims=True)
        power = power / (QUERY_HEADS * HEAD_SIZE)
        scale = jnp.where(step_of_row == step, lax.rsqrt(power + 1e-05), scale)
    normed = (hidden * scale * gain_rows[...]).astype(jnp.bfloat16)
    half = normed.shape[0] // 2
    first = lax.axis_index("pair") == 0
    mine[...] = jnp.where(first, normed[:half], normed[half:])
    theirs[...] = jnp.where(first, normed[half:], normed[:half])


def branch_factor(scale, branch):
    guidance = scale[lax.axis_index("wide")]
    return jnp.where(branch == 0, guidance, 1.0 - guidance)


def own_part_kernel(scale, mine, out, factor):
    branch = lax.axis_index("pair")
    out[...] = branch_factor(scale, branch) * mine[...].astype(jnp.float32)
    factor[...] = jnp.full(factor.shape, branch_factor(scale, 1 - branch), jnp.float32)


def combine_kernel(factor, own_part, received, spread):
    other_part = factor[0:1, :] * received[...].astype(jnp.float32)
    guided = (own_part[...] + other_part).astype(jnp.bfloat16)
    spread[...] = jnp.broadcast_to(guided[None], spread.shape)


def project_kernel(rows, weight, mine, theirs, wide_rows):
    pairs, per_pair, lanes = rows.shape
    half = pairs // 2
    for pair in range(pairs):
        wide_rows[pl.ds(pair * per_pair, per_pair), :] = rows[pair].astype(jnp.float32)

    def head_rows(head):
        steps = [
            wide_rows[pl.ds(head * DECODE_STEPS + step, pairs, stride=per_pair), :]
            for step in range(DECODE_STEPS)
        ]
        return jnp.concatenate(
            [rows_of_step[part * half : (part + 1) * half] for part in range(2) for rows_of_step in steps], axis=0
        ).astype(jnp.bfloat16)

    total = jnp.zeros((DECODE_STEPS * pairs, mine.shape[1]), jnp.float32)
    for two in range(per_pair // DECODE_STEPS // 2):
        left = jnp.concatenate([head_rows(2 * two), head_rows(2 * two + 1)], axis=1)
        total = total + jnp.dot(
            left, weight[pl.ds(two * 2 * lanes, 2 * lanes), :], preferred_element_type=jnp.float32
        )
    first = lax.axis_index("pair") == 0
    low, high = total[: mine.shape[0]], total[mine.shape[0] :]
    mine[...] = jnp.where(first, low, high)
    theirs[...] = jnp.where(first, high, low)


def to_lanes(column):
    size = column.shape[0]
    eye = lax.broadcasted_iota(jnp.int32, (size, size), 0) == lax.broadcasted_iota(jnp.int32, (size, size), 1)
    return jnp.sum(jnp.where(eye, column, jnp.zeros_like(column)), axis=0, keepdims=True)


def to_column(lanes):
    size = lanes.shape[1]
    eye = lax.broadcasted_iota(jnp.int32, (size, size), 0) == lax.broadcasted_iota(jnp.int32, (size, size), 1)
    return jnp.sum(jnp.where(eye, lanes, jnp.zeros_like(lanes)), axis=1, keepdims=True)


def allowed_entries(blocks, shape):
    half = blocks.shape[1]
    flags = jnp.concatenate([blocks[step] for step in range(DECODE_STEPS)], axis=0)
    block = lax.broadcasted_iota(jnp.int32, shape, 1) // BLK
    flag = jnp.zeros(shape, jnp.int32)
    for index in range(blocks.shape[2]):
        flag = jnp.where(block == index, flags[:, index : index + 1], flag)
    return flag > 0


def stats_kernel(mine, received, blocks, sampled, guided_out, stats):
    guided = mine[...] + received[...]
    guided_out[...] = guided
    count, width = guided.shape
    half = count // DECODE_STEPS
    allowed = allowed_entries(blocks, guided.shape)
    top = jnp.max(jnp.where(allowed, guided, NEG_FILL), axis=1, keepdims=True)
    total = jnp.sum(jnp.where(allowed, jnp.exp(guided - top), 0.0), axis=1, keepdims=True)
    chosen = jnp.concatenate([to_column(sampled[pl.ds(step, 1), :]) for step in range(DECODE_STEPS)], axis=0)
    column = lax.broadcasted_iota(jnp.int32, guided.shape, 1) + lax.axis_index("wide") * width
    picked = jnp.sum(jnp.where(column == chosen, guided, 0.0), axis=1, keepdims=True)
    lanes = jnp.concatenate([to_lanes(top), to_lanes(total), to_lanes(picked)], axis=1)
    pad = stats.shape[2] - lanes.shape[1]
    if pad > 0:
        lanes = jnp.concatenate([lanes, jnp.zeros((1, pad), jnp.float32)], axis=1)
    stats[...] = jnp.broadcast_to(lanes[None], stats.shape)


def finish_kernel(guided, stats, blocks, logprobs, tokens):
    count, width = guided.shape
    half = count // DECODE_STEPS
    parts = stats[...].reshape(stats.shape[0], stats.shape[2])
    tops = parts[:, 0:count]
    top = jnp.max(tops, axis=0, keepdims=True)
    total = jnp.sum(parts[:, count : 2 * count] * jnp.exp(tops - top), axis=0, keepdims=True)
    picked = jnp.sum(parts[:, 2 * count : 3 * count], axis=0, keepdims=True)
    normalizer = top + jnp.log(total)
    token = picked - normalizer
    for step in range(DECODE_STEPS):
        tokens[pl.ds(step, 1), :] = token[:, step * half : (step + 1) * half]
    allowed = allowed_entries(blocks, guided.shape)
    result = jnp.where(allowed, guided[...] - to_column(normalizer), 0.0)
    logprobs[...] = result.reshape(logprobs.shape)


def by_head(array):
    return array.reshape(array.shape[0], 2, KEY_VALUE_HEADS, HEAD_SIZE).transpose(0, 2, 1, 3)


def step_rows(array):
    split = array.reshape(DECODE_STEPS, QUERY_HEADS, HEAD_SIZE)
    return split.transpose(1, 0, 2).reshape(QUERY_HEADS * DECODE_STEPS, HEAD_SIZE)


def shards(
    wide,
    queries,
    cache,
    fresh_key_value,
    lengths,
    residual,
    norm_gain,
    vocab_weight,
    guidance,
    allowed_blocks,
    sampled,
):
    steps, half_pairs, blocks_here = allowed_blocks.shape
    width = vocab_weight.shape[1]
    pairs = guidance.shape[0]
    rows = steps * QUERY_HEADS
    cache_by_head = by_head(cache[0, 0])
    vmem, smem, hbm = in_vmem(), in_smem(), pl.BlockSpec(memory_space=pltpu.HBM)
    half_rows = jax.ShapeDtypeStruct((rows // 2, HEAD_SIZE), jnp.bfloat16)
    flat = jax.ShapeDtypeStruct((steps * half_pairs, width), jnp.float32)

    def swap(array):
        return lax.ppermute(array, "pair", [(0, 1), (1, 0)])

    mine, theirs = call(
        attend_kernel,
        (half_rows, half_rows),
        [smem] + [hbm] * 5,
        [
            pltpu.VMEM((KEY_VALUE_HEADS, cache.shape[2], 2, HEAD_SIZE), jnp.bfloat16),
            pltpu.VMEM((rows, HEAD_SIZE), jnp.float32),
            pltpu.VMEM((rows, HEAD_SIZE), jnp.bfloat16),
            pltpu.VMEM((rows, HEAD_SIZE), jnp.bfloat16),
            pltpu.VMEM((QUERY_HEADS, HEAD_SIZE), jnp.float32),
            pltpu.SemaphoreType.DMA(((BLOCKS + 1) * KEY_VALUE_HEADS + 3,)),
        ],
        limit=60 << 20,
    )(
        lengths,
        step_rows(queries[0, 0]),
        cache_by_head,
        by_head(fresh_key_value[0, 0]),
        step_rows(residual[0, 0]),
        norm_gain.reshape(QUERY_HEADS, HEAD_SIZE),
    )
    received = swap(theirs)
    own_part, factor = call(
        own_part_kernel,
        (jax.ShapeDtypeStruct(half_rows.shape, jnp.float32), jax.ShapeDtypeStruct((8, HEAD_SIZE), jnp.float32)),
        [smem, vmem],
    )(guidance, mine)
    spread = call(combine_kernel, jax.ShapeDtypeStruct((wide,) + half_rows.shape, jnp.bfloat16), [vmem] * 3)(
        factor, own_part, received
    )

    gathered = lax.all_to_all(spread, "wide", 0, 0, tiled=True)
    mine, theirs = call(
        project_kernel,
        (flat, flat),
        [vmem, vmem],
        [pltpu.VMEM((pairs * rows // 2, HEAD_SIZE), jnp.float32)],
    )(gathered, vocab_weight)

    lanes = pl.cdiv(3 * steps * half_pairs, 128) * 128
    guided, stats = call(
        stats_kernel,
        (flat, jax.ShapeDtypeStruct((wide, 1, lanes), jnp.float32)),
        [vmem] * 4,
    )(mine, swap(theirs), allowed_blocks, sampled)
    logprobs, tokens = call(
        finish_kernel,
        (
            jax.ShapeDtypeStruct((steps, half_pairs, width), jnp.float32),
            jax.ShapeDtypeStruct((steps, half_pairs), jnp.float32),
        ),
        [vmem] * 3,
    )(guided, lax.all_to_all(stats, "wide", 0, 0, tiled=True), allowed_blocks)
    return (logprobs, tokens)


def solution(mesh):
    placed = (
        P("pair", "wide", None, None),
        P("pair", "wide", None, None, None),
        P("pair", "wide", None, None, None),
        P("pair", "wide"),
        P("pair", "wide", None, None),
        P(),
        P("pair", "wide"),
        P(),
        P(None, "pair", "wide"),
        P(None, "pair"),
    )
    return jax.shard_map(
        functools.partial(shards, mesh.shape["wide"]),
        mesh=mesh,
        in_specs=placed,
        out_specs=(P(None, "pair", "wide"), P(None, "pair")),
        check_vma=False,
    )
```

```python
import functools
import math

import jax
import jax.numpy as jnp
from jax import lax
from jax.experimental import pallas as pl
from jax.experimental.pallas import tpu as pltpu
from jax.sharding import PartitionSpec as P

QUERY_HEADS = 64
KEY_VALUE_HEADS = 8
HEAD_SIZE = 128
BLK = 32
DECODE_STEPS = 2
SLOT_ROWS = 2 * KEY_VALUE_HEADS
HEAD_ROWS = DECODE_STEPS * (QUERY_HEADS // KEY_VALUE_HEADS)
NEG_FILL = -1e30
CHUNKS = 4


def in_vmem():
    return pl.BlockSpec(memory_space=pltpu.VMEM)


def in_smem():
    return pl.BlockSpec(memory_space=pltpu.SMEM)


def call(kernel, out_shape, in_specs, scratch=(), limit=16 << 20, cost=None):
    return pl.pallas_call(
        kernel,
        out_shape=out_shape,
        in_specs=in_specs,
        out_specs=jax.tree.map(lambda _: in_vmem(), out_shape),
        scratch_shapes=list(scratch),
        compiler_params=pltpu.CompilerParams(vmem_limit_bytes=limit),
        cost_estimate=cost,
    )


def attend_kernel(
    lengths, queries_in, cache, fresh_in, residual_in, gain_in, mine, theirs,
    stage, wide_rows, gain_rows, queries, fresh, residual, gain, arrived,
):
    rows = cache.shape[0]
    slots = rows // SLOT_ROWS
    part = rows // CHUNKS
    copies = [
        pltpu.make_async_copy(
            cache.at[pl.ds(index * part, part)], stage.at[pl.ds(index * part, part)], arrived.at[index]
        )
        for index in range(CHUNKS)
    ]
    small = [
        pltpu.make_async_copy(source, target, arrived.at[CHUNKS + index])
        for index, (source, target) in enumerate(
            ((gain_in, gain), (fresh_in, fresh), (queries_in, queries), (residual_in, residual))
        )
    ]
    for copy in copies + small:
        copy.start()
    for index, copy in enumerate(copies):
        copy.wait()

        def widen(step, carry):
            at = pl.ds(pl.multiple_of(index * part + step * 256, 256), 256)
            wide_rows[at, :] = stage[at, :].astype(jnp.float32)
            return carry

        lax.fori_loop(0, part // 256, widen, 0)
    for copy in small:
        copy.wait()
    gain_rows[pl.ds(0, QUERY_HEADS, stride=2), :] = gain[...]
    gain_rows[pl.ds(1, QUERY_HEADS, stride=2), :] = gain[...]
    wide_rows[pl.ds(rows - DECODE_STEPS * SLOT_ROWS, DECODE_STEPS * SLOT_ROWS), :] = fresh[...].astype(jnp.float32)
    factor = 1.0 / math.sqrt(HEAD_SIZE)
    scores = []
    for head in range(KEY_VALUE_HEADS):
        keys = wide_rows[pl.ds(2 * head, slots, stride=SLOT_ROWS), :].astype(jnp.bfloat16)
        scores.append(
            lax.dot_general(
                queries[pl.ds(head * HEAD_ROWS, HEAD_ROWS), :],
                keys,
                (((1,), (1,)), ((), ())),
                preferred_element_type=jnp.float32,
            )
        )
    score = jnp.concatenate(scores, axis=0)
    slot = lax.broadcasted_iota(jnp.int32, score.shape, 1)
    step_of_row = lax.rem(lax.broadcasted_iota(jnp.int32, score.shape, 0), DECODE_STEPS)
    first_fresh = slots - DECODE_STEPS
    live = (slot < lengths[0, 0]) | ((slot >= first_fresh) & (slot - first_fresh <= step_of_row))
    score = jnp.where(live, score * factor, NEG_FILL)
    weight = jnp.exp(score - jnp.max(score, axis=1, keepdims=True))
    weight = (weight / jnp.sum(weight, axis=1, keepdims=True)).astype(jnp.bfloat16)
    mixed = []
    for head in range(KEY_VALUE_HEADS):
        values = wide_rows[pl.ds(2 * head + 1, slots, stride=SLOT_ROWS), :].astype(jnp.bfloat16)
        mixed.append(
            jnp.dot(
                weight[head * HEAD_ROWS : (head + 1) * HEAD_ROWS], values, preferred_element_type=jnp.float32
            )
        )
    hidden = jnp.concatenate(mixed, axis=0) + residual[...].astype(jnp.float32)
    row_power = jnp.sum(hidden * hidden, axis=1, keepdims=True)
    step_of_row = lax.rem(lax.broadcasted_iota(jnp.int32, row_power.shape, 0), DECODE_STEPS)
    scale = jnp.zeros_like(row_power)
    for step in range(DECODE_STEPS):
        power = jnp.sum(jnp.where(step_of_row == step, row_power, 0.0), axis=0, keepdims=True)
        power = power / (QUERY_HEADS * HEAD_SIZE)
        scale = jnp.where(step_of_row == step, lax.rsqrt(power + 1e-05), scale)
    normed = (hidden * scale * gain_rows[...]).astype(jnp.bfloat16)
    half = normed.shape[0] // 2
    first = lax.axis_index("pair") == 0
    mine[...] = jnp.where(first, normed[:half], normed[half:])
    theirs[...] = jnp.where(first, normed[half:], normed[:half])


def branch_factor(scale, branch):
    guidance = scale[lax.axis_index("wide")]
    return jnp.where(branch == 0, guidance, 1.0 - guidance)


def own_part_kernel(scale, mine, out, factor):
    branch = lax.axis_index("pair")
    out[...] = branch_factor(scale, branch) * mine[...].astype(jnp.float32)
    factor[...] = jnp.full(factor.shape, branch_factor(scale, 1 - branch), jnp.float32)


def combine_kernel(factor, own_part, received, spread):
    other_part = factor[0:1, :] * received[...].astype(jnp.float32)
    guided = (own_part[...] + other_part).astype(jnp.bfloat16)
    spread[...] = jnp.broadcast_to(guided[None], spread.shape)


def project_kernel(near, far, weight, mine, theirs, wide_rows):
    pairs = 2 * near.shape[0]
    per_pair, lanes = near.shape[1:]
    half = pairs // 2
    parity = lax.axis_index("wide") % 2
    for rows, offset in ((near, parity), (far, 1 - parity)):
        for index in range(half):
            at = pl.multiple_of((2 * index + offset) * per_pair, per_pair)
            wide_rows[pl.ds(at, per_pair), :] = rows[index].astype(jnp.float32)

    def head_rows(head):
        steps = [
            wide_rows[pl.ds(head * DECODE_STEPS + step, pairs, stride=per_pair), :]
            for step in range(DECODE_STEPS)
        ]
        return jnp.concatenate(
            [rows_of_step[part * half : (part + 1) * half] for part in range(2) for rows_of_step in steps], axis=0
        ).astype(jnp.bfloat16)

    total = jnp.zeros((DECODE_STEPS * pairs, mine.shape[1]), jnp.float32)
    for two in range(per_pair // DECODE_STEPS // 2):
        left = jnp.concatenate([head_rows(2 * two), head_rows(2 * two + 1)], axis=1)
        total = total + jnp.dot(
            left, weight[pl.ds(two * 2 * lanes, 2 * lanes), :], preferred_element_type=jnp.float32
        )
    first = lax.axis_index("pair") == 0
    low, high = total[: mine.shape[0]], total[mine.shape[0] :]
    mine[...] = jnp.where(first, low, high)
    theirs[...] = jnp.where(first, high, low)


def to_lanes(column):
    size = column.shape[0]
    eye = lax.broadcasted_iota(jnp.int32, (size, size), 0) == lax.broadcasted_iota(jnp.int32, (size, size), 1)
    return jnp.sum(jnp.where(eye, column, jnp.zeros_like(column)), axis=0, keepdims=True)


def to_column(lanes):
    size = lanes.shape[1]
    eye = lax.broadcasted_iota(jnp.int32, (size, size), 0) == lax.broadcasted_iota(jnp.int32, (size, size), 1)
    return jnp.sum(jnp.where(eye, lanes, jnp.zeros_like(lanes)), axis=1, keepdims=True)


def allowed_entries(blocks, shape):
    half = blocks.shape[1]
    flags = jnp.concatenate([blocks[step] for step in range(DECODE_STEPS)], axis=0)
    block = lax.broadcasted_iota(jnp.int32, shape, 1) // BLK
    flag = jnp.zeros(shape, jnp.int32)
    for index in range(blocks.shape[2]):
        flag = jnp.where(block == index, flags[:, index : index + 1], flag)
    return flag > 0


def stats_kernel(mine, received, blocks, sampled, guided_out, stats):
    guided = mine[...] + received[...]
    guided_out[...] = guided
    count, width = guided.shape
    half = count // DECODE_STEPS
    allowed = allowed_entries(blocks, guided.shape)
    top = jnp.max(jnp.where(allowed, guided, NEG_FILL), axis=1, keepdims=True)
    total = jnp.sum(jnp.where(allowed, jnp.exp(guided - top), 0.0), axis=1, keepdims=True)
    chosen = jnp.concatenate([to_column(sampled[pl.ds(step, 1), :]) for step in range(DECODE_STEPS)], axis=0)
    column = lax.broadcasted_iota(jnp.int32, guided.shape, 1) + lax.axis_index("wide") * width
    picked = jnp.sum(jnp.where(column == chosen, guided, 0.0), axis=1, keepdims=True)
    lanes = jnp.concatenate([to_lanes(top), to_lanes(total), to_lanes(picked)], axis=1)
    pad = stats.shape[2] - lanes.shape[1]
    if pad > 0:
        lanes = jnp.concatenate([lanes, jnp.zeros((1, pad), jnp.float32)], axis=1)
    stats[...] = jnp.broadcast_to(lanes[None], stats.shape)


def finish_kernel(guided, stats, blocks, logprobs, tokens):
    count, width = guided.shape
    half = count // DECODE_STEPS
    parts = stats[...].reshape(stats.shape[0], stats.shape[2])
    tops = parts[:, 0:count]
    top = jnp.max(tops, axis=0, keepdims=True)
    total = jnp.sum(parts[:, count : 2 * count] * jnp.exp(tops - top), axis=0, keepdims=True)
    picked = jnp.sum(parts[:, 2 * count : 3 * count], axis=0, keepdims=True)
    normalizer = top + jnp.log(total)
    token = picked - normalizer
    for step in range(DECODE_STEPS):
        tokens[pl.ds(step, 1), :] = token[:, step * half : (step + 1) * half]
    allowed = allowed_entries(blocks, guided.shape)
    result = jnp.where(allowed, guided[...] - to_column(normalizer), 0.0)
    logprobs[...] = result.reshape(logprobs.shape)


def slot_rows(array):
    slots = array.shape[0]
    split = array.reshape(slots, 2, KEY_VALUE_HEADS, HEAD_SIZE)
    return split.transpose(0, 2, 1, 3).reshape(slots * SLOT_ROWS, HEAD_SIZE)


def step_rows(array):
    split = array.reshape(DECODE_STEPS, QUERY_HEADS, HEAD_SIZE)
    return split.transpose(1, 0, 2).reshape(QUERY_HEADS * DECODE_STEPS, HEAD_SIZE)


def shards(
    wide,
    queries,
    cache,
    fresh_key_value,
    lengths,
    residual,
    norm_gain,
    vocab_weight,
    guidance,
    allowed_blocks,
    sampled,
):
    steps, half_pairs, blocks_here = allowed_blocks.shape
    width = vocab_weight.shape[1]
    pairs = guidance.shape[0]
    rows = steps * QUERY_HEADS
    cache_rows = slot_rows(cache[0, 0])
    vmem, smem, hbm = in_vmem(), in_smem(), pl.BlockSpec(memory_space=pltpu.HBM)
    half_rows = jax.ShapeDtypeStruct((rows // 2, HEAD_SIZE), jnp.bfloat16)
    flat = jax.ShapeDtypeStruct((steps * half_pairs, width), jnp.float32)

    def swap(array):
        return lax.ppermute(array, "pair", [(0, 1), (1, 0)])

    mine, theirs = call(
        attend_kernel,
        (half_rows, half_rows),
        [smem] + [hbm] * 5,
        [
            pltpu.VMEM(cache_rows.shape, jnp.bfloat16),
            pltpu.VMEM(cache_rows.shape, jnp.float32),
            pltpu.VMEM((rows, HEAD_SIZE), jnp.float32),
            pltpu.VMEM((rows, HEAD_SIZE), jnp.bfloat16),
            pltpu.VMEM((steps * SLOT_ROWS, HEAD_SIZE), jnp.bfloat16),
            pltpu.VMEM((rows, HEAD_SIZE), jnp.bfloat16),
            pltpu.VMEM((QUERY_HEADS, HEAD_SIZE), jnp.float32),
            pltpu.SemaphoreType.DMA((CHUNKS + 4,)),
        ],
        limit=60 << 20,
    )(
        lengths,
        step_rows(queries[0, 0]),
        cache_rows,
        slot_rows(fresh_key_value[0, 0]),
        step_rows(residual[0, 0]),
        norm_gain.reshape(QUERY_HEADS, HEAD_SIZE),
    )
    received = swap(theirs)
    own_part, factor = call(
        own_part_kernel,
        (jax.ShapeDtypeStruct(half_rows.shape, jnp.float32), jax.ShapeDtypeStruct((8, HEAD_SIZE), jnp.float32)),
        [smem, vmem],
    )(guidance, mine)
    spread = call(combine_kernel, jax.ShapeDtypeStruct((wide // 2,) + half_rows.shape, jnp.bfloat16), [vmem] * 3)(
        factor, own_part, received
    )
    same_core = [list(range(core, wide, 2)) for core in range(2)]
    near = lax.all_to_all(spread, "wide", 0, 0, axis_index_groups=same_core, tiled=True)
    far = lax.ppermute(near, "wide", [(source, source ^ 1) for source in range(wide)])
    mine, theirs = call(
        project_kernel,
        (flat, flat),
        [vmem] * 3,
        [pltpu.VMEM((pairs * rows // 2, HEAD_SIZE), jnp.float32)],
    )(near, far, vocab_weight)

    lanes = pl.cdiv(3 * steps * half_pairs, 128) * 128
    guided, stats = call(
        stats_kernel,
        (flat, jax.ShapeDtypeStruct((wide, 1, lanes), jnp.float32)),
        [vmem] * 4,
    )(mine, swap(theirs), allowed_blocks, sampled)
    logprobs, tokens = call(
        finish_kernel,
        (
            jax.ShapeDtypeStruct((steps, half_pairs, width), jnp.float32),
            jax.ShapeDtypeStruct((steps, half_pairs), jnp.float32),
        ),
        [vmem] * 3,
    )(guided, lax.all_to_all(stats, "wide", 0, 0, tiled=True), allowed_blocks)
    return (logprobs, tokens)


def solution(mesh):
    placed = (
        P("pair", "wide", None, None),
        P("pair", "wide", None, None, None),
        P("pair", "wide", None, None, None),
        P("pair", "wide"),
        P("pair", "wide", None, None),
        P(),
        P("pair", "wide"),
        P(),
        P(None, "pair", "wide"),
        P(None, "pair"),
    )
    return jax.shard_map(
        functools.partial(shards, mesh.shape["wide"]),
        mesh=mesh,
        in_specs=placed,
        out_specs=(P(None, "pair", "wide"), P(None, "pair")),
        check_vma=False,
    )
```

```python
import functools
import math

import jax
import jax.numpy as jnp
from jax import lax
from jax.experimental import pallas as pl
from jax.experimental.pallas import tpu as pltpu
from jax.sharding import PartitionSpec as P

QUERY_HEADS = 64
KEY_VALUE_HEADS = 8
HEAD_SIZE = 128
BLK = 32
DECODE_STEPS = 2
SLOT_ROWS = 2 * KEY_VALUE_HEADS
SLOT_PITCH = SLOT_ROWS + 1
UNROLL = 32
HEAD_ROWS = DECODE_STEPS * (QUERY_HEADS // KEY_VALUE_HEADS)
NEG_FILL = -1e30
CHUNKS = 4


def in_vmem():
    return pl.BlockSpec(memory_space=pltpu.VMEM)


def in_smem():
    return pl.BlockSpec(memory_space=pltpu.SMEM)


def call(kernel, out_shape, in_specs, scratch=(), limit=16 << 20, cost=None):
    return pl.pallas_call(
        kernel,
        out_shape=out_shape,
        in_specs=in_specs,
        out_specs=jax.tree.map(lambda _: in_vmem(), out_shape),
        scratch_shapes=list(scratch),
        compiler_params=pltpu.CompilerParams(vmem_limit_bytes=limit),
        cost_estimate=cost,
    )


def attend_kernel(
    lengths, queries_in, cache, fresh_in, residual_in, gain_in, mine, theirs,
    stage, wide_rows, gain_rows, queries, fresh, residual, gain, arrived,
):
    rows = cache.shape[0]
    slots = rows // SLOT_ROWS
    part = rows // CHUNKS
    copies = [
        pltpu.make_async_copy(
            cache.at[pl.ds(index * part, part)], stage.at[pl.ds(index * part, part)], arrived.at[index]
        )
        for index in range(CHUNKS)
    ]
    small = [
        pltpu.make_async_copy(source, target, arrived.at[CHUNKS + index])
        for index, (source, target) in enumerate(
            ((gain_in, gain), (fresh_in, fresh), (queries_in, queries), (residual_in, residual))
        )
    ]
    for copy in copies + small:
        copy.start()
    for index, copy in enumerate(copies):
        copy.wait()

        def widen(step, carry):
            first = index * (part // SLOT_ROWS) + step * UNROLL
            source = pl.multiple_of(first * SLOT_ROWS, UNROLL * SLOT_ROWS)
            target = pl.multiple_of(first * SLOT_PITCH, 8)
            for slot in range(UNROLL):
                wide_rows[pl.ds(target + slot * SLOT_PITCH, SLOT_ROWS), :] = stage[
                    pl.ds(source + slot * SLOT_ROWS, SLOT_ROWS), :
                ].astype(jnp.float32)
            return carry

        lax.fori_loop(0, part // (SLOT_ROWS * UNROLL), widen, 0)
    for copy in small:
        copy.wait()
    gain_rows[pl.ds(0, QUERY_HEADS, stride=2), :] = gain[...]
    gain_rows[pl.ds(1, QUERY_HEADS, stride=2), :] = gain[...]
    for step in range(DECODE_STEPS):
        wide_rows[pl.ds((slots - DECODE_STEPS + step) * SLOT_PITCH, SLOT_ROWS), :] = fresh[
            pl.ds(step * SLOT_ROWS, SLOT_ROWS), :
        ].astype(jnp.float32)
    factor = 1.0 / math.sqrt(HEAD_SIZE)
    scores = []
    for head in range(KEY_VALUE_HEADS):
        keys = wide_rows[pl.ds(2 * head, slots, stride=SLOT_PITCH), :].astype(jnp.bfloat16)
        scores.append(
            lax.dot_general(
                queries[pl.ds(head * HEAD_ROWS, HEAD_ROWS), :],
                keys,
                (((1,), (1,)), ((), ())),
                preferred_element_type=jnp.float32,
            )
        )
    score = jnp.concatenate(scores, axis=0)
    slot = lax.broadcasted_iota(jnp.int32, score.shape, 1)
    step_of_row = lax.rem(lax.broadcasted_iota(jnp.int32, score.shape, 0), DECODE_STEPS)
    first_fresh = slots - DECODE_STEPS
    live = (slot < lengths[0, 0]) | ((slot >= first_fresh) & (slot - first_fresh <= step_of_row))
    score = jnp.where(live, score * factor, NEG_FILL)
    weight = jnp.exp(score - jnp.max(score, axis=1, keepdims=True))
    weight = (weight / jnp.sum(weight, axis=1, keepdims=True)).astype(jnp.bfloat16)
    mixed = []
    for head in range(KEY_VALUE_HEADS):
        values = wide_rows[pl.ds(2 * head + 1, slots, stride=SLOT_PITCH), :].astype(jnp.bfloat16)
        mixed.append(
            jnp.dot(
                weight[head * HEAD_ROWS : (head + 1) * HEAD_ROWS], values, preferred_element_type=jnp.float32
            )
        )
    hidden = jnp.concatenate(mixed, axis=0) + residual[...].astype(jnp.float32)
    row_power = jnp.sum(hidden * hidden, axis=1, keepdims=True)
    step_of_row = lax.rem(lax.broadcasted_iota(jnp.int32, row_power.shape, 0), DECODE_STEPS)
    scale = jnp.zeros_like(row_power)
    for step in range(DECODE_STEPS):
        power = jnp.sum(jnp.where(step_of_row == step, row_power, 0.0), axis=0, keepdims=True)
        power = power / (QUERY_HEADS * HEAD_SIZE)
        scale = jnp.where(step_of_row == step, lax.rsqrt(power + 1e-05), scale)
    normed = (hidden * scale * gain_rows[...]).astype(jnp.bfloat16)
    half = normed.shape[0] // 2
    first = lax.axis_index("pair") == 0
    mine[...] = jnp.where(first, normed[:half], normed[half:])
    theirs[...] = jnp.where(first, normed[half:], normed[:half])


def branch_factor(scale, branch):
    guidance = scale[lax.axis_index("wide")]
    return jnp.where(branch == 0, guidance, 1.0 - guidance)


def own_part_kernel(scale, mine, out, factor):
    branch = lax.axis_index("pair")
    out[...] = branch_factor(scale, branch) * mine[...].astype(jnp.float32)
    factor[...] = jnp.full(factor.shape, branch_factor(scale, 1 - branch), jnp.float32)


def combine_kernel(factor, own_part, received, spread):
    other_part = factor[0:1, :] * received[...].astype(jnp.float32)
    guided = (own_part[...] + other_part).astype(jnp.bfloat16)
    spread[...] = jnp.broadcast_to(guided[None], spread.shape)


def project_kernel(near, far, weight, mine, theirs, wide_rows):
    pairs = 2 * near.shape[0]
    per_pair, lanes = near.shape[1:]
    half = pairs // 2
    pitch = per_pair + 1
    parity = lax.axis_index("wide") % 2
    for rows, offset in ((near, parity), (far, 1 - parity)):
        for index in range(half):
            wide_rows[pl.ds((2 * index + offset) * pitch, per_pair), :] = rows[index].astype(jnp.float32)

    def head_rows(head):
        steps = [
            wide_rows[pl.ds(head * DECODE_STEPS + step, pairs, stride=pitch), :]
            for step in range(DECODE_STEPS)
        ]
        return jnp.concatenate(
            [rows_of_step[part * half : (part + 1) * half] for part in range(2) for rows_of_step in steps], axis=0
        ).astype(jnp.bfloat16)

    total = jnp.zeros((DECODE_STEPS * pairs, mine.shape[1]), jnp.float32)
    for two in range(per_pair // DECODE_STEPS // 2):
        left = jnp.concatenate([head_rows(2 * two), head_rows(2 * two + 1)], axis=1)
        total = total + jnp.dot(
            left, weight[pl.ds(two * 2 * lanes, 2 * lanes), :], preferred_element_type=jnp.float32
        )
    first = lax.axis_index("pair") == 0
    low, high = total[: mine.shape[0]], total[mine.shape[0] :]
    mine[...] = jnp.where(first, low, high)
    theirs[...] = jnp.where(first, high, low)


def to_lanes(column):
    size = column.shape[0]
    eye = lax.broadcasted_iota(jnp.int32, (size, size), 0) == lax.broadcasted_iota(jnp.int32, (size, size), 1)
    return jnp.sum(jnp.where(eye, column, jnp.zeros_like(column)), axis=0, keepdims=True)


def to_column(lanes):
    size = lanes.shape[1]
    eye = lax.broadcasted_iota(jnp.int32, (size, size), 0) == lax.broadcasted_iota(jnp.int32, (size, size), 1)
    return jnp.sum(jnp.where(eye, lanes, jnp.zeros_like(lanes)), axis=1, keepdims=True)


def allowed_entries(blocks, shape):
    half = blocks.shape[1]
    flags = jnp.concatenate([blocks[step] for step in range(DECODE_STEPS)], axis=0)
    block = lax.broadcasted_iota(jnp.int32, shape, 1) // BLK
    flag = jnp.zeros(shape, jnp.int32)
    for index in range(blocks.shape[2]):
        flag = jnp.where(block == index, flags[:, index : index + 1], flag)
    return flag > 0


def stats_kernel(mine, received, blocks, sampled, guided_out, stats):
    guided = mine[...] + received[...]
    guided_out[...] = guided
    count, width = guided.shape
    half = count // DECODE_STEPS
    allowed = allowed_entries(blocks, guided.shape)
    top = jnp.max(jnp.where(allowed, guided, NEG_FILL), axis=1, keepdims=True)
    total = jnp.sum(jnp.where(allowed, jnp.exp(guided - top), 0.0), axis=1, keepdims=True)
    chosen = jnp.concatenate([to_column(sampled[pl.ds(step, 1), :]) for step in range(DECODE_STEPS)], axis=0)
    column = lax.broadcasted_iota(jnp.int32, guided.shape, 1) + lax.axis_index("wide") * width
    picked = jnp.sum(jnp.where(column == chosen, guided, 0.0), axis=1, keepdims=True)
    lanes = jnp.concatenate([to_lanes(top), to_lanes(total), to_lanes(picked)], axis=1)
    pad = stats.shape[2] - lanes.shape[1]
    if pad > 0:
        lanes = jnp.concatenate([lanes, jnp.zeros((1, pad), jnp.float32)], axis=1)
    stats[...] = jnp.broadcast_to(lanes[None], stats.shape)


def finish_kernel(guided, stats, blocks, logprobs, tokens):
    count, width = guided.shape
    half = count // DECODE_STEPS
    parts = stats[...].reshape(stats.shape[0], stats.shape[2])
    tops = parts[:, 0:count]
    top = jnp.max(tops, axis=0, keepdims=True)
    total = jnp.sum(parts[:, count : 2 * count] * jnp.exp(tops - top), axis=0, keepdims=True)
    picked = jnp.sum(parts[:, 2 * count : 3 * count], axis=0, keepdims=True)
    normalizer = top + jnp.log(total)
    token = picked - normalizer
    for step in range(DECODE_STEPS):
        tokens[pl.ds(step, 1), :] = token[:, step * half : (step + 1) * half]
    allowed = allowed_entries(blocks, guided.shape)
    result = jnp.where(allowed, guided[...] - to_column(normalizer), 0.0)
    logprobs[...] = result.reshape(logprobs.shape)


def slot_rows(array):
    slots = array.shape[0]
    split = array.reshape(slots, 2, KEY_VALUE_HEADS, HEAD_SIZE)
    return split.transpose(0, 2, 1, 3).reshape(slots * SLOT_ROWS, HEAD_SIZE)


def step_rows(array):
    split = array.reshape(DECODE_STEPS, QUERY_HEADS, HEAD_SIZE)
    return split.transpose(1, 0, 2).reshape(QUERY_HEADS * DECODE_STEPS, HEAD_SIZE)


def shards(
    wide,
    queries,
    cache,
    fresh_key_value,
    lengths,
    residual,
    norm_gain,
    vocab_weight,
    guidance,
    allowed_blocks,
    sampled,
):
    steps, half_pairs, blocks_here = allowed_blocks.shape
    width = vocab_weight.shape[1]
    pairs = guidance.shape[0]
    rows = steps * QUERY_HEADS
    cache_rows = slot_rows(cache[0, 0])
    vmem, smem, hbm = in_vmem(), in_smem(), pl.BlockSpec(memory_space=pltpu.HBM)
    half_rows = jax.ShapeDtypeStruct((rows // 2, HEAD_SIZE), jnp.bfloat16)
    flat = jax.ShapeDtypeStruct((steps * half_pairs, width), jnp.float32)

    def swap(array):
        return lax.ppermute(array, "pair", [(0, 1), (1, 0)])

    mine, theirs = call(
        attend_kernel,
        (half_rows, half_rows),
        [smem] + [hbm] * 5,
        [
            pltpu.VMEM(cache_rows.shape, jnp.bfloat16),
            pltpu.VMEM((cache.shape[2] * SLOT_PITCH, HEAD_SIZE), jnp.float32),
            pltpu.VMEM((rows, HEAD_SIZE), jnp.float32),
            pltpu.VMEM((rows, HEAD_SIZE), jnp.bfloat16),
            pltpu.VMEM((steps * SLOT_ROWS, HEAD_SIZE), jnp.bfloat16),
            pltpu.VMEM((rows, HEAD_SIZE), jnp.bfloat16),
            pltpu.VMEM((QUERY_HEADS, HEAD_SIZE), jnp.float32),
            pltpu.SemaphoreType.DMA((CHUNKS + 4,)),
        ],
        limit=60 << 20,
    )(
        lengths,
        step_rows(queries[0, 0]),
        cache_rows,
        slot_rows(fresh_key_value[0, 0]),
        step_rows(residual[0, 0]),
        norm_gain.reshape(QUERY_HEADS, HEAD_SIZE),
    )
    received = swap(theirs)
    own_part, factor = call(
        own_part_kernel,
        (jax.ShapeDtypeStruct(half_rows.shape, jnp.float32), jax.ShapeDtypeStruct((8, HEAD_SIZE), jnp.float32)),
        [smem, vmem],
    )(guidance, mine)
    spread = call(combine_kernel, jax.ShapeDtypeStruct((wide // 2,) + half_rows.shape, jnp.bfloat16), [vmem] * 3)(
        factor, own_part, received
    )
    same_core = [list(range(core, wide, 2)) for core in range(2)]
    near = lax.all_to_all(spread, "wide", 0, 0, axis_index_groups=same_core, tiled=True)
    far = lax.ppermute(near, "wide", [(source, source ^ 1) for source in range(wide)])
    mine, theirs = call(
        project_kernel,
        (flat, flat),
        [vmem] * 3,
        [pltpu.VMEM((pairs * (rows // 2 + 1), HEAD_SIZE), jnp.float32)],
    )(near, far, vocab_weight)

    lanes = pl.cdiv(3 * steps * half_pairs, 128) * 128
    guided, stats = call(
        stats_kernel,
        (flat, jax.ShapeDtypeStruct((wide, 1, lanes), jnp.float32)),
        [vmem] * 4,
    )(mine, swap(theirs), allowed_blocks, sampled)
    logprobs, tokens = call(
        finish_kernel,
        (
            jax.ShapeDtypeStruct((steps, half_pairs, width), jnp.float32),
            jax.ShapeDtypeStruct((steps, half_pairs), jnp.float32),
        ),
        [vmem] * 3,
    )(guided, lax.all_to_all(stats, "wide", 0, 0, tiled=True), allowed_blocks)
    return (logprobs, tokens)


def solution(mesh):
    placed = (
        P("pair", "wide", None, None),
        P("pair", "wide", None, None, None),
        P("pair", "wide", None, None, None),
        P("pair", "wide"),
        P("pair", "wide", None, None),
        P(),
        P("pair", "wide"),
        P(),
        P(None, "pair", "wide"),
        P(None, "pair"),
    )
    return jax.shard_map(
        functools.partial(shards, mesh.shape["wide"]),
        mesh=mesh,
        in_specs=placed,
        out_specs=(P(None, "pair", "wide"), P(None, "pair")),
        check_vma=False,
    )
```

```python
import functools
import math

import jax
import jax.numpy as jnp
from jax import lax
from jax.experimental import pallas as pl
from jax.experimental.pallas import tpu as pltpu
from jax.sharding import PartitionSpec as P

QUERY_HEADS = 64
KEY_VALUE_HEADS = 8
HEAD_SIZE = 128
BLK = 32
DECODE_STEPS = 2
SLOT_ROWS = 2 * KEY_VALUE_HEADS
SLOT_PITCH = SLOT_ROWS + 1
BLOCK = 64
HEAD_ROWS = DECODE_STEPS * (QUERY_HEADS // KEY_VALUE_HEADS)
NEG_FILL = -1e30


def in_vmem():
    return pl.BlockSpec(memory_space=pltpu.VMEM)


def in_smem():
    return pl.BlockSpec(memory_space=pltpu.SMEM)


def call(kernel, out_shape, in_specs, scratch=(), limit=16 << 20, cost=None):
    return pl.pallas_call(
        kernel,
        out_shape=out_shape,
        in_specs=in_specs,
        out_specs=jax.tree.map(lambda _: in_vmem(), out_shape),
        scratch_shapes=list(scratch),
        compiler_params=pltpu.CompilerParams(vmem_limit_bytes=limit),
        cost_estimate=cost,
    )


def attend_kernel(
    lengths, queries_in, cache, fresh_in, residual_in, gain_in, mine, theirs,
    stage, wide_rows, gain_rows, queries, fresh, residual, gain, arrived,
):
    rows = cache.shape[0]
    slots = rows // SLOT_ROWS

    def block_copy(block):
        at = pl.ds(pl.multiple_of(block * (BLOCK * SLOT_ROWS), BLOCK * SLOT_ROWS), BLOCK * SLOT_ROWS)
        return pltpu.make_async_copy(cache.at[at], stage.at[at], arrived.at[block])

    def start(block, carry):
        block_copy(block).start()
        return carry

    def clear(block, carry):
        target = pl.multiple_of(block * (BLOCK * SLOT_PITCH), 8)
        wide_rows[pl.ds(target, BLOCK * SLOT_PITCH), :] = jnp.zeros((BLOCK * SLOT_PITCH, HEAD_SIZE), jnp.float32)
        return carry

    def widen(block, carry):
        block_copy(block).wait()
        source = pl.multiple_of(block * (BLOCK * SLOT_ROWS), BLOCK * SLOT_ROWS)
        target = pl.multiple_of(block * (BLOCK * SLOT_PITCH), 8)
        for slot in range(BLOCK):
            wide_rows[pl.ds(target + slot * SLOT_PITCH, SLOT_ROWS), :] = stage[
                pl.ds(source + slot * SLOT_ROWS, SLOT_ROWS), :
            ].astype(jnp.float32)
        return carry

    blocks = slots // BLOCK
    live_blocks = lax.div(lengths[0, 0] + (BLOCK - 1), BLOCK)
    lax.fori_loop(0, live_blocks, start, 0)
    small = [
        pltpu.make_async_copy(source, target, arrived.at[blocks + index])
        for index, (source, target) in enumerate(
            ((gain_in, gain), (fresh_in, fresh), (queries_in, queries), (residual_in, residual))
        )
    ]
    for copy in small:
        copy.start()
    lax.fori_loop(live_blocks, blocks, clear, 0)
    lax.fori_loop(0, live_blocks, widen, 0)
    for copy in small:
        copy.wait()
    gain_rows[pl.ds(0, QUERY_HEADS, stride=2), :] = gain[...]
    gain_rows[pl.ds(1, QUERY_HEADS, stride=2), :] = gain[...]
    for step in range(DECODE_STEPS):
        wide_rows[pl.ds((slots - DECODE_STEPS + step) * SLOT_PITCH, SLOT_ROWS), :] = fresh[
            pl.ds(step * SLOT_ROWS, SLOT_ROWS), :
        ].astype(jnp.float32)
    factor = 1.0 / math.sqrt(HEAD_SIZE)
    scores = []
    for head in range(KEY_VALUE_HEADS):
        keys = wide_rows[pl.ds(2 * head, slots, stride=SLOT_PITCH), :].astype(jnp.bfloat16)
        scores.append(
            lax.dot_general(
                queries[pl.ds(head * HEAD_ROWS, HEAD_ROWS), :],
                keys,
                (((1,), (1,)), ((), ())),
                preferred_element_type=jnp.float32,
            )
        )
    score = jnp.concatenate(scores, axis=0)
    slot = lax.broadcasted_iota(jnp.int32, score.shape, 1)
    step_of_row = lax.rem(lax.broadcasted_iota(jnp.int32, score.shape, 0), DECODE_STEPS)
    first_fresh = slots - DECODE_STEPS
    live = (slot < lengths[0, 0]) | ((slot >= first_fresh) & (slot - first_fresh <= step_of_row))
    score = jnp.where(live, score * factor, NEG_FILL)
    weight = jnp.exp(score - jnp.max(score, axis=1, keepdims=True))
    weight = (weight / jnp.sum(weight, axis=1, keepdims=True)).astype(jnp.bfloat16)
    mixed = []
    for head in range(KEY_VALUE_HEADS):
        values = wide_rows[pl.ds(2 * head + 1, slots, stride=SLOT_PITCH), :].astype(jnp.bfloat16)
        mixed.append(
            jnp.dot(
                weight[head * HEAD_ROWS : (head + 1) * HEAD_ROWS], values, preferred_element_type=jnp.float32
            )
        )
    hidden = jnp.concatenate(mixed, axis=0) + residual[...].astype(jnp.float32)
    row_power = jnp.sum(hidden * hidden, axis=1, keepdims=True)
    step_of_row = lax.rem(lax.broadcasted_iota(jnp.int32, row_power.shape, 0), DECODE_STEPS)
    scale = jnp.zeros_like(row_power)
    for step in range(DECODE_STEPS):
        power = jnp.sum(jnp.where(step_of_row == step, row_power, 0.0), axis=0, keepdims=True)
        power = power / (QUERY_HEADS * HEAD_SIZE)
        scale = jnp.where(step_of_row == step, lax.rsqrt(power + 1e-05), scale)
    normed = (hidden * scale * gain_rows[...]).astype(jnp.bfloat16)
    half = normed.shape[0] // 2
    first = lax.axis_index("pair") == 0
    mine[...] = jnp.where(first, normed[:half], normed[half:])
    theirs[...] = jnp.where(first, normed[half:], normed[:half])


def branch_factor(scale, branch):
    guidance = scale[lax.axis_index("wide")]
    return jnp.where(branch == 0, guidance, 1.0 - guidance)


def own_part_kernel(scale, mine, out, factor):
    branch = lax.axis_index("pair")
    out[...] = branch_factor(scale, branch) * mine[...].astype(jnp.float32)
    factor[...] = jnp.full(factor.shape, branch_factor(scale, 1 - branch), jnp.float32)


def combine_kernel(factor, own_part, received, spread):
    other_part = factor[0:1, :] * received[...].astype(jnp.float32)
    guided = (own_part[...] + other_part).astype(jnp.bfloat16)
    spread[...] = jnp.broadcast_to(guided[None], spread.shape)


def project_kernel(near, far, weight, mine, theirs, wide_rows):
    pairs = 2 * near.shape[0]
    per_pair, lanes = near.shape[1:]
    half = pairs // 2
    pitch = per_pair + 1
    parity = lax.axis_index("wide") % 2
    for rows, offset in ((near, parity), (far, 1 - parity)):
        for index in range(half):
            wide_rows[pl.ds((2 * index + offset) * pitch, per_pair), :] = rows[index].astype(jnp.float32)

    def head_rows(head):
        steps = [
            wide_rows[pl.ds(head * DECODE_STEPS + step, pairs, stride=pitch), :]
            for step in range(DECODE_STEPS)
        ]
        return jnp.concatenate(
            [rows_of_step[part * half : (part + 1) * half] for part in range(2) for rows_of_step in steps], axis=0
        ).astype(jnp.bfloat16)

    total = jnp.zeros((DECODE_STEPS * pairs, mine.shape[1]), jnp.float32)
    for two in range(per_pair // DECODE_STEPS // 2):
        left = jnp.concatenate([head_rows(2 * two), head_rows(2 * two + 1)], axis=1)
        total = total + jnp.dot(
            left, weight[pl.ds(two * 2 * lanes, 2 * lanes), :], preferred_element_type=jnp.float32
        )
    first = lax.axis_index("pair") == 0
    low, high = total[: mine.shape[0]], total[mine.shape[0] :]
    mine[...] = jnp.where(first, low, high)
    theirs[...] = jnp.where(first, high, low)


def to_lanes(column):
    size = column.shape[0]
    eye = lax.broadcasted_iota(jnp.int32, (size, size), 0) == lax.broadcasted_iota(jnp.int32, (size, size), 1)
    return jnp.sum(jnp.where(eye, column, jnp.zeros_like(column)), axis=0, keepdims=True)


def to_column(lanes):
    size = lanes.shape[1]
    eye = lax.broadcasted_iota(jnp.int32, (size, size), 0) == lax.broadcasted_iota(jnp.int32, (size, size), 1)
    return jnp.sum(jnp.where(eye, lanes, jnp.zeros_like(lanes)), axis=1, keepdims=True)


def allowed_entries(blocks, shape):
    half = blocks.shape[1]
    flags = jnp.concatenate([blocks[step] for step in range(DECODE_STEPS)], axis=0)
    block = lax.broadcasted_iota(jnp.int32, shape, 1) // BLK
    flag = jnp.zeros(shape, jnp.int32)
    for index in range(blocks.shape[2]):
        flag = jnp.where(block == index, flags[:, index : index + 1], flag)
    return flag > 0


def stats_kernel(mine, received, blocks, sampled, guided_out, stats):
    guided = mine[...] + received[...]
    guided_out[...] = guided
    count, width = guided.shape
    half = count // DECODE_STEPS
    allowed = allowed_entries(blocks, guided.shape)
    top = jnp.max(jnp.where(allowed, guided, NEG_FILL), axis=1, keepdims=True)
    total = jnp.sum(jnp.where(allowed, jnp.exp(guided - top), 0.0), axis=1, keepdims=True)
    chosen = jnp.concatenate([to_column(sampled[pl.ds(step, 1), :]) for step in range(DECODE_STEPS)], axis=0)
    column = lax.broadcasted_iota(jnp.int32, guided.shape, 1) + lax.axis_index("wide") * width
    picked = jnp.sum(jnp.where(column == chosen, guided, 0.0), axis=1, keepdims=True)
    lanes = jnp.concatenate([to_lanes(top), to_lanes(total), to_lanes(picked)], axis=1)
    pad = stats.shape[2] - lanes.shape[1]
    if pad > 0:
        lanes = jnp.concatenate([lanes, jnp.zeros((1, pad), jnp.float32)], axis=1)
    stats[...] = jnp.broadcast_to(lanes[None], stats.shape)


def finish_kernel(guided, stats, blocks, logprobs, tokens):
    count, width = guided.shape
    half = count // DECODE_STEPS
    parts = stats[...].reshape(stats.shape[0], stats.shape[2])
    tops = parts[:, 0:count]
    top = jnp.max(tops, axis=0, keepdims=True)
    total = jnp.sum(parts[:, count : 2 * count] * jnp.exp(tops - top), axis=0, keepdims=True)
    picked = jnp.sum(parts[:, 2 * count : 3 * count], axis=0, keepdims=True)
    normalizer = top + jnp.log(total)
    token = picked - normalizer
    for step in range(DECODE_STEPS):
        tokens[pl.ds(step, 1), :] = token[:, step * half : (step + 1) * half]
    allowed = allowed_entries(blocks, guided.shape)
    result = jnp.where(allowed, guided[...] - to_column(normalizer), 0.0)
    logprobs[...] = result.reshape(logprobs.shape)


def slot_rows(array):
    slots = array.shape[0]
    split = array.reshape(slots, 2, KEY_VALUE_HEADS, HEAD_SIZE)
    return split.transpose(0, 2, 1, 3).reshape(slots * SLOT_ROWS, HEAD_SIZE)


def step_rows(array):
    split = array.reshape(DECODE_STEPS, QUERY_HEADS, HEAD_SIZE)
    return split.transpose(1, 0, 2).reshape(QUERY_HEADS * DECODE_STEPS, HEAD_SIZE)


def shards(
    wide,
    queries,
    cache,
    fresh_key_value,
    lengths,
    residual,
    norm_gain,
    vocab_weight,
    guidance,
    allowed_blocks,
    sampled,
):
    steps, half_pairs, blocks_here = allowed_blocks.shape
    width = vocab_weight.shape[1]
    pairs = guidance.shape[0]
    rows = steps * QUERY_HEADS
    cache_rows = slot_rows(cache[0, 0])
    vmem, smem, hbm = in_vmem(), in_smem(), pl.BlockSpec(memory_space=pltpu.HBM)
    half_rows = jax.ShapeDtypeStruct((rows // 2, HEAD_SIZE), jnp.bfloat16)
    flat = jax.ShapeDtypeStruct((steps * half_pairs, width), jnp.float32)

    def swap(array):
        return lax.ppermute(array, "pair", [(0, 1), (1, 0)])

    mine, theirs = call(
        attend_kernel,
        (half_rows, half_rows),
        [smem] + [hbm] * 5,
        [
            pltpu.VMEM(cache_rows.shape, jnp.bfloat16),
            pltpu.VMEM((cache.shape[2] * SLOT_PITCH, HEAD_SIZE), jnp.float32),
            pltpu.VMEM((rows, HEAD_SIZE), jnp.float32),
            pltpu.VMEM((rows, HEAD_SIZE), jnp.bfloat16),
            pltpu.VMEM((steps * SLOT_ROWS, HEAD_SIZE), jnp.bfloat16),
            pltpu.VMEM((rows, HEAD_SIZE), jnp.bfloat16),
            pltpu.VMEM((QUERY_HEADS, HEAD_SIZE), jnp.float32),
            pltpu.SemaphoreType.DMA((cache.shape[2] // BLOCK + 4,)),
        ],
        limit=60 << 20,
    )(
        lengths,
        step_rows(queries[0, 0]),
        cache_rows,
        slot_rows(fresh_key_value[0, 0]),
        step_rows(residual[0, 0]),
        norm_gain.reshape(QUERY_HEADS, HEAD_SIZE),
    )
    received = swap(theirs)
    own_part, factor = call(
        own_part_kernel,
        (jax.ShapeDtypeStruct(half_rows.shape, jnp.float32), jax.ShapeDtypeStruct((8, HEAD_SIZE), jnp.float32)),
        [smem, vmem],
    )(guidance, mine)
    spread = call(combine_kernel, jax.ShapeDtypeStruct((wide // 2,) + half_rows.shape, jnp.bfloat16), [vmem] * 3)(
        factor, own_part, received
    )
    same_core = [list(range(core, wide, 2)) for core in range(2)]
    near = lax.all_to_all(spread, "wide", 0, 0, axis_index_groups=same_core, tiled=True)
    far = lax.ppermute(near, "wide", [(source, source ^ 1) for source in range(wide)])
    mine, theirs = call(
        project_kernel,
        (flat, flat),
        [vmem] * 3,
        [pltpu.VMEM((pairs * (rows // 2 + 1), HEAD_SIZE), jnp.float32)],
    )(near, far, vocab_weight)

    lanes = pl.cdiv(3 * steps * half_pairs, 128) * 128
    guided, stats = call(
        stats_kernel,
        (flat, jax.ShapeDtypeStruct((wide, 1, lanes), jnp.float32)),
        [vmem] * 4,
    )(mine, swap(theirs), allowed_blocks, sampled)
    logprobs, tokens = call(
        finish_kernel,
        (
            jax.ShapeDtypeStruct((steps, half_pairs, width), jnp.float32),
            jax.ShapeDtypeStruct((steps, half_pairs), jnp.float32),
        ),
        [vmem] * 3,
    )(guided, lax.all_to_all(stats, "wide", 0, 0, tiled=True), allowed_blocks)
    return (logprobs, tokens)


def solution(mesh):
    placed = (
        P("pair", "wide", None, None),
        P("pair", "wide", None, None, None),
        P("pair", "wide", None, None, None),
        P("pair", "wide"),
        P("pair", "wide", None, None),
        P(),
        P("pair", "wide"),
        P(),
        P(None, "pair", "wide"),
        P(None, "pair"),
    )
    return jax.shard_map(
        functools.partial(shards, mesh.shape["wide"]),
        mesh=mesh,
        in_specs=placed,
        out_specs=(P(None, "pair", "wide"), P(None, "pair")),
        check_vma=False,
    )
```

```python
import functools
import math

import jax
import jax.numpy as jnp
from jax import lax
from jax.experimental import pallas as pl
from jax.experimental.pallas import tpu as pltpu
from jax.sharding import PartitionSpec as P

QUERY_HEADS = 64
KEY_VALUE_HEADS = 8
HEAD_SIZE = 128
BLK = 32
DECODE_STEPS = 2
SLOT_ROWS = 2 * KEY_VALUE_HEADS
SLOT_PITCH = SLOT_ROWS + 1
BLOCK = 64
HEAD_ROWS = DECODE_STEPS * (QUERY_HEADS // KEY_VALUE_HEADS)
NEG_FILL = -1e30


def in_vmem():
    return pl.BlockSpec(memory_space=pltpu.VMEM)


def in_smem():
    return pl.BlockSpec(memory_space=pltpu.SMEM)


def call(kernel, out_shape, in_specs, scratch=(), limit=16 << 20, cost=None):
    return pl.pallas_call(
        kernel,
        out_shape=out_shape,
        in_specs=in_specs,
        out_specs=jax.tree.map(lambda _: in_vmem(), out_shape),
        scratch_shapes=list(scratch),
        compiler_params=pltpu.CompilerParams(vmem_limit_bytes=limit),
        cost_estimate=cost,
    )


def attend_kernel(
    lengths, queries_in, cache, fresh_in, residual_in, gain_in, mine, theirs,
    stage, wide_rows, gain_rows, queries, fresh, residual, gain, arrived,
):
    rows = cache.shape[0]
    slots = rows // SLOT_ROWS

    def block_copy(block):
        at = pl.ds(pl.multiple_of(block * (BLOCK * SLOT_ROWS), BLOCK * SLOT_ROWS), BLOCK * SLOT_ROWS)
        return pltpu.make_async_copy(cache.at[at], stage.at[at], arrived.at[block])

    def start(block, carry):
        block_copy(block).start()
        return carry

    def clear(block, carry):
        target = pl.multiple_of(block * (BLOCK * SLOT_PITCH), 8)
        wide_rows[pl.ds(target, BLOCK * SLOT_PITCH), :] = jnp.zeros((BLOCK * SLOT_PITCH, HEAD_SIZE), jnp.float32)
        return carry

    def widen(block, carry):
        block_copy(block).wait()
        source = pl.multiple_of(block * (BLOCK * SLOT_ROWS), BLOCK * SLOT_ROWS)
        target = pl.multiple_of(block * (BLOCK * SLOT_PITCH), 8)
        for slot in range(BLOCK):
            wide_rows[pl.ds(target + slot * SLOT_PITCH, SLOT_ROWS), :] = stage[
                pl.ds(source + slot * SLOT_ROWS, SLOT_ROWS), :
            ].astype(jnp.float32)
        return carry

    blocks = slots // BLOCK
    live_blocks = lax.div(lengths[0, 0] + (BLOCK - 1), BLOCK)
    lax.fori_loop(0, live_blocks, start, 0)
    small = [
        pltpu.make_async_copy(source, target, arrived.at[blocks + index])
        for index, (source, target) in enumerate(
            ((gain_in, gain), (fresh_in, fresh), (queries_in, queries), (residual_in, residual))
        )
    ]
    for copy in small:
        copy.start()
    lax.fori_loop(live_blocks, blocks, clear, 0)
    lax.fori_loop(0, live_blocks, widen, 0)
    for copy in small:
        copy.wait()
    gain_rows[pl.ds(0, QUERY_HEADS, stride=2), :] = gain[...]
    gain_rows[pl.ds(1, QUERY_HEADS, stride=2), :] = gain[...]
    for step in range(DECODE_STEPS):
        wide_rows[pl.ds((slots - DECODE_STEPS + step) * SLOT_PITCH, SLOT_ROWS), :] = fresh[
            pl.ds(step * SLOT_ROWS, SLOT_ROWS), :
        ].astype(jnp.float32)
    factor = 1.0 / math.sqrt(HEAD_SIZE)
    scores = []
    for head in range(KEY_VALUE_HEADS):
        keys = wide_rows[pl.ds(2 * head, slots, stride=SLOT_PITCH), :].astype(jnp.bfloat16)
        scores.append(
            lax.dot_general(
                queries[pl.ds(head * HEAD_ROWS, HEAD_ROWS), :],
                keys,
                (((1,), (1,)), ((), ())),
                preferred_element_type=jnp.float32,
            )
        )
    score = jnp.concatenate(scores, axis=0)
    slot = lax.broadcasted_iota(jnp.int32, score.shape, 1)
    step_of_row = lax.rem(lax.broadcasted_iota(jnp.int32, score.shape, 0), DECODE_STEPS)
    first_fresh = slots - DECODE_STEPS
    live = (slot < lengths[0, 0]) | ((slot >= first_fresh) & (slot - first_fresh <= step_of_row))
    score = jnp.where(live, score * factor, NEG_FILL)
    weight = jnp.exp(score - jnp.max(score, axis=1, keepdims=True))
    weight = (weight / jnp.sum(weight, axis=1, keepdims=True)).astype(jnp.bfloat16)
    mixed = []
    for head in range(KEY_VALUE_HEADS):
        values = wide_rows[pl.ds(2 * head + 1, slots, stride=SLOT_PITCH), :].astype(jnp.bfloat16)
        mixed.append(
            jnp.dot(
                weight[head * HEAD_ROWS : (head + 1) * HEAD_ROWS], values, preferred_element_type=jnp.float32
            )
        )
    hidden = jnp.concatenate(mixed, axis=0) + residual[...].astype(jnp.float32)
    row_power = jnp.sum(hidden * hidden, axis=1, keepdims=True)
    step_of_row = lax.rem(lax.broadcasted_iota(jnp.int32, row_power.shape, 0), DECODE_STEPS)
    scale = jnp.zeros_like(row_power)
    for step in range(DECODE_STEPS):
        power = jnp.sum(jnp.where(step_of_row == step, row_power, 0.0), axis=0, keepdims=True)
        power = power / (QUERY_HEADS * HEAD_SIZE)
        scale = jnp.where(step_of_row == step, lax.rsqrt(power + 1e-05), scale)
    normed = (hidden * scale * gain_rows[...]).astype(jnp.bfloat16)
    half = normed.shape[0] // 2
    first = lax.axis_index("pair") == 0
    mine[...] = jnp.where(first, normed[:half], normed[half:])
    theirs[...] = jnp.where(first, normed[half:], normed[:half])


def branch_factor(scale, branch):
    guidance = scale[lax.axis_index("wide")]
    return jnp.where(branch == 0, guidance, 1.0 - guidance)


def own_part_kernel(scale, mine, out, factor):
    branch = lax.axis_index("pair")
    out[...] = branch_factor(scale, branch) * mine[...].astype(jnp.float32)
    factor[...] = jnp.full(factor.shape, branch_factor(scale, 1 - branch), jnp.float32)


def combine_kernel(factor, own_part, received, spread):
    other_part = factor[0:1, :] * received[...].astype(jnp.float32)
    guided = (own_part[...] + other_part).astype(jnp.bfloat16)
    spread[...] = jnp.broadcast_to(guided[None], spread.shape)


def project_kernel(rows, weight, other_weight, mine, theirs, wide_rows):
    pairs, per_pair, lanes = rows.shape
    half = pairs // 2
    pitch = per_pair + 1
    for pair in range(pairs):
        wide_rows[pl.ds(pair * pitch, per_pair), :] = rows[pair].astype(jnp.float32)

    def head_rows(head):
        steps = [
            wide_rows[pl.ds(head * DECODE_STEPS + step, pairs, stride=pitch), :] for step in range(DECODE_STEPS)
        ]
        return jnp.concatenate(steps, axis=0).astype(jnp.bfloat16)

    totals = [jnp.zeros((DECODE_STEPS * pairs, weight.shape[1]), jnp.float32)] * 2
    for two in range(per_pair // DECODE_STEPS // 2):
        left = jnp.concatenate([head_rows(2 * two), head_rows(2 * two + 1)], axis=1)
        totals = [
            total + jnp.dot(left, part[pl.ds(two * 2 * lanes, 2 * lanes), :], preferred_element_type=jnp.float32)
            for total, part in zip(totals, (weight, other_weight))
        ]
    total = jnp.concatenate(totals, axis=1)
    low, high = (
        jnp.concatenate(
            [total[step * pairs + part * half : step * pairs + (part + 1) * half] for step in range(DECODE_STEPS)],
            axis=0,
        )
        for part in range(2)
    )
    first = lax.axis_index("pair") == 0
    mine[...] = jnp.where(first, low, high)
    theirs[...] = jnp.where(first, high, low)


def to_lanes(column):
    size = column.shape[0]
    eye = lax.broadcasted_iota(jnp.int32, (size, size), 0) == lax.broadcasted_iota(jnp.int32, (size, size), 1)
    return jnp.sum(jnp.where(eye, column, jnp.zeros_like(column)), axis=0, keepdims=True)


def to_column(lanes):
    size = lanes.shape[1]
    eye = lax.broadcasted_iota(jnp.int32, (size, size), 0) == lax.broadcasted_iota(jnp.int32, (size, size), 1)
    return jnp.sum(jnp.where(eye, lanes, jnp.zeros_like(lanes)), axis=1, keepdims=True)


def allowed_entries(blocks, parity, width):
    count = blocks.shape[1] // 2
    flags = jnp.concatenate(
        [blocks[step, pl.ds(2 * pair + parity, 1), :] for step in range(DECODE_STEPS) for pair in range(count)], axis=0
    )
    block = lax.broadcasted_iota(jnp.int32, (flags.shape[0], width), 1) // BLK
    flag = jnp.zeros(block.shape, jnp.int32)
    for index in range(blocks.shape[2]):
        flag = jnp.where(block == index, flags[:, index : index + 1], flag)
    return flag > 0


def stats_kernel(mine, received, blocks, other_blocks, sampled, guided_out, other_out, stats):
    guided = mine[...] + received[...]
    rows, both = guided.shape
    width = both // 2
    guided_out[...] = guided[:, :width]
    other_out[...] = guided[:, width:]
    position = lax.axis_index("wide")
    parity = position % 2
    allowed = jnp.concatenate(
        [
            jnp.where(parity == 0, *(allowed_entries(part, q, width).astype(jnp.int32) for q in range(2)))
            for part in (blocks, other_blocks)
        ],
        axis=1,
    ) > 0
    top = jnp.max(jnp.where(allowed, guided, NEG_FILL), axis=1, keepdims=True)
    total = jnp.sum(jnp.where(allowed, jnp.exp(guided - top), 0.0), axis=1, keepdims=True)
    count = rows // DECODE_STEPS
    spot = (count, 2 * count)
    of_parity = lax.broadcasted_iota(jnp.int32, spot, 1) == 2 * lax.broadcasted_iota(jnp.int32, spot, 0) + parity
    chosen = jnp.concatenate(
        [
            jnp.sum(jnp.where(of_parity, sampled[pl.ds(step, 1), :], 0), axis=1, keepdims=True)
            for step in range(DECODE_STEPS)
        ],
        axis=0,
    )
    lane = lax.broadcasted_iota(jnp.int32, guided.shape, 1)
    column = jnp.where(lane < width, position * width + lane, (position ^ 1) * width + lane - width)
    picked = jnp.sum(jnp.where(column == chosen, guided, 0.0), axis=1, keepdims=True)
    stats[...] = jnp.broadcast_to(
        jnp.concatenate([to_lanes(top), to_lanes(total), to_lanes(picked)], axis=0)[None], stats.shape
    )


def finish_kernel(guided, received, stats, blocks, logprobs, tokens):
    rows, width = guided.shape
    count = rows // DECODE_STEPS
    chips = stats.shape[0] // 2
    near = lax.axis_index("wide") % 2
    token_rows = [jnp.zeros((1, 2 * count), jnp.float32)] * DECODE_STEPS
    results = []
    for parity in range(2):
        parts = [stats[2 * chip + parity] for chip in range(chips)]
        top = functools.reduce(jnp.maximum, [part[0:1] for part in parts])
        total = sum(part[1:2] * jnp.exp(part[0:1] - top) for part in parts)
        normalizer = top + jnp.log(total)
        token = sum(part[2:3] for part in parts) - normalizer
        values = jnp.where(near == parity, guided[...], received[...])
        results.append(jnp.where(allowed_entries(blocks, parity, width), values - to_column(normalizer), 0.0))
        spot = (count, 2 * count)
        here = lax.broadcasted_iota(jnp.int32, spot, 1) == 2 * lax.broadcasted_iota(jnp.int32, spot, 0) + parity
        for step in range(DECODE_STEPS):
            mine = slice(step * count, (step + 1) * count)
            spread = jnp.sum(jnp.where(here, to_column(token[:, mine]), 0.0), axis=0, keepdims=True)
            token_rows[step] = token_rows[step] + spread
    for step in range(DECODE_STEPS):
        tokens[pl.ds(step, 1), :] = token_rows[step]
        for pair in range(count):
            row = step * count + pair
            for parity, result in enumerate(results):
                logprobs[step, pl.ds(2 * pair + parity, 1), :] = result[row : row + 1]


def slot_rows(array):
    slots = array.shape[0]
    split = array.reshape(slots, 2, KEY_VALUE_HEADS, HEAD_SIZE)
    return split.transpose(0, 2, 1, 3).reshape(slots * SLOT_ROWS, HEAD_SIZE)


def step_rows(array):
    split = array.reshape(DECODE_STEPS, QUERY_HEADS, HEAD_SIZE)
    return split.transpose(1, 0, 2).reshape(QUERY_HEADS * DECODE_STEPS, HEAD_SIZE)


def shards(
    wide,
    queries,
    cache,
    fresh_key_value,
    lengths,
    residual,
    norm_gain,
    vocab_weight,
    guidance,
    allowed_blocks,
    sampled,
):
    steps, half_pairs, blocks_here = allowed_blocks.shape
    width = vocab_weight.shape[1]
    pairs = guidance.shape[0]
    rows = steps * QUERY_HEADS
    cache_rows = slot_rows(cache[0, 0])
    vmem, smem, hbm = in_vmem(), in_smem(), pl.BlockSpec(memory_space=pltpu.HBM)
    half_rows = jax.ShapeDtypeStruct((rows // 2, HEAD_SIZE), jnp.bfloat16)
    chips = wide // 2
    flat = jax.ShapeDtypeStruct((steps * chips // 2, width), jnp.float32)
    flat_two = jax.ShapeDtypeStruct((steps * chips // 2, 2 * width), jnp.float32)

    def other_core(array):
        return lax.ppermute(array, "wide", [(source, source ^ 1) for source in range(wide)])

    def swap(array):
        return lax.ppermute(array, "pair", [(0, 1), (1, 0)])

    mine, theirs = call(
        attend_kernel,
        (half_rows, half_rows),
        [smem] + [hbm] * 5,
        [
            pltpu.VMEM(cache_rows.shape, jnp.bfloat16),
            pltpu.VMEM((cache.shape[2] * SLOT_PITCH, HEAD_SIZE), jnp.float32),
            pltpu.VMEM((rows, HEAD_SIZE), jnp.float32),
            pltpu.VMEM((rows, HEAD_SIZE), jnp.bfloat16),
            pltpu.VMEM((steps * SLOT_ROWS, HEAD_SIZE), jnp.bfloat16),
            pltpu.VMEM((rows, HEAD_SIZE), jnp.bfloat16),
            pltpu.VMEM((QUERY_HEADS, HEAD_SIZE), jnp.float32),
            pltpu.SemaphoreType.DMA((cache.shape[2] // BLOCK + 4,)),
        ],
        limit=60 << 20,
    )(
        lengths,
        step_rows(queries[0, 0]),
        cache_rows,
        slot_rows(fresh_key_value[0, 0]),
        step_rows(residual[0, 0]),
        norm_gain.reshape(QUERY_HEADS, HEAD_SIZE),
    )
    received = swap(theirs)
    own_part, factor = call(
        own_part_kernel,
        (jax.ShapeDtypeStruct(half_rows.shape, jnp.float32), jax.ShapeDtypeStruct((8, HEAD_SIZE), jnp.float32)),
        [smem, vmem],
    )(guidance, mine)
    weight_in, received = lax.optimization_barrier((vocab_weight, received))
    other_weight, other_blocks = other_core(weight_in), other_core(allowed_blocks)
    spread = call(combine_kernel, jax.ShapeDtypeStruct((chips,) + half_rows.shape, jnp.bfloat16), [vmem] * 3)(
        factor, own_part, received
    )
    same_core = [list(range(core, wide, 2)) for core in range(2)]
    gathered = lax.all_to_all(spread, "wide", 0, 0, axis_index_groups=same_core, tiled=True)
    mine, theirs = call(
        project_kernel,
        (flat_two, flat_two),
        [vmem] * 3,
        [pltpu.VMEM((chips * (rows // 2 + 1), HEAD_SIZE), jnp.float32)],
    )(gathered, vocab_weight, other_weight)
    guided, other_guided, stats = call(
        stats_kernel,
        (flat, flat, jax.ShapeDtypeStruct((wide, 3, steps * chips // 2), jnp.float32)),
        [vmem] * 5,
    )(mine, swap(theirs), allowed_blocks, other_blocks, sampled)
    other_guided = other_core(other_guided)
    logprobs, tokens = call(
        finish_kernel,
        (
            jax.ShapeDtypeStruct((steps, half_pairs, width), jnp.float32),
            jax.ShapeDtypeStruct((steps, half_pairs), jnp.float32),
        ),
        [vmem] * 4,
    )(guided, other_guided, lax.all_to_all(stats, "wide", 0, 0, tiled=True), allowed_blocks)
    return (logprobs, tokens)


def solution(mesh):
    placed = (
        P("pair", "wide", None, None),
        P("pair", "wide", None, None, None),
        P("pair", "wide", None, None, None),
        P("pair", "wide"),
        P("pair", "wide", None, None),
        P(),
        P("pair", "wide"),
        P(),
        P(None, "pair", "wide"),
        P(None, "pair"),
    )
    return jax.shard_map(
        functools.partial(shards, mesh.shape["wide"]),
        mesh=mesh,
        in_specs=placed,
        out_specs=(P(None, "pair", "wide"), P(None, "pair")),
        check_vma=False,
    )
```

```python
import functools
import math

import jax
import jax.numpy as jnp
from jax import lax
from jax.experimental import pallas as pl
from jax.experimental.pallas import tpu as pltpu
from jax.sharding import PartitionSpec as P

QUERY_HEADS = 64
KEY_VALUE_HEADS = 8
HEAD_SIZE = 128
BLK = 32
DECODE_STEPS = 2
SLOT_ROWS = 2 * KEY_VALUE_HEADS
SLOT_PITCH = SLOT_ROWS + 1
BLOCK = 64
HEAD_ROWS = DECODE_STEPS * (QUERY_HEADS // KEY_VALUE_HEADS)
NEG_FILL = -1e30


def in_vmem():
    return pl.BlockSpec(memory_space=pltpu.VMEM)


def in_smem():
    return pl.BlockSpec(memory_space=pltpu.SMEM)


def call(kernel, out_shape, in_specs, scratch=(), limit=16 << 20, cost=None):
    return pl.pallas_call(
        kernel,
        out_shape=out_shape,
        in_specs=in_specs,
        out_specs=jax.tree.map(lambda _: in_vmem(), out_shape),
        scratch_shapes=list(scratch),
        compiler_params=pltpu.CompilerParams(vmem_limit_bytes=limit),
        cost_estimate=cost,
    )


def attend_kernel(
    lengths, queries_in, cache, fresh_in, residual_in, gain_in, mine, theirs,
    stage, wide_rows, gain_rows, queries, fresh, residual, gain, arrived,
):
    rows = cache.shape[0]
    slots = rows // SLOT_ROWS

    def block_copy(block):
        at = pl.ds(pl.multiple_of(block * (BLOCK * SLOT_ROWS), BLOCK * SLOT_ROWS), BLOCK * SLOT_ROWS)
        return pltpu.make_async_copy(cache.at[at], stage.at[at], arrived.at[block])

    def start(block, carry):
        block_copy(block).start()
        return carry

    def clear(block, carry):
        target = pl.multiple_of(block * (BLOCK * SLOT_PITCH), 8)
        wide_rows[pl.ds(target, BLOCK * SLOT_PITCH), :] = jnp.zeros((BLOCK * SLOT_PITCH, HEAD_SIZE), jnp.float32)
        return carry

    def widen(block, carry):
        block_copy(block).wait()
        source = pl.multiple_of(block * (BLOCK * SLOT_ROWS), BLOCK * SLOT_ROWS)
        target = pl.multiple_of(block * (BLOCK * SLOT_PITCH), 8)
        for slot in range(BLOCK):
            wide_rows[pl.ds(target + slot * SLOT_PITCH, SLOT_ROWS), :] = stage[
                pl.ds(source + slot * SLOT_ROWS, SLOT_ROWS), :
            ].astype(jnp.float32)
        return carry

    blocks = slots // BLOCK
    live_blocks = lax.div(lengths[0, 0] + (BLOCK - 1), BLOCK)
    lax.fori_loop(0, live_blocks, start, 0)
    small = [
        pltpu.make_async_copy(source, target, arrived.at[blocks + index])
        for index, (source, target) in enumerate(
            ((gain_in, gain), (fresh_in, fresh), (queries_in, queries), (residual_in, residual))
        )
    ]
    for copy in small:
        copy.start()
    lax.fori_loop(live_blocks, blocks, clear, 0)
    lax.fori_loop(0, live_blocks, widen, 0)
    for copy in small:
        copy.wait()
    gain_rows[pl.ds(0, QUERY_HEADS, stride=2), :] = gain[...]
    gain_rows[pl.ds(1, QUERY_HEADS, stride=2), :] = gain[...]
    for step in range(DECODE_STEPS):
        wide_rows[pl.ds((slots - DECODE_STEPS + step) * SLOT_PITCH, SLOT_ROWS), :] = fresh[
            pl.ds(step * SLOT_ROWS, SLOT_ROWS), :
        ].astype(jnp.float32)
    factor = 1.0 / math.sqrt(HEAD_SIZE)
    scores = []
    for head in range(KEY_VALUE_HEADS):
        keys = wide_rows[pl.ds(2 * head, slots, stride=SLOT_PITCH), :].astype(jnp.bfloat16)
        scores.append(
            lax.dot_general(
                queries[pl.ds(head * HEAD_ROWS, HEAD_ROWS), :],
                keys,
                (((1,), (1,)), ((), ())),
                preferred_element_type=jnp.float32,
            )
        )
    score = jnp.concatenate(scores, axis=0)
    slot = lax.broadcasted_iota(jnp.int32, score.shape, 1)
    step_of_row = lax.rem(lax.broadcasted_iota(jnp.int32, score.shape, 0), DECODE_STEPS)
    first_fresh = slots - DECODE_STEPS
    live = (slot < lengths[0, 0]) | ((slot >= first_fresh) & (slot - first_fresh <= step_of_row))
    score = jnp.where(live, score * factor, NEG_FILL)
    weight = jnp.exp(score - jnp.max(score, axis=1, keepdims=True))
    weight = (weight / jnp.sum(weight, axis=1, keepdims=True)).astype(jnp.bfloat16)
    mixed = []
    for head in range(KEY_VALUE_HEADS):
        values = wide_rows[pl.ds(2 * head + 1, slots, stride=SLOT_PITCH), :].astype(jnp.bfloat16)
        mixed.append(
            jnp.dot(
                weight[head * HEAD_ROWS : (head + 1) * HEAD_ROWS], values, preferred_element_type=jnp.float32
            )
        )
    hidden = jnp.concatenate(mixed, axis=0) + residual[...].astype(jnp.float32)
    row_power = jnp.sum(hidden * hidden, axis=1, keepdims=True)
    step_of_row = lax.rem(lax.broadcasted_iota(jnp.int32, row_power.shape, 0), DECODE_STEPS)
    scale = jnp.zeros_like(row_power)
    for step in range(DECODE_STEPS):
        power = jnp.sum(jnp.where(step_of_row == step, row_power, 0.0), axis=0, keepdims=True)
        power = power / (QUERY_HEADS * HEAD_SIZE)
        scale = jnp.where(step_of_row == step, lax.rsqrt(power + 1e-05), scale)
    normed = (hidden * scale * gain_rows[...]).astype(jnp.bfloat16)
    half = normed.shape[0] // 2
    first = lax.axis_index("pair") == 0
    mine[...] = jnp.where(first, normed[:half], normed[half:])
    theirs[...] = jnp.where(first, normed[half:], normed[:half])


def branch_factor(scale, branch):
    guidance = scale[lax.axis_index("wide")]
    return jnp.where(branch == 0, guidance, 1.0 - guidance)


def own_part_kernel(scale, mine, out, factor):
    branch = lax.axis_index("pair")
    out[...] = branch_factor(scale, branch) * mine[...].astype(jnp.float32)
    factor[...] = jnp.full(factor.shape, branch_factor(scale, 1 - branch), jnp.float32)


def combine_kernel(factor, own_part, received, spread):
    other_part = factor[0:1, :] * received[...].astype(jnp.float32)
    guided = (own_part[...] + other_part).astype(jnp.bfloat16)
    spread[...] = jnp.broadcast_to(guided[None], spread.shape)


def project_kernel(rows, weight, other_weight, mine, theirs, wide_rows):
    pairs, per_pair, lanes = rows.shape
    half = pairs // 2
    pitch = per_pair + 1
    for pair in range(pairs):
        wide_rows[pl.ds(pair * pitch, per_pair), :] = rows[pair].astype(jnp.float32)

    def head_rows(head):
        steps = [
            wide_rows[pl.ds(head * DECODE_STEPS + step, pairs, stride=pitch), :] for step in range(DECODE_STEPS)
        ]
        return jnp.concatenate(steps, axis=0).astype(jnp.bfloat16)

    totals = [jnp.zeros((DECODE_STEPS * pairs, weight.shape[1]), jnp.float32)] * 2
    for two in range(per_pair // DECODE_STEPS // 2):
        left = jnp.concatenate([head_rows(2 * two), head_rows(2 * two + 1)], axis=1)
        totals = [
            total + jnp.dot(left, part[pl.ds(two * 2 * lanes, 2 * lanes), :], preferred_element_type=jnp.float32)
            for total, part in zip(totals, (weight, other_weight))
        ]
    total = jnp.concatenate(totals, axis=1)
    low, high = (
        jnp.concatenate(
            [total[step * pairs + part * half : step * pairs + (part + 1) * half] for step in range(DECODE_STEPS)],
            axis=0,
        )
        for part in range(2)
    )
    first = lax.axis_index("pair") == 0
    mine[...] = jnp.where(first, low, high)
    theirs[...] = jnp.where(first, high, low)


def to_lanes(column):
    size = column.shape[0]
    eye = lax.broadcasted_iota(jnp.int32, (size, size), 0) == lax.broadcasted_iota(jnp.int32, (size, size), 1)
    return jnp.sum(jnp.where(eye, column, jnp.zeros_like(column)), axis=0, keepdims=True)


def to_column(lanes):
    size = lanes.shape[1]
    eye = lax.broadcasted_iota(jnp.int32, (size, size), 0) == lax.broadcasted_iota(jnp.int32, (size, size), 1)
    return jnp.sum(jnp.where(eye, lanes, jnp.zeros_like(lanes)), axis=1, keepdims=True)


def allowed_entries(blocks, parity, width):
    count = blocks.shape[1] // 2
    flags = jnp.concatenate(
        [blocks[step, pl.ds(2 * pair + parity, 1), :] for step in range(DECODE_STEPS) for pair in range(count)], axis=0
    )
    block = lax.broadcasted_iota(jnp.int32, (flags.shape[0], width), 1) // BLK
    flag = jnp.zeros(block.shape, jnp.int32)
    for index in range(blocks.shape[2]):
        flag = jnp.where(block == index, flags[:, index : index + 1], flag)
    return flag > 0


def stats_kernel(mine, received, blocks, other_blocks, sampled, guided_out, other_out, stats):
    guided = mine[...] + received[...]
    rows, both = guided.shape
    width = both // 2
    guided_out[...] = guided[:, :width]
    other_out[...] = guided[:, width:]
    position = lax.axis_index("wide")
    parity = position % 2
    allowed = jnp.concatenate(
        [
            jnp.where(parity == 0, *(allowed_entries(part, q, width).astype(jnp.int32) for q in range(2)))
            for part in (blocks, other_blocks)
        ],
        axis=1,
    ) > 0
    top = jnp.max(jnp.where(allowed, guided, NEG_FILL), axis=1, keepdims=True)
    total = jnp.sum(jnp.where(allowed, jnp.exp(guided - top), 0.0), axis=1, keepdims=True)
    count = rows // DECODE_STEPS
    spot = (count, 2 * count)
    of_parity = lax.broadcasted_iota(jnp.int32, spot, 1) == 2 * lax.broadcasted_iota(jnp.int32, spot, 0) + parity
    chosen = jnp.concatenate(
        [
            jnp.sum(jnp.where(of_parity, sampled[pl.ds(step, 1), :], 0), axis=1, keepdims=True)
            for step in range(DECODE_STEPS)
        ],
        axis=0,
    )
    lane = lax.broadcasted_iota(jnp.int32, guided.shape, 1)
    column = jnp.where(lane < width, position * width + lane, (position ^ 1) * width + lane - width)
    picked = jnp.sum(jnp.where(column == chosen, guided, 0.0), axis=1, keepdims=True)
    stats[...] = jnp.broadcast_to(
        jnp.concatenate([to_lanes(top), to_lanes(total), to_lanes(picked)], axis=0)[None], stats.shape
    )


def finish_kernel(guided, received, stats, blocks, logprobs, tokens):
    rows, width = guided.shape
    count = rows // DECODE_STEPS
    chips = stats.shape[0] // 2
    near = lax.axis_index("wide") % 2
    token_rows = [jnp.zeros((1, 2 * count), jnp.float32)] * DECODE_STEPS
    results = []
    for parity in range(2):
        parts = [stats[2 * chip + parity] for chip in range(chips)]
        top = functools.reduce(jnp.maximum, [part[0:1] for part in parts])
        total = sum(part[1:2] * jnp.exp(part[0:1] - top) for part in parts)
        normalizer = top + jnp.log(total)
        token = sum(part[2:3] for part in parts) - normalizer
        values = jnp.where(near == parity, guided[...], received[...])
        results.append(jnp.where(allowed_entries(blocks, parity, width), values - to_column(normalizer), 0.0))
        spot = (count, 2 * count)
        here = lax.broadcasted_iota(jnp.int32, spot, 1) == 2 * lax.broadcasted_iota(jnp.int32, spot, 0) + parity
        for step in range(DECODE_STEPS):
            mine = slice(step * count, (step + 1) * count)
            spread = jnp.sum(jnp.where(here, to_column(token[:, mine]), 0.0), axis=0, keepdims=True)
            token_rows[step] = token_rows[step] + spread
    for step in range(DECODE_STEPS):
        tokens[pl.ds(step, 1), :] = token_rows[step]
        for pair in range(count):
            row = step * count + pair
            for parity, result in enumerate(results):
                logprobs[step, pl.ds(2 * pair + parity, 1), :] = result[row : row + 1]


def slot_rows(array):
    slots = array.shape[0]
    split = array.reshape(slots, 2, KEY_VALUE_HEADS, HEAD_SIZE)
    return split.transpose(0, 2, 1, 3).reshape(slots * SLOT_ROWS, HEAD_SIZE)


def step_rows(array):
    split = array.reshape(DECODE_STEPS, QUERY_HEADS, HEAD_SIZE)
    return split.transpose(1, 0, 2).reshape(QUERY_HEADS * DECODE_STEPS, HEAD_SIZE)


def shards(
    wide,
    queries,
    cache,
    fresh_key_value,
    lengths,
    residual,
    norm_gain,
    vocab_weight,
    guidance,
    allowed_blocks,
    sampled,
):
    steps, half_pairs, blocks_here = allowed_blocks.shape
    width = vocab_weight.shape[1]
    pairs = guidance.shape[0]
    rows = steps * QUERY_HEADS
    cache_rows = slot_rows(cache[0, 0])
    vmem, smem, hbm = in_vmem(), in_smem(), pl.BlockSpec(memory_space=pltpu.HBM)
    half_rows = jax.ShapeDtypeStruct((rows // 2, HEAD_SIZE), jnp.bfloat16)
    chips = wide // 2
    flat = jax.ShapeDtypeStruct((steps * chips // 2, width), jnp.float32)
    flat_two = jax.ShapeDtypeStruct((steps * chips // 2, 2 * width), jnp.float32)

    def other_core(array):
        return lax.ppermute(array, "wide", [(source, source ^ 1) for source in range(wide)])

    def swap(array):
        return lax.ppermute(array, "pair", [(0, 1), (1, 0)])

    mine, theirs = call(
        attend_kernel,
        (half_rows, half_rows),
        [smem] + [hbm] * 5,
        [
            pltpu.VMEM(cache_rows.shape, jnp.bfloat16),
            pltpu.VMEM((cache.shape[2] * SLOT_PITCH, HEAD_SIZE), jnp.float32),
            pltpu.VMEM((rows, HEAD_SIZE), jnp.float32),
            pltpu.VMEM((rows, HEAD_SIZE), jnp.bfloat16),
            pltpu.VMEM((steps * SLOT_ROWS, HEAD_SIZE), jnp.bfloat16),
            pltpu.VMEM((rows, HEAD_SIZE), jnp.bfloat16),
            pltpu.VMEM((QUERY_HEADS, HEAD_SIZE), jnp.float32),
            pltpu.SemaphoreType.DMA((cache.shape[2] // BLOCK + 4,)),
        ],
        limit=60 << 20,
    )(
        lengths,
        step_rows(queries[0, 0]),
        cache_rows,
        slot_rows(fresh_key_value[0, 0]),
        step_rows(residual[0, 0]),
        norm_gain.reshape(QUERY_HEADS, HEAD_SIZE),
    )
    received = swap(theirs)
    own_part, factor = call(
        own_part_kernel,
        (jax.ShapeDtypeStruct(half_rows.shape, jnp.float32), jax.ShapeDtypeStruct((8, HEAD_SIZE), jnp.float32)),
        [smem, vmem],
    )(guidance, mine)
    weight_in, own_part, received = lax.optimization_barrier((vocab_weight, own_part, received))
    other_weight, other_blocks = other_core(weight_in), other_core(allowed_blocks)
    spread = call(combine_kernel, jax.ShapeDtypeStruct((chips,) + half_rows.shape, jnp.bfloat16), [vmem] * 3)(
        factor, own_part, received
    )
    same_core = [list(range(core, wide, 2)) for core in range(2)]
    gathered = lax.all_to_all(spread, "wide", 0, 0, axis_index_groups=same_core, tiled=True)
    mine, theirs = call(
        project_kernel,
        (flat_two, flat_two),
        [vmem] * 3,
        [pltpu.VMEM((chips * (rows // 2 + 1), HEAD_SIZE), jnp.float32)],
    )(gathered, vocab_weight, other_weight)
    guided, other_guided, stats = call(
        stats_kernel,
        (flat, flat, jax.ShapeDtypeStruct((wide, 3, steps * chips // 2), jnp.float32)),
        [vmem] * 5,
    )(mine, swap(theirs), allowed_blocks, other_blocks, sampled)
    other_guided = other_core(other_guided)
    logprobs, tokens = call(
        finish_kernel,
        (
            jax.ShapeDtypeStruct((steps, half_pairs, width), jnp.float32),
            jax.ShapeDtypeStruct((steps, half_pairs), jnp.float32),
        ),
        [vmem] * 4,
    )(guided, other_guided, lax.all_to_all(stats, "wide", 0, 0, tiled=True), allowed_blocks)
    return (logprobs, tokens)


def solution(mesh):
    placed = (
        P("pair", "wide", None, None),
        P("pair", "wide", None, None, None),
        P("pair", "wide", None, None, None),
        P("pair", "wide"),
        P("pair", "wide", None, None),
        P(),
        P("pair", "wide"),
        P(),
        P(None, "pair", "wide"),
        P(None, "pair"),
    )
    return jax.shard_map(
        functools.partial(shards, mesh.shape["wide"]),
        mesh=mesh,
        in_specs=placed,
        out_specs=(P(None, "pair", "wide"), P(None, "pair")),
        check_vma=False,
    )
```

```python
import functools
import math

import jax
import jax.numpy as jnp
from jax import lax
from jax.experimental import pallas as pl
from jax.experimental.pallas import tpu as pltpu
from jax.sharding import PartitionSpec as P

QUERY_HEADS = 64
KEY_VALUE_HEADS = 8
HEAD_SIZE = 128
BLK = 32
DECODE_STEPS = 2
SLOT_ROWS = 2 * KEY_VALUE_HEADS
SLOT_PITCH = SLOT_ROWS + 1
BLOCK = 64
HEAD_ROWS = DECODE_STEPS * (QUERY_HEADS // KEY_VALUE_HEADS)
NEG_FILL = -1e30


def in_vmem():
    return pl.BlockSpec(memory_space=pltpu.VMEM)


def in_smem():
    return pl.BlockSpec(memory_space=pltpu.SMEM)


def call(kernel, out_shape, in_specs, scratch=(), limit=16 << 20, cost=None):
    return pl.pallas_call(
        kernel,
        out_shape=out_shape,
        in_specs=in_specs,
        out_specs=jax.tree.map(lambda _: in_vmem(), out_shape),
        scratch_shapes=list(scratch),
        compiler_params=pltpu.CompilerParams(vmem_limit_bytes=limit),
        cost_estimate=cost,
    )


def attend_kernel(
    lengths, queries_in, cache, fresh_in, residual_in, gain_in, mine, theirs,
    stage, wide_rows, gain_rows, queries, fresh, residual, gain, arrived,
):
    rows = cache.shape[0]
    slots = rows // SLOT_ROWS

    def block_copy(block):
        at = pl.ds(pl.multiple_of(block * (BLOCK * SLOT_ROWS), BLOCK * SLOT_ROWS), BLOCK * SLOT_ROWS)
        return pltpu.make_async_copy(cache.at[at], stage.at[at], arrived.at[block])

    def start(block, carry):
        block_copy(block).start()
        return carry

    def clear(block, carry):
        target = pl.multiple_of(block * (BLOCK * SLOT_PITCH), 8)
        wide_rows[pl.ds(target, BLOCK * SLOT_PITCH), :] = jnp.zeros((BLOCK * SLOT_PITCH, HEAD_SIZE), jnp.float32)
        return carry

    def widen(block, carry):
        block_copy(block).wait()
        source = pl.multiple_of(block * (BLOCK * SLOT_ROWS), BLOCK * SLOT_ROWS)
        target = pl.multiple_of(block * (BLOCK * SLOT_PITCH), 8)
        for slot in range(BLOCK):
            wide_rows[pl.ds(target + slot * SLOT_PITCH, SLOT_ROWS), :] = stage[
                pl.ds(source + slot * SLOT_ROWS, SLOT_ROWS), :
            ].astype(jnp.float32)
        return carry

    blocks = slots // BLOCK
    live_blocks = lax.div(lengths[0, 0] + (BLOCK - 1), BLOCK)
    lax.fori_loop(0, live_blocks, start, 0)
    small = [
        pltpu.make_async_copy(source, target, arrived.at[blocks + index])
        for index, (source, target) in enumerate(
            ((gain_in, gain), (fresh_in, fresh), (queries_in, queries), (residual_in, residual))
        )
    ]
    for copy in small:
        copy.start()
    lax.fori_loop(live_blocks, blocks, clear, 0)
    lax.fori_loop(0, live_blocks, widen, 0)
    for copy in small:
        copy.wait()
    gain_rows[pl.ds(0, QUERY_HEADS, stride=2), :] = gain[...]
    gain_rows[pl.ds(1, QUERY_HEADS, stride=2), :] = gain[...]
    for step in range(DECODE_STEPS):
        wide_rows[pl.ds((slots - DECODE_STEPS + step) * SLOT_PITCH, SLOT_ROWS), :] = fresh[
            pl.ds(step * SLOT_ROWS, SLOT_ROWS), :
        ].astype(jnp.float32)
    factor = 1.0 / math.sqrt(HEAD_SIZE)
    scores = []
    for head in range(KEY_VALUE_HEADS):
        keys = wide_rows[pl.ds(2 * head, slots, stride=SLOT_PITCH), :].astype(jnp.bfloat16)
        scores.append(
            lax.dot_general(
                queries[pl.ds(head * HEAD_ROWS, HEAD_ROWS), :],
                keys,
                (((1,), (1,)), ((), ())),
                preferred_element_type=jnp.float32,
            )
        )
    score = jnp.concatenate(scores, axis=0)
    slot = lax.broadcasted_iota(jnp.int32, score.shape, 1)
    step_of_row = lax.rem(lax.broadcasted_iota(jnp.int32, score.shape, 0), DECODE_STEPS)
    first_fresh = slots - DECODE_STEPS
    live = (slot < lengths[0, 0]) | ((slot >= first_fresh) & (slot - first_fresh <= step_of_row))
    score = jnp.where(live, score * factor, NEG_FILL)
    weight = jnp.exp(score - jnp.max(score, axis=1, keepdims=True))
    weight = (weight / jnp.sum(weight, axis=1, keepdims=True)).astype(jnp.bfloat16)
    mixed = []
    for head in range(KEY_VALUE_HEADS):
        values = wide_rows[pl.ds(2 * head + 1, slots, stride=SLOT_PITCH), :].astype(jnp.bfloat16)
        mixed.append(
            jnp.dot(
                weight[head * HEAD_ROWS : (head + 1) * HEAD_ROWS], values, preferred_element_type=jnp.float32
            )
        )
    hidden = jnp.concatenate(mixed, axis=0) + residual[...].astype(jnp.float32)
    row_power = jnp.sum(hidden * hidden, axis=1, keepdims=True)
    step_of_row = lax.rem(lax.broadcasted_iota(jnp.int32, row_power.shape, 0), DECODE_STEPS)
    scale = jnp.zeros_like(row_power)
    for step in range(DECODE_STEPS):
        power = jnp.sum(jnp.where(step_of_row == step, row_power, 0.0), axis=0, keepdims=True)
        power = power / (QUERY_HEADS * HEAD_SIZE)
        scale = jnp.where(step_of_row == step, lax.rsqrt(power + 1e-05), scale)
    normed = (hidden * scale * gain_rows[...]).astype(jnp.bfloat16)
    half = normed.shape[0] // 2
    first = lax.axis_index("pair") == 0
    mine[...] = jnp.where(first, normed[:half], normed[half:])
    theirs[...] = jnp.where(first, normed[half:], normed[:half])


def branch_factor(scale, branch):
    guidance = scale[lax.axis_index("wide")]
    return jnp.where(branch == 0, guidance, 1.0 - guidance)


def own_part_kernel(scale, mine, out, factor):
    branch = lax.axis_index("pair")
    out[...] = branch_factor(scale, branch) * mine[...].astype(jnp.float32)
    factor[...] = jnp.full(factor.shape, branch_factor(scale, 1 - branch), jnp.float32)


def combine_kernel(factor, own_part, received, spread):
    other_part = factor[0:1, :] * received[...].astype(jnp.float32)
    guided = (own_part[...] + other_part).astype(jnp.bfloat16)
    spread[...] = jnp.broadcast_to(guided[None], spread.shape)


def project_kernel(rows, weight, other_weight, mine, theirs, wide_rows):
    pairs, per_pair, lanes = rows.shape
    half = pairs // 2
    pitch = per_pair + 1
    for pair in range(pairs):
        wide_rows[pl.ds(pair * pitch, per_pair), :] = rows[pair].astype(jnp.float32)

    def head_rows(head):
        steps = [
            wide_rows[pl.ds(head * DECODE_STEPS + step, pairs, stride=pitch), :] for step in range(DECODE_STEPS)
        ]
        return jnp.concatenate(steps, axis=0).astype(jnp.bfloat16)

    totals = [jnp.zeros((DECODE_STEPS * pairs, weight.shape[1]), jnp.float32)] * 2
    for two in range(per_pair // DECODE_STEPS // 2):
        left = jnp.concatenate([head_rows(2 * two), head_rows(2 * two + 1)], axis=1)
        totals = [
            total + jnp.dot(left, part[pl.ds(two * 2 * lanes, 2 * lanes), :], preferred_element_type=jnp.float32)
            for total, part in zip(totals, (weight, other_weight))
        ]
    total = jnp.concatenate(totals, axis=1)
    low, high = (
        jnp.concatenate(
            [total[step * pairs + part * half : step * pairs + (part + 1) * half] for step in range(DECODE_STEPS)],
            axis=0,
        )
        for part in range(2)
    )
    first = lax.axis_index("pair") == 0
    mine[...] = jnp.where(first, low, high)
    theirs[...] = jnp.where(first, high, low)


def to_lanes(column):
    size = column.shape[0]
    eye = lax.broadcasted_iota(jnp.int32, (size, size), 0) == lax.broadcasted_iota(jnp.int32, (size, size), 1)
    return jnp.sum(jnp.where(eye, column, jnp.zeros_like(column)), axis=0, keepdims=True)


def to_column(lanes):
    size = lanes.shape[1]
    eye = lax.broadcasted_iota(jnp.int32, (size, size), 0) == lax.broadcasted_iota(jnp.int32, (size, size), 1)
    return jnp.sum(jnp.where(eye, lanes, jnp.zeros_like(lanes)), axis=1, keepdims=True)


def allowed_entries(blocks, parity, width):
    count = blocks.shape[1] // 2
    flags = jnp.concatenate(
        [blocks[step, pl.ds(2 * pair + parity, 1), :] for step in range(DECODE_STEPS) for pair in range(count)], axis=0
    )
    block = lax.broadcasted_iota(jnp.int32, (flags.shape[0], width), 1) // BLK
    flag = jnp.zeros(block.shape, jnp.int32)
    for index in range(blocks.shape[2]):
        flag = jnp.where(block == index, flags[:, index : index + 1], flag)
    return flag > 0


def stats_kernel(mine, received, blocks, other_blocks, sampled, guided_out, other_out, stats):
    guided = mine[...] + received[...]
    rows, both = guided.shape
    width = both // 2
    guided_out[...] = guided[:, :width]
    other_out[...] = guided[:, width:]
    position = lax.axis_index("wide")
    parity = position % 2
    allowed = jnp.concatenate(
        [
            jnp.where(parity == 0, *(allowed_entries(part, q, width).astype(jnp.int32) for q in range(2)))
            for part in (blocks, other_blocks)
        ],
        axis=1,
    ) > 0
    top = jnp.max(jnp.where(allowed, guided, NEG_FILL), axis=1, keepdims=True)
    total = jnp.sum(jnp.where(allowed, jnp.exp(guided - top), 0.0), axis=1, keepdims=True)
    count = rows // DECODE_STEPS
    spot = (count, 2 * count)
    of_parity = lax.broadcasted_iota(jnp.int32, spot, 1) == 2 * lax.broadcasted_iota(jnp.int32, spot, 0) + parity
    chosen = jnp.concatenate(
        [
            jnp.sum(jnp.where(of_parity, sampled[pl.ds(step, 1), :], 0), axis=1, keepdims=True)
            for step in range(DECODE_STEPS)
        ],
        axis=0,
    )
    lane = lax.broadcasted_iota(jnp.int32, guided.shape, 1)
    column = jnp.where(lane < width, position * width + lane, (position ^ 1) * width + lane - width)
    picked = jnp.sum(jnp.where(column == chosen, guided, 0.0), axis=1, keepdims=True)
    stats[...] = jnp.broadcast_to(
        jnp.concatenate([to_lanes(top), to_lanes(total), to_lanes(picked)], axis=0)[None], stats.shape
    )


def finish_kernel(guided, received, stats, blocks, logprobs, tokens):
    rows, width = guided.shape
    count = rows // DECODE_STEPS
    chips = stats.shape[0] // 2
    near = lax.axis_index("wide") % 2
    token_rows = [jnp.zeros((1, 2 * count), jnp.float32)] * DECODE_STEPS
    results = []
    for parity in range(2):
        parts = [stats[2 * chip + parity] for chip in range(chips)]
        top = functools.reduce(jnp.maximum, [part[0:1] for part in parts])
        total = sum(part[1:2] * jnp.exp(part[0:1] - top) for part in parts)
        normalizer = top + jnp.log(total)
        token = sum(part[2:3] for part in parts) - normalizer
        values = jnp.where(near == parity, guided[...], received[...])
        results.append(jnp.where(allowed_entries(blocks, parity, width), values - to_column(normalizer), 0.0))
        spot = (count, 2 * count)
        here = lax.broadcasted_iota(jnp.int32, spot, 1) == 2 * lax.broadcasted_iota(jnp.int32, spot, 0) + parity
        for step in range(DECODE_STEPS):
            mine = slice(step * count, (step + 1) * count)
            spread = jnp.sum(jnp.where(here, to_column(token[:, mine]), 0.0), axis=0, keepdims=True)
            token_rows[step] = token_rows[step] + spread
    for step in range(DECODE_STEPS):
        tokens[pl.ds(step, 1), :] = token_rows[step]
        for pair in range(count):
            row = step * count + pair
            for parity, result in enumerate(results):
                logprobs[step, pl.ds(2 * pair + parity, 1), :] = result[row : row + 1]


def slot_rows(array):
    slots = array.shape[0]
    split = array.reshape(slots, 2, KEY_VALUE_HEADS, HEAD_SIZE)
    return split.transpose(0, 2, 1, 3).reshape(slots * SLOT_ROWS, HEAD_SIZE)


def step_rows(array):
    split = array.reshape(DECODE_STEPS, QUERY_HEADS, HEAD_SIZE)
    return split.transpose(1, 0, 2).reshape(QUERY_HEADS * DECODE_STEPS, HEAD_SIZE)


def shards(
    wide,
    queries,
    cache,
    fresh_key_value,
    lengths,
    residual,
    norm_gain,
    vocab_weight,
    guidance,
    allowed_blocks,
    sampled,
):
    steps, half_pairs, blocks_here = allowed_blocks.shape
    width = vocab_weight.shape[1]
    pairs = guidance.shape[0]
    rows = steps * QUERY_HEADS
    cache_rows = slot_rows(cache[0, 0])
    vmem, smem, hbm = in_vmem(), in_smem(), pl.BlockSpec(memory_space=pltpu.HBM)
    half_rows = jax.ShapeDtypeStruct((rows // 2, HEAD_SIZE), jnp.bfloat16)
    chips = wide // 2
    flat = jax.ShapeDtypeStruct((steps * chips // 2, width), jnp.float32)
    flat_two = jax.ShapeDtypeStruct((steps * chips // 2, 2 * width), jnp.float32)

    def other_core(array):
        return lax.ppermute(array, "wide", [(source, source ^ 1) for source in range(wide)])

    def swap(array):
        return lax.ppermute(array, "pair", [(0, 1), (1, 0)])

    mine, theirs = call(
        attend_kernel,
        (half_rows, half_rows),
        [smem] + [hbm] * 5,
        [
            pltpu.VMEM(cache_rows.shape, jnp.bfloat16),
            pltpu.VMEM((cache.shape[2] * SLOT_PITCH, HEAD_SIZE), jnp.float32),
            pltpu.VMEM((rows, HEAD_SIZE), jnp.float32),
            pltpu.VMEM((rows, HEAD_SIZE), jnp.bfloat16),
            pltpu.VMEM((steps * SLOT_ROWS, HEAD_SIZE), jnp.bfloat16),
            pltpu.VMEM((rows, HEAD_SIZE), jnp.bfloat16),
            pltpu.VMEM((QUERY_HEADS, HEAD_SIZE), jnp.float32),
            pltpu.SemaphoreType.DMA((cache.shape[2] // BLOCK + 4,)),
        ],
        limit=58 << 20,
    )(
        lengths,
        step_rows(queries[0, 0]),
        cache_rows,
        slot_rows(fresh_key_value[0, 0]),
        step_rows(residual[0, 0]),
        norm_gain.reshape(QUERY_HEADS, HEAD_SIZE),
    )
    received = swap(theirs)
    own_part, factor = call(
        own_part_kernel,
        (jax.ShapeDtypeStruct(half_rows.shape, jnp.float32), jax.ShapeDtypeStruct((8, HEAD_SIZE), jnp.float32)),
        [smem, vmem],
    )(guidance, mine)
    other_weight, other_blocks = other_core(vocab_weight), other_core(allowed_blocks)
    spread = call(combine_kernel, jax.ShapeDtypeStruct((chips,) + half_rows.shape, jnp.bfloat16), [vmem] * 3)(
        factor, own_part, received
    )
    same_core = [list(range(core, wide, 2)) for core in range(2)]
    gathered = lax.all_to_all(spread, "wide", 0, 0, axis_index_groups=same_core, tiled=True)
    mine, theirs = call(
        project_kernel,
        (flat_two, flat_two),
        [vmem] * 3,
        [pltpu.VMEM((chips * (rows // 2 + 1), HEAD_SIZE), jnp.float32)],
    )(gathered, vocab_weight, other_weight)
    guided, other_guided, stats = call(
        stats_kernel,
        (flat, flat, jax.ShapeDtypeStruct((wide, 3, steps * chips // 2), jnp.float32)),
        [vmem] * 5,
    )(mine, swap(theirs), allowed_blocks, other_blocks, sampled)
    other_guided = other_core(other_guided)
    logprobs, tokens = call(
        finish_kernel,
        (
            jax.ShapeDtypeStruct((steps, half_pairs, width), jnp.float32),
            jax.ShapeDtypeStruct((steps, half_pairs), jnp.float32),
        ),
        [vmem] * 4,
    )(guided, other_guided, lax.all_to_all(stats, "wide", 0, 0, tiled=True), allowed_blocks)
    return (logprobs, tokens)


def solution(mesh):
    placed = (
        P("pair", "wide", None, None),
        P("pair", "wide", None, None, None),
        P("pair", "wide", None, None, None),
        P("pair", "wide"),
        P("pair", "wide", None, None),
        P(),
        P("pair", "wide"),
        P(),
        P(None, "pair", "wide"),
        P(None, "pair"),
    )
    return jax.shard_map(
        functools.partial(shards, mesh.shape["wide"]),
        mesh=mesh,
        in_specs=placed,
        out_specs=(P(None, "pair", "wide"), P(None, "pair")),
        check_vma=False,
    )
```

```python
import functools
import math

import jax
import jax.numpy as jnp
from jax import lax
from jax.experimental import pallas as pl
from jax.experimental.pallas import tpu as pltpu
from jax.sharding import PartitionSpec as P

QUERY_HEADS = 64
KEY_VALUE_HEADS = 8
HEAD_SIZE = 128
BLK = 32
DECODE_STEPS = 2
SLOT_ROWS = 2 * KEY_VALUE_HEADS
SLOT_PITCH = SLOT_ROWS + 1
BLOCK = 64
HEAD_ROWS = DECODE_STEPS * (QUERY_HEADS // KEY_VALUE_HEADS)
NEG_FILL = -1e30


def in_vmem():
    return pl.BlockSpec(memory_space=pltpu.VMEM)


def in_smem():
    return pl.BlockSpec(memory_space=pltpu.SMEM)


def call(kernel, out_shape, in_specs, scratch=(), limit=16 << 20, cost=None):
    return pl.pallas_call(
        kernel,
        out_shape=out_shape,
        in_specs=in_specs,
        out_specs=jax.tree.map(lambda _: in_vmem(), out_shape),
        scratch_shapes=list(scratch),
        compiler_params=pltpu.CompilerParams(vmem_limit_bytes=limit),
        cost_estimate=cost,
    )


def attend_kernel(
    lengths, queries_in, cache, fresh_in, residual_in, gain_in, mine, theirs,
    stage, wide_rows, mixed, gain_rows, queries, fresh, residual, gain, arrived,
):
    rows = cache.shape[0]
    slots = rows // SLOT_ROWS

    def block_copy(block):
        at = pl.ds(pl.multiple_of(block * (BLOCK * SLOT_ROWS), BLOCK * SLOT_ROWS), BLOCK * SLOT_ROWS)
        return pltpu.make_async_copy(cache.at[at], stage.at[at], arrived.at[block])

    def start(block, carry):
        block_copy(block).start()
        return carry

    def clear(block, carry):
        target = pl.multiple_of(block * (BLOCK * SLOT_PITCH), 8)
        wide_rows[pl.ds(target, BLOCK * SLOT_PITCH), :] = jnp.zeros((BLOCK * SLOT_PITCH, HEAD_SIZE), jnp.float32)
        return carry

    def widen(block, carry):
        block_copy(block).wait()
        source = pl.multiple_of(block * (BLOCK * SLOT_ROWS), BLOCK * SLOT_ROWS)
        target = pl.multiple_of(block * (BLOCK * SLOT_PITCH), 8)
        for slot in range(BLOCK):
            wide_rows[pl.ds(target + slot * SLOT_PITCH, SLOT_ROWS), :] = stage[
                pl.ds(source + slot * SLOT_ROWS, SLOT_ROWS), :
            ].astype(jnp.float32)
        return carry

    blocks = slots // BLOCK
    live_blocks = lax.div(lengths[0, 0] + (BLOCK - 1), BLOCK)
    lax.fori_loop(0, live_blocks, start, 0)
    small = [
        pltpu.make_async_copy(source, target, arrived.at[blocks + index])
        for index, (source, target) in enumerate(
            ((gain_in, gain), (fresh_in, fresh), (queries_in, queries), (residual_in, residual))
        )
    ]
    for copy in small:
        copy.start()
    sizes = [slots // 4, slots // 2, slots]
    fits = [lengths[0, 0] <= size - DECODE_STEPS for size in sizes[:-1]]
    used_blocks = jnp.where(fits[0], sizes[0] // BLOCK, jnp.where(fits[1], sizes[1] // BLOCK, blocks))
    lax.fori_loop(live_blocks, used_blocks, clear, 0)
    lax.fori_loop(0, live_blocks, widen, 0)
    for copy in small:
        copy.wait()
    gain_rows[pl.ds(0, QUERY_HEADS, stride=2), :] = gain[...]
    gain_rows[pl.ds(1, QUERY_HEADS, stride=2), :] = gain[...]
    factor = 1.0 / math.sqrt(HEAD_SIZE)

    def attend(count):
        first_fresh = count - DECODE_STEPS
        for step in range(DECODE_STEPS):
            wide_rows[pl.ds((first_fresh + step) * SLOT_PITCH, SLOT_ROWS), :] = fresh[
                pl.ds(step * SLOT_ROWS, SLOT_ROWS), :
            ].astype(jnp.float32)
        scores = []
        for head in range(KEY_VALUE_HEADS):
            keys = wide_rows[pl.ds(2 * head, count, stride=SLOT_PITCH), :].astype(jnp.bfloat16)
            scores.append(
                lax.dot_general(
                    queries[pl.ds(head * HEAD_ROWS, HEAD_ROWS), :],
                    keys,
                    (((1,), (1,)), ((), ())),
                    preferred_element_type=jnp.float32,
                )
            )
        score = jnp.concatenate(scores, axis=0)
        slot = lax.broadcasted_iota(jnp.int32, score.shape, 1)
        step_of_row = lax.rem(lax.broadcasted_iota(jnp.int32, score.shape, 0), DECODE_STEPS)
        live = (slot < lengths[0, 0]) | ((slot >= first_fresh) & (slot - first_fresh <= step_of_row))
        score = jnp.where(live, score * factor, NEG_FILL)
        weight = jnp.exp(score - jnp.max(score, axis=1, keepdims=True))
        weight = (weight / jnp.sum(weight, axis=1, keepdims=True)).astype(jnp.bfloat16)
        for head in range(KEY_VALUE_HEADS):
            values = wide_rows[pl.ds(2 * head + 1, count, stride=SLOT_PITCH), :].astype(jnp.bfloat16)
            mixed[pl.ds(head * HEAD_ROWS, HEAD_ROWS), :] = jnp.dot(
                weight[head * HEAD_ROWS : (head + 1) * HEAD_ROWS], values, preferred_element_type=jnp.float32
            )

    pl.when(fits[0])(lambda: attend(sizes[0]))
    pl.when(jnp.logical_not(fits[0]) & fits[1])(lambda: attend(sizes[1]))
    pl.when(jnp.logical_not(fits[1]))(lambda: attend(sizes[2]))
    hidden = mixed[...] + residual[...].astype(jnp.float32)
    row_power = jnp.sum(hidden * hidden, axis=1, keepdims=True)
    step_of_row = lax.rem(lax.broadcasted_iota(jnp.int32, row_power.shape, 0), DECODE_STEPS)
    scale = jnp.zeros_like(row_power)
    for step in range(DECODE_STEPS):
        power = jnp.sum(jnp.where(step_of_row == step, row_power, 0.0), axis=0, keepdims=True)
        power = power / (QUERY_HEADS * HEAD_SIZE)
        scale = jnp.where(step_of_row == step, lax.rsqrt(power + 1e-05), scale)
    normed = (hidden * scale * gain_rows[...]).astype(jnp.bfloat16)
    half = normed.shape[0] // 2
    first = lax.axis_index("pair") == 0
    mine[...] = jnp.where(first, normed[:half], normed[half:])
    theirs[...] = jnp.where(first, normed[half:], normed[:half])


def branch_factor(scale, branch):
    guidance = scale[lax.axis_index("wide")]
    return jnp.where(branch == 0, guidance, 1.0 - guidance)


def own_part_kernel(scale, mine, out, factor):
    branch = lax.axis_index("pair")
    out[...] = branch_factor(scale, branch) * mine[...].astype(jnp.float32)
    factor[...] = jnp.full(factor.shape, branch_factor(scale, 1 - branch), jnp.float32)


def combine_kernel(factor, own_part, received, spread):
    other_part = factor[0:1, :] * received[...].astype(jnp.float32)
    guided = (own_part[...] + other_part).astype(jnp.bfloat16)
    spread[...] = jnp.broadcast_to(guided[None], spread.shape)


def project_kernel(rows, weight, other_weight, mine, theirs, wide_rows):
    pairs, per_pair, lanes = rows.shape
    half = pairs // 2
    pitch = per_pair + 1
    for pair in range(pairs):
        wide_rows[pl.ds(pair * pitch, per_pair), :] = rows[pair].astype(jnp.float32)

    def head_rows(head):
        steps = [
            wide_rows[pl.ds(head * DECODE_STEPS + step, pairs, stride=pitch), :] for step in range(DECODE_STEPS)
        ]
        return jnp.concatenate(steps, axis=0).astype(jnp.bfloat16)

    totals = [jnp.zeros((DECODE_STEPS * pairs, weight.shape[1]), jnp.float32)] * 2
    for two in range(per_pair // DECODE_STEPS // 2):
        left = jnp.concatenate([head_rows(2 * two), head_rows(2 * two + 1)], axis=1)
        totals = [
            total + jnp.dot(left, part[pl.ds(two * 2 * lanes, 2 * lanes), :], preferred_element_type=jnp.float32)
            for total, part in zip(totals, (weight, other_weight))
        ]
    total = jnp.concatenate(totals, axis=1)
    low, high = (
        jnp.concatenate(
            [total[step * pairs + part * half : step * pairs + (part + 1) * half] for step in range(DECODE_STEPS)],
            axis=0,
        )
        for part in range(2)
    )
    first = lax.axis_index("pair") == 0
    mine[...] = jnp.where(first, low, high)
    theirs[...] = jnp.where(first, high, low)


def to_lanes(column):
    size = column.shape[0]
    eye = lax.broadcasted_iota(jnp.int32, (size, size), 0) == lax.broadcasted_iota(jnp.int32, (size, size), 1)
    return jnp.sum(jnp.where(eye, column, jnp.zeros_like(column)), axis=0, keepdims=True)


def to_column(lanes):
    size = lanes.shape[1]
    eye = lax.broadcasted_iota(jnp.int32, (size, size), 0) == lax.broadcasted_iota(jnp.int32, (size, size), 1)
    return jnp.sum(jnp.where(eye, lanes, jnp.zeros_like(lanes)), axis=1, keepdims=True)


def allowed_entries(blocks, parity, width):
    count = blocks.shape[1] // 2
    flags = jnp.concatenate(
        [blocks[step, pl.ds(2 * pair + parity, 1), :] for step in range(DECODE_STEPS) for pair in range(count)], axis=0
    )
    block = lax.broadcasted_iota(jnp.int32, (flags.shape[0], width), 1) // BLK
    flag = jnp.zeros(block.shape, jnp.int32)
    for index in range(blocks.shape[2]):
        flag = jnp.where(block == index, flags[:, index : index + 1], flag)
    return flag > 0


def stats_kernel(mine, received, blocks, other_blocks, sampled, guided_out, other_out, stats):
    guided = mine[...] + received[...]
    rows, both = guided.shape
    width = both // 2
    guided_out[...] = guided[:, :width]
    other_out[...] = guided[:, width:]
    position = lax.axis_index("wide")
    parity = position % 2
    allowed = jnp.concatenate(
        [
            jnp.where(parity == 0, *(allowed_entries(part, q, width).astype(jnp.int32) for q in range(2)))
            for part in (blocks, other_blocks)
        ],
        axis=1,
    ) > 0
    top = jnp.max(jnp.where(allowed, guided, NEG_FILL), axis=1, keepdims=True)
    total = jnp.sum(jnp.where(allowed, jnp.exp(guided - top), 0.0), axis=1, keepdims=True)
    count = rows // DECODE_STEPS
    spot = (count, 2 * count)
    of_parity = lax.broadcasted_iota(jnp.int32, spot, 1) == 2 * lax.broadcasted_iota(jnp.int32, spot, 0) + parity
    chosen = jnp.concatenate(
        [
            jnp.sum(jnp.where(of_parity, sampled[pl.ds(step, 1), :], 0), axis=1, keepdims=True)
            for step in range(DECODE_STEPS)
        ],
        axis=0,
    )
    lane = lax.broadcasted_iota(jnp.int32, guided.shape, 1)
    column = jnp.where(lane < width, position * width + lane, (position ^ 1) * width + lane - width)
    picked = jnp.sum(jnp.where(column == chosen, guided, 0.0), axis=1, keepdims=True)
    stats[...] = jnp.broadcast_to(
        jnp.concatenate([to_lanes(top), to_lanes(total), to_lanes(picked)], axis=0)[None], stats.shape
    )


def finish_kernel(guided, received, stats, blocks, logprobs, tokens):
    rows, width = guided.shape
    count = rows // DECODE_STEPS
    chips = stats.shape[0] // 2
    near = lax.axis_index("wide") % 2
    token_rows = [jnp.zeros((1, 2 * count), jnp.float32)] * DECODE_STEPS
    results = []
    for parity in range(2):
        parts = [stats[2 * chip + parity] for chip in range(chips)]
        top = functools.reduce(jnp.maximum, [part[0:1] for part in parts])
        total = sum(part[1:2] * jnp.exp(part[0:1] - top) for part in parts)
        normalizer = top + jnp.log(total)
        token = sum(part[2:3] for part in parts) - normalizer
        values = jnp.where(near == parity, guided[...], received[...])
        results.append(jnp.where(allowed_entries(blocks, parity, width), values - to_column(normalizer), 0.0))
        spot = (count, 2 * count)
        here = lax.broadcasted_iota(jnp.int32, spot, 1) == 2 * lax.broadcasted_iota(jnp.int32, spot, 0) + parity
        for step in range(DECODE_STEPS):
            mine = slice(step * count, (step + 1) * count)
            spread = jnp.sum(jnp.where(here, to_column(token[:, mine]), 0.0), axis=0, keepdims=True)
            token_rows[step] = token_rows[step] + spread
    for step in range(DECODE_STEPS):
        tokens[pl.ds(step, 1), :] = token_rows[step]
        for pair in range(count):
            row = step * count + pair
            for parity, result in enumerate(results):
                logprobs[step, pl.ds(2 * pair + parity, 1), :] = result[row : row + 1]


def slot_rows(array):
    slots = array.shape[0]
    split = array.reshape(slots, 2, KEY_VALUE_HEADS, HEAD_SIZE)
    return split.transpose(0, 2, 1, 3).reshape(slots * SLOT_ROWS, HEAD_SIZE)


def step_rows(array):
    split = array.reshape(DECODE_STEPS, QUERY_HEADS, HEAD_SIZE)
    return split.transpose(1, 0, 2).reshape(QUERY_HEADS * DECODE_STEPS, HEAD_SIZE)


def shards(
    wide,
    queries,
    cache,
    fresh_key_value,
    lengths,
    residual,
    norm_gain,
    vocab_weight,
    guidance,
    allowed_blocks,
    sampled,
):
    steps, half_pairs, blocks_here = allowed_blocks.shape
    width = vocab_weight.shape[1]
    pairs = guidance.shape[0]
    rows = steps * QUERY_HEADS
    cache_rows = slot_rows(cache[0, 0])
    vmem, smem, hbm = in_vmem(), in_smem(), pl.BlockSpec(memory_space=pltpu.HBM)
    half_rows = jax.ShapeDtypeStruct((rows // 2, HEAD_SIZE), jnp.bfloat16)
    chips = wide // 2
    flat = jax.ShapeDtypeStruct((steps * chips // 2, width), jnp.float32)
    flat_two = jax.ShapeDtypeStruct((steps * chips // 2, 2 * width), jnp.float32)

    def other_core(array):
        return lax.ppermute(array, "wide", [(source, source ^ 1) for source in range(wide)])

    def swap(array):
        return lax.ppermute(array, "pair", [(0, 1), (1, 0)])

    mine, theirs = call(
        attend_kernel,
        (half_rows, half_rows),
        [smem] + [hbm] * 5,
        [
            pltpu.VMEM(cache_rows.shape, jnp.bfloat16),
            pltpu.VMEM((cache.shape[2] * SLOT_PITCH, HEAD_SIZE), jnp.float32),
            pltpu.VMEM((rows, HEAD_SIZE), jnp.float32),
            pltpu.VMEM((rows, HEAD_SIZE), jnp.float32),
            pltpu.VMEM((rows, HEAD_SIZE), jnp.bfloat16),
            pltpu.VMEM((steps * SLOT_ROWS, HEAD_SIZE), jnp.bfloat16),
            pltpu.VMEM((rows, HEAD_SIZE), jnp.bfloat16),
            pltpu.VMEM((QUERY_HEADS, HEAD_SIZE), jnp.float32),
            pltpu.SemaphoreType.DMA((cache.shape[2] // BLOCK + 4,)),
        ],
        limit=58 << 20,
    )(
        lengths,
        step_rows(queries[0, 0]),
        cache_rows,
        slot_rows(fresh_key_value[0, 0]),
        step_rows(residual[0, 0]),
        norm_gain.reshape(QUERY_HEADS, HEAD_SIZE),
    )
    received = swap(theirs)
    own_part, factor = call(
        own_part_kernel,
        (jax.ShapeDtypeStruct(half_rows.shape, jnp.float32), jax.ShapeDtypeStruct((8, HEAD_SIZE), jnp.float32)),
        [smem, vmem],
    )(guidance, mine)
    other_weight, other_blocks = other_core(vocab_weight), other_core(allowed_blocks)
    spread = call(combine_kernel, jax.ShapeDtypeStruct((chips,) + half_rows.shape, jnp.bfloat16), [vmem] * 3)(
        factor, own_part, received
    )
    same_core = [list(range(core, wide, 2)) for core in range(2)]
    gathered = lax.all_to_all(spread, "wide", 0, 0, axis_index_groups=same_core, tiled=True)
    mine, theirs = call(
        project_kernel,
        (flat_two, flat_two),
        [vmem] * 3,
        [pltpu.VMEM((chips * (rows // 2 + 1), HEAD_SIZE), jnp.float32)],
    )(gathered, vocab_weight, other_weight)
    guided, other_guided, stats = call(
        stats_kernel,
        (flat, flat, jax.ShapeDtypeStruct((wide, 3, steps * chips // 2), jnp.float32)),
        [vmem] * 5,
    )(mine, swap(theirs), allowed_blocks, other_blocks, sampled)
    other_guided = other_core(other_guided)
    logprobs, tokens = call(
        finish_kernel,
        (
            jax.ShapeDtypeStruct((steps, half_pairs, width), jnp.float32),
            jax.ShapeDtypeStruct((steps, half_pairs), jnp.float32),
        ),
        [vmem] * 4,
    )(guided, other_guided, lax.all_to_all(stats, "wide", 0, 0, tiled=True), allowed_blocks)
    return (logprobs, tokens)


def solution(mesh):
    placed = (
        P("pair", "wide", None, None),
        P("pair", "wide", None, None, None),
        P("pair", "wide", None, None, None),
        P("pair", "wide"),
        P("pair", "wide", None, None),
        P(),
        P("pair", "wide"),
        P(),
        P(None, "pair", "wide"),
        P(None, "pair"),
    )
    return jax.shard_map(
        functools.partial(shards, mesh.shape["wide"]),
        mesh=mesh,
        in_specs=placed,
        out_specs=(P(None, "pair", "wide"), P(None, "pair")),
        check_vma=False,
    )
```

```python
import functools
import math

import jax
import jax.numpy as jnp
from jax import lax
from jax.experimental import pallas as pl
from jax.experimental.pallas import tpu as pltpu
from jax.sharding import PartitionSpec as P

QUERY_HEADS = 64
KEY_VALUE_HEADS = 8
HEAD_SIZE = 128
BLK = 32
DECODE_STEPS = 2
SLOT_ROWS = 2 * KEY_VALUE_HEADS
SLOT_PITCH = SLOT_ROWS + 1
BLOCK = 64
HEAD_ROWS = DECODE_STEPS * (QUERY_HEADS // KEY_VALUE_HEADS)
NEG_FILL = -1e30


def in_vmem():
    return pl.BlockSpec(memory_space=pltpu.VMEM)


def in_smem():
    return pl.BlockSpec(memory_space=pltpu.SMEM)


def call(kernel, out_shape, in_specs, scratch=(), limit=16 << 20, cost=None):
    return pl.pallas_call(
        kernel,
        out_shape=out_shape,
        in_specs=in_specs,
        out_specs=jax.tree.map(lambda _: in_vmem(), out_shape, is_leaf=lambda x: hasattr(x, 'shape')),
        scratch_shapes=list(scratch),
        compiler_params=pltpu.CompilerParams(vmem_limit_bytes=limit),
        cost_estimate=cost,
    )


def attend_kernel(
    lengths, queries_in, cache, fresh_in, residual_in, gain_in, mine, theirs,
    stage, wide_rows, gain_rows, queries, fresh, residual, gain, arrived,
):
    rows = cache.shape[0]
    slots = rows // SLOT_ROWS

    def block_copy(block):
        at = pl.ds(pl.multiple_of(block * (BLOCK * SLOT_ROWS), BLOCK * SLOT_ROWS), BLOCK * SLOT_ROWS)
        return pltpu.make_async_copy(cache.at[at], stage.at[at], arrived.at[block])

    def start(block, carry):
        block_copy(block).start()
        return carry

    def clear(block, carry):
        target = pl.multiple_of(block * (BLOCK * SLOT_PITCH), 8)
        wide_rows[pl.ds(target, BLOCK * SLOT_PITCH), :] = jnp.zeros((BLOCK * SLOT_PITCH, HEAD_SIZE), jnp.float32)
        return carry

    def widen(block, carry):
        block_copy(block).wait()
        source = pl.multiple_of(block * (BLOCK * SLOT_ROWS), BLOCK * SLOT_ROWS)
        target = pl.multiple_of(block * (BLOCK * SLOT_PITCH), 8)
        for slot in range(BLOCK):
            wide_rows[pl.ds(target + slot * SLOT_PITCH, SLOT_ROWS), :] = stage[
                pl.ds(source + slot * SLOT_ROWS, SLOT_ROWS), :
            ].astype(jnp.float32)
        return carry

    blocks = slots // BLOCK
    live_blocks = lax.div(lengths[0, 0] + (BLOCK - 1), BLOCK)
    lax.fori_loop(0, live_blocks, start, 0)
    small = [
        pltpu.make_async_copy(source, target, arrived.at[blocks + index])
        for index, (source, target) in enumerate(
            ((gain_in, gain), (fresh_in, fresh), (queries_in, queries), (residual_in, residual))
        )
    ]
    for copy in small:
        copy.start()
    lax.fori_loop(live_blocks, blocks, clear, 0)
    lax.fori_loop(0, live_blocks, widen, 0)
    for copy in small:
        copy.wait()
    gain_rows[pl.ds(0, QUERY_HEADS, stride=2), :] = gain[...]
    gain_rows[pl.ds(1, QUERY_HEADS, stride=2), :] = gain[...]
    for step in range(DECODE_STEPS):
        wide_rows[pl.ds((slots - DECODE_STEPS + step) * SLOT_PITCH, SLOT_ROWS), :] = fresh[
            pl.ds(step * SLOT_ROWS, SLOT_ROWS), :
        ].astype(jnp.float32)
    factor = 1.0 / math.sqrt(HEAD_SIZE)
    scores = []
    for head in range(KEY_VALUE_HEADS):
        keys = wide_rows[pl.ds(2 * head, slots, stride=SLOT_PITCH), :].astype(jnp.bfloat16)
        scores.append(
            lax.dot_general(
                queries[pl.ds(head * HEAD_ROWS, HEAD_ROWS), :],
                keys,
                (((1,), (1,)), ((), ())),
                preferred_element_type=jnp.float32,
            )
        )
    score = jnp.concatenate(scores, axis=0)
    slot = lax.broadcasted_iota(jnp.int32, score.shape, 1)
    step_of_row = lax.rem(lax.broadcasted_iota(jnp.int32, score.shape, 0), DECODE_STEPS)
    first_fresh = slots - DECODE_STEPS
    live = (slot < lengths[0, 0]) | ((slot >= first_fresh) & (slot - first_fresh <= step_of_row))
    score = jnp.where(live, score * factor, NEG_FILL)
    weight = jnp.exp(score - jnp.max(score, axis=1, keepdims=True))
    weight = (weight / jnp.sum(weight, axis=1, keepdims=True)).astype(jnp.bfloat16)
    mixed = []
    for head in range(KEY_VALUE_HEADS):
        values = wide_rows[pl.ds(2 * head + 1, slots, stride=SLOT_PITCH), :].astype(jnp.bfloat16)
        mixed.append(
            jnp.dot(
                weight[head * HEAD_ROWS : (head + 1) * HEAD_ROWS], values, preferred_element_type=jnp.float32
            )
        )
    hidden = jnp.concatenate(mixed, axis=0) + residual[...].astype(jnp.float32)
    row_power = jnp.sum(hidden * hidden, axis=1, keepdims=True)
    step_of_row = lax.rem(lax.broadcasted_iota(jnp.int32, row_power.shape, 0), DECODE_STEPS)
    scale = jnp.zeros_like(row_power)
    for step in range(DECODE_STEPS):
        power = jnp.sum(jnp.where(step_of_row == step, row_power, 0.0), axis=0, keepdims=True)
        power = power / (QUERY_HEADS * HEAD_SIZE)
        scale = jnp.where(step_of_row == step, lax.rsqrt(power + 1e-05), scale)
    normed = (hidden * scale * gain_rows[...]).astype(jnp.bfloat16)
    half = normed.shape[0] // 2
    first = lax.axis_index("pair") == 0
    mine[...] = jnp.where(first, normed[:half], normed[half:])
    theirs[...] = jnp.where(first, normed[half:], normed[:half])


def branch_factor(scale, branch):
    guidance = scale[lax.axis_index("wide")]
    return jnp.where(branch == 0, guidance, 1.0 - guidance)


def own_part_kernel(scale, mine, out, factor):
    branch = lax.axis_index("pair")
    out[...] = branch_factor(scale, branch) * mine[...].astype(jnp.float32)
    factor[...] = jnp.full(factor.shape, branch_factor(scale, 1 - branch), jnp.float32)


def combine_kernel(factor, own_part, received, spread):
    other_part = factor[0:1, :] * received[...].astype(jnp.float32)
    guided = (own_part[...] + other_part).astype(jnp.bfloat16)
    spread[...] = jnp.broadcast_to(guided[None], spread.shape)


def project_kernel(rows, weight, other_weight, mine, theirs, wide_rows):
    pairs, per_pair, lanes = rows.shape
    half = pairs // 2
    pitch = per_pair + 1
    for pair in range(pairs):
        wide_rows[pl.ds(pair * pitch, per_pair), :] = rows[pair].astype(jnp.float32)

    def head_rows(head):
        steps = [
            wide_rows[pl.ds(head * DECODE_STEPS + step, pairs, stride=pitch), :] for step in range(DECODE_STEPS)
        ]
        return jnp.concatenate(steps, axis=0).astype(jnp.bfloat16)

    totals = [jnp.zeros((DECODE_STEPS * pairs, weight.shape[1]), jnp.float32)] * 2
    for two in range(per_pair // DECODE_STEPS // 2):
        left = jnp.concatenate([head_rows(2 * two), head_rows(2 * two + 1)], axis=1)
        totals = [
            total + jnp.dot(left, part[pl.ds(two * 2 * lanes, 2 * lanes), :], preferred_element_type=jnp.float32)
            for total, part in zip(totals, (weight, other_weight))
        ]
    total = jnp.concatenate(totals, axis=1)
    low, high = (
        jnp.concatenate(
            [total[step * pairs + part * half : step * pairs + (part + 1) * half] for step in range(DECODE_STEPS)],
            axis=0,
        )
        for part in range(2)
    )
    first = lax.axis_index("pair") == 0
    mine[...] = jnp.where(first, low, high)
    theirs[...] = jnp.where(first, high, low)


def to_lanes(column):
    size = column.shape[0]
    eye = lax.broadcasted_iota(jnp.int32, (size, size), 0) == lax.broadcasted_iota(jnp.int32, (size, size), 1)
    return jnp.sum(jnp.where(eye, column, jnp.zeros_like(column)), axis=0, keepdims=True)


def to_column(lanes):
    size = lanes.shape[1]
    eye = lax.broadcasted_iota(jnp.int32, (size, size), 0) == lax.broadcasted_iota(jnp.int32, (size, size), 1)
    return jnp.sum(jnp.where(eye, lanes, jnp.zeros_like(lanes)), axis=1, keepdims=True)


def allowed_entries(blocks, parity, width):
    count = blocks.shape[1] // 2
    flags = jnp.concatenate(
        [blocks[step, pl.ds(2 * pair + parity, 1), :] for step in range(DECODE_STEPS) for pair in range(count)], axis=0
    )
    block = lax.broadcasted_iota(jnp.int32, (flags.shape[0], width), 1) // BLK
    flag = jnp.zeros(block.shape, jnp.int32)
    for index in range(blocks.shape[2]):
        flag = jnp.where(block == index, flags[:, index : index + 1], flag)
    return flag > 0


def stats_kernel(mine, received, blocks, other_blocks, sampled, guided_out, other_out, stats):
    guided = mine[...] + received[...]
    rows, both = guided.shape
    width = both // 2
    guided_out[...] = guided[:, :width]
    other_out[...] = guided[:, width:]
    position = lax.axis_index("wide")
    parity = position % 2
    allowed = jnp.concatenate(
        [
            jnp.where(parity == 0, *(allowed_entries(part, q, width).astype(jnp.int32) for q in range(2)))
            for part in (blocks, other_blocks)
        ],
        axis=1,
    ) > 0
    top = jnp.max(jnp.where(allowed, guided, NEG_FILL), axis=1, keepdims=True)
    total = jnp.sum(jnp.where(allowed, jnp.exp(guided - top), 0.0), axis=1, keepdims=True)
    count = rows // DECODE_STEPS
    spot = (count, 2 * count)
    of_parity = lax.broadcasted_iota(jnp.int32, spot, 1) == 2 * lax.broadcasted_iota(jnp.int32, spot, 0) + parity
    chosen = jnp.concatenate(
        [
            jnp.sum(jnp.where(of_parity, sampled[pl.ds(step, 1), :], 0), axis=1, keepdims=True)
            for step in range(DECODE_STEPS)
        ],
        axis=0,
    )
    lane = lax.broadcasted_iota(jnp.int32, guided.shape, 1)
    column = jnp.where(lane < width, position * width + lane, (position ^ 1) * width + lane - width)
    picked = jnp.sum(jnp.where(column == chosen, guided, 0.0), axis=1, keepdims=True)
    stats[...] = jnp.broadcast_to(
        jnp.concatenate([to_lanes(top), to_lanes(total), to_lanes(picked)], axis=0)[None], stats.shape
    )


def finish_kernel(guided, received, stats, blocks, logprobs, tokens):
    rows, width = guided.shape
    count = rows // DECODE_STEPS
    chips = stats.shape[0] // 2
    near = lax.axis_index("wide") % 2
    token_rows = [jnp.zeros((1, 2 * count), jnp.float32)] * DECODE_STEPS
    results = []
    for parity in range(2):
        parts = [stats[2 * chip + parity] for chip in range(chips)]
        top = functools.reduce(jnp.maximum, [part[0:1] for part in parts])
        total = sum(part[1:2] * jnp.exp(part[0:1] - top) for part in parts)
        normalizer = top + jnp.log(total)
        token = sum(part[2:3] for part in parts) - normalizer
        values = jnp.where(near == parity, guided[...], received[...])
        results.append(jnp.where(allowed_entries(blocks, parity, width), values - to_column(normalizer), 0.0))
        spot = (count, 2 * count)
        here = lax.broadcasted_iota(jnp.int32, spot, 1) == 2 * lax.broadcasted_iota(jnp.int32, spot, 0) + parity
        for step in range(DECODE_STEPS):
            mine = slice(step * count, (step + 1) * count)
            spread = jnp.sum(jnp.where(here, to_column(token[:, mine]), 0.0), axis=0, keepdims=True)
            token_rows[step] = token_rows[step] + spread
    for step in range(DECODE_STEPS):
        tokens[pl.ds(step, 1), :] = token_rows[step]
        for pair in range(count):
            row = step * count + pair
            for parity, result in enumerate(results):
                logprobs[step, pl.ds(2 * pair + parity, 1), :] = result[row : row + 1]


def slot_rows(array):
    slots = array.shape[0]
    split = array.reshape(slots, 2, KEY_VALUE_HEADS, HEAD_SIZE)
    return split.transpose(0, 2, 1, 3).reshape(slots * SLOT_ROWS, HEAD_SIZE)


def step_rows(array):
    split = array.reshape(DECODE_STEPS, QUERY_HEADS, HEAD_SIZE)
    return split.transpose(1, 0, 2).reshape(QUERY_HEADS * DECODE_STEPS, HEAD_SIZE)


def shards(
    wide,
    queries,
    cache,
    fresh_key_value,
    lengths,
    residual,
    norm_gain,
    vocab_weight,
    guidance,
    allowed_blocks,
    sampled,
):
    steps, half_pairs, blocks_here = allowed_blocks.shape
    width = vocab_weight.shape[1]
    pairs = guidance.shape[0]
    rows = steps * QUERY_HEADS
    cache_rows = slot_rows(cache[0, 0])
    vmem, smem, hbm = in_vmem(), in_smem(), pl.BlockSpec(memory_space=pltpu.HBM)
    half_rows = jax.ShapeDtypeStruct((rows // 2, HEAD_SIZE), jnp.bfloat16)
    chips = wide // 2
    flat = jax.ShapeDtypeStruct((steps * chips // 2, width), jnp.float32)
    flat_two = jax.ShapeDtypeStruct((steps * chips // 2, 2 * width), jnp.float32)

    def other_core(array):
        return lax.ppermute(array, "wide", [(source, source ^ 1) for source in range(wide)])

    def swap(array):
        return lax.ppermute(array, "pair", [(0, 1), (1, 0)])

    mine, theirs = call(
        attend_kernel,
        (pltpu.VMEM(half_rows.shape, half_rows.dtype), pltpu.VMEM(half_rows.shape, half_rows.dtype)),
        [smem] + [hbm] * 5,
        [
            pltpu.VMEM(cache_rows.shape, jnp.bfloat16),
            pltpu.VMEM((cache.shape[2] * SLOT_PITCH, HEAD_SIZE), jnp.float32),
            pltpu.VMEM((rows, HEAD_SIZE), jnp.float32),
            pltpu.VMEM((rows, HEAD_SIZE), jnp.bfloat16),
            pltpu.VMEM((steps * SLOT_ROWS, HEAD_SIZE), jnp.bfloat16),
            pltpu.VMEM((rows, HEAD_SIZE), jnp.bfloat16),
            pltpu.VMEM((QUERY_HEADS, HEAD_SIZE), jnp.float32),
            pltpu.SemaphoreType.DMA((cache.shape[2] // BLOCK + 4,)),
        ],
        limit=58 << 20,
    )(
        lengths,
        step_rows(queries[0, 0]),
        cache_rows,
        slot_rows(fresh_key_value[0, 0]),
        step_rows(residual[0, 0]),
        norm_gain.reshape(QUERY_HEADS, HEAD_SIZE),
    )
    received = swap(theirs)
    own_part, factor = call(
        own_part_kernel,
        (jax.ShapeDtypeStruct(half_rows.shape, jnp.float32), jax.ShapeDtypeStruct((8, HEAD_SIZE), jnp.float32)),
        [smem, vmem],
    )(guidance, mine)
    other_weight, other_blocks = other_core(vocab_weight), other_core(allowed_blocks)
    spread = call(combine_kernel, jax.ShapeDtypeStruct((chips,) + half_rows.shape, jnp.bfloat16), [vmem] * 3)(
        factor, own_part, received
    )
    same_core = [list(range(core, wide, 2)) for core in range(2)]
    gathered = lax.all_to_all(spread, "wide", 0, 0, axis_index_groups=same_core, tiled=True)
    mine, theirs = call(
        project_kernel,
        (flat_two, flat_two),
        [vmem] * 3,
        [pltpu.VMEM((chips * (rows // 2 + 1), HEAD_SIZE), jnp.float32)],
    )(gathered, vocab_weight, other_weight)
    guided, other_guided, stats = call(
        stats_kernel,
        (flat, flat, jax.ShapeDtypeStruct((wide, 3, steps * chips // 2), jnp.float32)),
        [vmem] * 5,
    )(mine, swap(theirs), allowed_blocks, other_blocks, sampled)
    other_guided = other_core(other_guided)
    logprobs, tokens = call(
        finish_kernel,
        (
            jax.ShapeDtypeStruct((steps, half_pairs, width), jnp.float32),
            jax.ShapeDtypeStruct((steps, half_pairs), jnp.float32),
        ),
        [vmem] * 4,
    )(guided, other_guided, lax.all_to_all(stats, "wide", 0, 0, tiled=True), allowed_blocks)
    return (logprobs, tokens)


def solution(mesh):
    placed = (
        P("pair", "wide", None, None),
        P("pair", "wide", None, None, None),
        P("pair", "wide", None, None, None),
        P("pair", "wide"),
        P("pair", "wide", None, None),
        P(),
        P("pair", "wide"),
        P(),
        P(None, "pair", "wide"),
        P(None, "pair"),
    )
    return jax.shard_map(
        functools.partial(shards, mesh.shape["wide"]),
        mesh=mesh,
        in_specs=placed,
        out_specs=(P(None, "pair", "wide"), P(None, "pair")),
        check_vma=False,
    )
```

```python
import functools
import math

import jax
import jax.numpy as jnp
from jax import lax
from jax.experimental import pallas as pl
from jax.experimental.pallas import tpu as pltpu
from jax.sharding import PartitionSpec as P

QUERY_HEADS = 64
KEY_VALUE_HEADS = 8
HEAD_SIZE = 128
BLK = 32
DECODE_STEPS = 2
SLOT_ROWS = 2 * KEY_VALUE_HEADS
SLOT_PITCH = SLOT_ROWS + 1
BLOCK = 64
HEAD_ROWS = DECODE_STEPS * (QUERY_HEADS // KEY_VALUE_HEADS)
NEG_FILL = -1e30


def in_vmem():
    return pl.BlockSpec(memory_space=pltpu.VMEM)


def in_smem():
    return pl.BlockSpec(memory_space=pltpu.SMEM)


def call(kernel, out_shape, in_specs, scratch=(), limit=16 << 20, cost=None):
    return pl.pallas_call(
        kernel,
        out_shape=out_shape,
        in_specs=in_specs,
        out_specs=jax.tree.map(lambda _: in_vmem(), out_shape, is_leaf=lambda x: hasattr(x, 'shape')),
        scratch_shapes=list(scratch),
        compiler_params=pltpu.CompilerParams(vmem_limit_bytes=limit),
        cost_estimate=cost,
    )


def attend_kernel(
    lengths, queries_in, cache, fresh_in, residual_in, gain_in, mine, theirs,
    stage, wide_rows, mixed, gain_rows, queries, fresh, residual, gain, arrived,
):
    rows = cache.shape[0]
    slots = rows // SLOT_ROWS

    def block_copy(block):
        at = pl.ds(pl.multiple_of(block * (BLOCK * SLOT_ROWS), BLOCK * SLOT_ROWS), BLOCK * SLOT_ROWS)
        return pltpu.make_async_copy(cache.at[at], stage.at[at], arrived.at[block])

    def start(block, carry):
        block_copy(block).start()
        return carry

    def clear(block, carry):
        target = pl.multiple_of(block * (BLOCK * SLOT_PITCH), 8)
        wide_rows[pl.ds(target, BLOCK * SLOT_PITCH), :] = jnp.zeros((BLOCK * SLOT_PITCH, HEAD_SIZE), jnp.float32)
        return carry

    def widen(block, carry):
        block_copy(block).wait()
        source = pl.multiple_of(block * (BLOCK * SLOT_ROWS), BLOCK * SLOT_ROWS)
        target = pl.multiple_of(block * (BLOCK * SLOT_PITCH), 8)
        for slot in range(BLOCK):
            wide_rows[pl.ds(target + slot * SLOT_PITCH, SLOT_ROWS), :] = stage[
                pl.ds(source + slot * SLOT_ROWS, SLOT_ROWS), :
            ].astype(jnp.float32)
        return carry

    blocks = slots // BLOCK
    live_blocks = lax.div(lengths[0, 0] + (BLOCK - 1), BLOCK)
    lax.fori_loop(0, live_blocks, start, 0)
    small = [
        pltpu.make_async_copy(source, target, arrived.at[blocks + index])
        for index, (source, target) in enumerate(
            ((gain_in, gain), (fresh_in, fresh), (queries_in, queries), (residual_in, residual))
        )
    ]
    for copy in small:
        copy.start()
    sizes = [slots // 4, slots // 2, slots]
    fits = [lengths[0, 0] <= size - DECODE_STEPS for size in sizes[:-1]]
    used_blocks = jnp.where(fits[0], sizes[0] // BLOCK, jnp.where(fits[1], sizes[1] // BLOCK, blocks))
    lax.fori_loop(live_blocks, used_blocks, clear, 0)
    lax.fori_loop(0, live_blocks, widen, 0)
    for copy in small:
        copy.wait()
    gain_rows[pl.ds(0, QUERY_HEADS, stride=2), :] = gain[...]
    gain_rows[pl.ds(1, QUERY_HEADS, stride=2), :] = gain[...]
    factor = 1.0 / math.sqrt(HEAD_SIZE)

    def attend(count):
        first_fresh = count - DECODE_STEPS
        for step in range(DECODE_STEPS):
            wide_rows[pl.ds((first_fresh + step) * SLOT_PITCH, SLOT_ROWS), :] = fresh[
                pl.ds(step * SLOT_ROWS, SLOT_ROWS), :
            ].astype(jnp.float32)
        scores = []
        for head in range(KEY_VALUE_HEADS):
            keys = wide_rows[pl.ds(2 * head, count, stride=SLOT_PITCH), :].astype(jnp.bfloat16)
            scores.append(
                lax.dot_general(
                    queries[pl.ds(head * HEAD_ROWS, HEAD_ROWS), :],
                    keys,
                    (((1,), (1,)), ((), ())),
                    preferred_element_type=jnp.float32,
                )
            )
        score = jnp.concatenate(scores, axis=0)
        slot = lax.broadcasted_iota(jnp.int32, score.shape, 1)
        step_of_row = lax.rem(lax.broadcasted_iota(jnp.int32, score.shape, 0), DECODE_STEPS)
        live = (slot < lengths[0, 0]) | ((slot >= first_fresh) & (slot - first_fresh <= step_of_row))
        score = jnp.where(live, score * factor, NEG_FILL)
        weight = jnp.exp(score - jnp.max(score, axis=1, keepdims=True))
        weight = (weight / jnp.sum(weight, axis=1, keepdims=True)).astype(jnp.bfloat16)
        for head in range(KEY_VALUE_HEADS):
            values = wide_rows[pl.ds(2 * head + 1, count, stride=SLOT_PITCH), :].astype(jnp.bfloat16)
            mixed[pl.ds(head * HEAD_ROWS, HEAD_ROWS), :] = jnp.dot(
                weight[head * HEAD_ROWS : (head + 1) * HEAD_ROWS], values, preferred_element_type=jnp.float32
            )

    pl.when(fits[0])(lambda: attend(sizes[0]))
    pl.when(jnp.logical_not(fits[0]) & fits[1])(lambda: attend(sizes[1]))
    pl.when(jnp.logical_not(fits[1]))(lambda: attend(sizes[2]))
    hidden = mixed[...] + residual[...].astype(jnp.float32)
    row_power = jnp.sum(hidden * hidden, axis=1, keepdims=True)
    step_of_row = lax.rem(lax.broadcasted_iota(jnp.int32, row_power.shape, 0), DECODE_STEPS)
    scale = jnp.zeros_like(row_power)
    for step in range(DECODE_STEPS):
        power = jnp.sum(jnp.where(step_of_row == step, row_power, 0.0), axis=0, keepdims=True)
        power = power / (QUERY_HEADS * HEAD_SIZE)
        scale = jnp.where(step_of_row == step, lax.rsqrt(power + 1e-05), scale)
    normed = (hidden * scale * gain_rows[...]).astype(jnp.bfloat16)
    half = normed.shape[0] // 2
    first = lax.axis_index("pair") == 0
    mine[...] = jnp.where(first, normed[:half], normed[half:])
    theirs[...] = jnp.where(first, normed[half:], normed[:half])


def branch_factor(scale, branch):
    guidance = scale[lax.axis_index("wide")]
    return jnp.where(branch == 0, guidance, 1.0 - guidance)


def own_part_kernel(scale, mine, out, factor):
    branch = lax.axis_index("pair")
    out[...] = branch_factor(scale, branch) * mine[...].astype(jnp.float32)
    factor[...] = jnp.full(factor.shape, branch_factor(scale, 1 - branch), jnp.float32)


def combine_kernel(factor, own_part, received, spread):
    other_part = factor[0:1, :] * received[...].astype(jnp.float32)
    guided = (own_part[...] + other_part).astype(jnp.bfloat16)
    spread[...] = jnp.broadcast_to(guided[None], spread.shape)


def project_kernel(rows, weight, other_weight, mine, theirs, wide_rows):
    pairs, per_pair, lanes = rows.shape
    half = pairs // 2
    pitch = per_pair + 1
    for pair in range(pairs):
        wide_rows[pl.ds(pair * pitch, per_pair), :] = rows[pair].astype(jnp.float32)

    def head_rows(head):
        steps = [
            wide_rows[pl.ds(head * DECODE_STEPS + step, pairs, stride=pitch), :] for step in range(DECODE_STEPS)
        ]
        return jnp.concatenate(steps, axis=0).astype(jnp.bfloat16)

    totals = [jnp.zeros((DECODE_STEPS * pairs, weight.shape[1]), jnp.float32)] * 2
    for two in range(per_pair // DECODE_STEPS // 2):
        left = jnp.concatenate([head_rows(2 * two), head_rows(2 * two + 1)], axis=1)
        totals = [
            total + jnp.dot(left, part[pl.ds(two * 2 * lanes, 2 * lanes), :], preferred_element_type=jnp.float32)
            for total, part in zip(totals, (weight, other_weight))
        ]
    total = jnp.concatenate(totals, axis=1)
    low, high = (
        jnp.concatenate(
            [total[step * pairs + part * half : step * pairs + (part + 1) * half] for step in range(DECODE_STEPS)],
            axis=0,
        )
        for part in range(2)
    )
    first = lax.axis_index("pair") == 0
    mine[...] = jnp.where(first, low, high)
    theirs[...] = jnp.where(first, high, low)


def to_lanes(column):
    size = column.shape[0]
    eye = lax.broadcasted_iota(jnp.int32, (size, size), 0) == lax.broadcasted_iota(jnp.int32, (size, size), 1)
    return jnp.sum(jnp.where(eye, column, jnp.zeros_like(column)), axis=0, keepdims=True)


def to_column(lanes):
    size = lanes.shape[1]
    eye = lax.broadcasted_iota(jnp.int32, (size, size), 0) == lax.broadcasted_iota(jnp.int32, (size, size), 1)
    return jnp.sum(jnp.where(eye, lanes, jnp.zeros_like(lanes)), axis=1, keepdims=True)


def allowed_entries(blocks, parity, width):
    count = blocks.shape[1] // 2
    flags = jnp.concatenate(
        [blocks[step, pl.ds(2 * pair + parity, 1), :] for step in range(DECODE_STEPS) for pair in range(count)], axis=0
    )
    block = lax.broadcasted_iota(jnp.int32, (flags.shape[0], width), 1) // BLK
    flag = jnp.zeros(block.shape, jnp.int32)
    for index in range(blocks.shape[2]):
        flag = jnp.where(block == index, flags[:, index : index + 1], flag)
    return flag > 0


def stats_kernel(mine, received, blocks, other_blocks, sampled, guided_out, other_out, stats):
    guided = mine[...] + received[...]
    rows, both = guided.shape
    width = both // 2
    guided_out[...] = guided[:, :width]
    other_out[...] = guided[:, width:]
    position = lax.axis_index("wide")
    parity = position % 2
    allowed = jnp.concatenate(
        [
            jnp.where(parity == 0, *(allowed_entries(part, q, width).astype(jnp.int32) for q in range(2)))
            for part in (blocks, other_blocks)
        ],
        axis=1,
    ) > 0
    top = jnp.max(jnp.where(allowed, guided, NEG_FILL), axis=1, keepdims=True)
    total = jnp.sum(jnp.where(allowed, jnp.exp(guided - top), 0.0), axis=1, keepdims=True)
    count = rows // DECODE_STEPS
    spot = (count, 2 * count)
    of_parity = lax.broadcasted_iota(jnp.int32, spot, 1) == 2 * lax.broadcasted_iota(jnp.int32, spot, 0) + parity
    chosen = jnp.concatenate(
        [
            jnp.sum(jnp.where(of_parity, sampled[pl.ds(step, 1), :], 0), axis=1, keepdims=True)
            for step in range(DECODE_STEPS)
        ],
        axis=0,
    )
    lane = lax.broadcasted_iota(jnp.int32, guided.shape, 1)
    column = jnp.where(lane < width, position * width + lane, (position ^ 1) * width + lane - width)
    picked = jnp.sum(jnp.where(column == chosen, guided, 0.0), axis=1, keepdims=True)
    lanes = jnp.concatenate([to_lanes(top), to_lanes(total), to_lanes(picked)], axis=1)
    pad = stats.shape[2] - lanes.shape[1]
    if pad > 0:
        lanes = jnp.concatenate([lanes, jnp.zeros((1, pad), jnp.float32)], axis=1)
    stats[...] = jnp.broadcast_to(lanes[None], stats.shape)


def finish_kernel(guided, received, stats, blocks, logprobs, tokens):
    rows, width = guided.shape
    count = rows // DECODE_STEPS
    chips = stats.shape[0] // 2
    near = lax.axis_index("wide") % 2
    token_rows = [jnp.zeros((1, 2 * count), jnp.float32)] * DECODE_STEPS
    results = []
    for parity in range(2):
        parts = jnp.concatenate([stats[2 * chip + parity] for chip in range(chips)], axis=0)
        tops = parts[:, 0:rows]
        top = jnp.max(tops, axis=0, keepdims=True)
        total = jnp.sum(parts[:, rows : 2 * rows] * jnp.exp(tops - top), axis=0, keepdims=True)
        normalizer = top + jnp.log(total)
        token = jnp.sum(parts[:, 2 * rows : 3 * rows], axis=0, keepdims=True) - normalizer
        values = jnp.where(near == parity, guided[...], received[...])
        results.append(jnp.where(allowed_entries(blocks, parity, width), values - to_column(normalizer), 0.0))
        spot = (count, 2 * count)
        here = lax.broadcasted_iota(jnp.int32, spot, 1) == 2 * lax.broadcasted_iota(jnp.int32, spot, 0) + parity
        for step in range(DECODE_STEPS):
            mine = slice(step * count, (step + 1) * count)
            spread = jnp.sum(jnp.where(here, to_column(token[:, mine]), 0.0), axis=0, keepdims=True)
            token_rows[step] = token_rows[step] + spread
    for step in range(DECODE_STEPS):
        tokens[pl.ds(step, 1), :] = token_rows[step]
        for pair in range(count):
            row = step * count + pair
            for parity, result in enumerate(results):
                logprobs[step, pl.ds(2 * pair + parity, 1), :] = result[row : row + 1]


def slot_rows(array):
    slots = array.shape[0]
    split = array.reshape(slots, 2, KEY_VALUE_HEADS, HEAD_SIZE)
    return split.transpose(0, 2, 1, 3).reshape(slots * SLOT_ROWS, HEAD_SIZE)


def step_rows(array):
    split = array.reshape(DECODE_STEPS, QUERY_HEADS, HEAD_SIZE)
    return split.transpose(1, 0, 2).reshape(QUERY_HEADS * DECODE_STEPS, HEAD_SIZE)


def shards(
    wide,
    queries,
    cache,
    fresh_key_value,
    lengths,
    residual,
    norm_gain,
    vocab_weight,
    guidance,
    allowed_blocks,
    sampled,
):
    steps, half_pairs, blocks_here = allowed_blocks.shape
    width = vocab_weight.shape[1]
    pairs = guidance.shape[0]
    rows = steps * QUERY_HEADS
    cache_rows = slot_rows(cache[0, 0])
    vmem, smem, hbm = in_vmem(), in_smem(), pl.BlockSpec(memory_space=pltpu.HBM)
    half_rows = jax.ShapeDtypeStruct((rows // 2, HEAD_SIZE), jnp.bfloat16)
    chips = wide // 2
    flat = jax.ShapeDtypeStruct((steps * chips // 2, width), jnp.float32)
    flat_two = jax.ShapeDtypeStruct((steps * chips // 2, 2 * width), jnp.float32)

    def other_core(array):
        return lax.ppermute(array, "wide", [(source, source ^ 1) for source in range(wide)])

    def swap(array):
        return lax.ppermute(array, "pair", [(0, 1), (1, 0)])

    mine, theirs = call(
        attend_kernel,
        (pltpu.VMEM(half_rows.shape, half_rows.dtype), pltpu.VMEM(half_rows.shape, half_rows.dtype)),
        [smem] + [hbm] * 5,
        [
            pltpu.VMEM(cache_rows.shape, jnp.bfloat16),
            pltpu.VMEM((cache.shape[2] * SLOT_PITCH, HEAD_SIZE), jnp.float32),
            pltpu.VMEM((rows, HEAD_SIZE), jnp.float32),
            pltpu.VMEM((rows, HEAD_SIZE), jnp.float32),
            pltpu.VMEM((rows, HEAD_SIZE), jnp.bfloat16),
            pltpu.VMEM((steps * SLOT_ROWS, HEAD_SIZE), jnp.bfloat16),
            pltpu.VMEM((rows, HEAD_SIZE), jnp.bfloat16),
            pltpu.VMEM((QUERY_HEADS, HEAD_SIZE), jnp.float32),
            pltpu.SemaphoreType.DMA((cache.shape[2] // BLOCK + 4,)),
        ],
        limit=58 << 20,
    )(
        lengths,
        step_rows(queries[0, 0]),
        cache_rows,
        slot_rows(fresh_key_value[0, 0]),
        step_rows(residual[0, 0]),
        norm_gain.reshape(QUERY_HEADS, HEAD_SIZE),
    )
    received = swap(theirs)
    own_part, factor = call(
        own_part_kernel,
        (jax.ShapeDtypeStruct(half_rows.shape, jnp.float32), jax.ShapeDtypeStruct((8, HEAD_SIZE), jnp.float32)),
        [smem, vmem],
    )(guidance, mine)
    other_weight, other_blocks = other_core(vocab_weight), other_core(allowed_blocks)
    spread = call(combine_kernel, jax.ShapeDtypeStruct((chips,) + half_rows.shape, jnp.bfloat16), [vmem] * 3)(
        factor, own_part, received
    )
    same_core = [list(range(core, wide, 2)) for core in range(2)]
    gathered = lax.all_to_all(spread, "wide", 0, 0, axis_index_groups=same_core, tiled=True)
    mine, theirs = call(
        project_kernel,
        (flat_two, flat_two),
        [vmem] * 3,
        [pltpu.VMEM((chips * (rows // 2 + 1), HEAD_SIZE), jnp.float32)],
    )(gathered, vocab_weight, other_weight)
    lanes = pl.cdiv(3 * steps * chips // 2, 128) * 128
    guided, other_guided, stats = call(
        stats_kernel,
        (flat, flat, jax.ShapeDtypeStruct((wide, 1, lanes), jnp.float32)),
        [vmem] * 5,
    )(mine, swap(theirs), allowed_blocks, other_blocks, sampled)
    other_guided = other_core(other_guided)
    logprobs, tokens = call(
        finish_kernel,
        (
            jax.ShapeDtypeStruct((steps, half_pairs, width), jnp.float32),
            jax.ShapeDtypeStruct((steps, half_pairs), jnp.float32),
        ),
        [vmem] * 4,
    )(guided, other_guided, lax.all_to_all(stats, "wide", 0, 0, tiled=True), allowed_blocks)
    return (logprobs, tokens)


def solution(mesh):
    placed = (
        P("pair", "wide", None, None),
        P("pair", "wide", None, None, None),
        P("pair", "wide", None, None, None),
        P("pair", "wide"),
        P("pair", "wide", None, None),
        P(),
        P("pair", "wide"),
        P(),
        P(None, "pair", "wide"),
        P(None, "pair"),
    )
    return jax.shard_map(
        functools.partial(shards, mesh.shape["wide"]),
        mesh=mesh,
        in_specs=placed,
        out_specs=(P(None, "pair", "wide"), P(None, "pair")),
        check_vma=False,
    )
```

```python
import functools
import math

import jax
import jax.numpy as jnp
from jax import lax
from jax.experimental import pallas as pl
from jax.experimental.pallas import tpu as pltpu
from jax.sharding import PartitionSpec as P

QUERY_HEADS = 64
KEY_VALUE_HEADS = 8
HEAD_SIZE = 128
BLK = 32
DECODE_STEPS = 2
SLOT_ROWS = 2 * KEY_VALUE_HEADS
SLOT_PITCH = SLOT_ROWS + 1
BLOCK = 64
HEAD_ROWS = DECODE_STEPS * (QUERY_HEADS // KEY_VALUE_HEADS)
NEG_FILL = -1e30


def in_vmem():
    return pl.BlockSpec(memory_space=pltpu.VMEM)


def in_smem():
    return pl.BlockSpec(memory_space=pltpu.SMEM)


def call(kernel, out_shape, in_specs, scratch=(), limit=16 << 20, cost=None):
    return pl.pallas_call(
        kernel,
        out_shape=out_shape,
        in_specs=in_specs,
        out_specs=jax.tree.map(lambda _: in_vmem(), out_shape, is_leaf=lambda x: hasattr(x, 'shape')),
        scratch_shapes=list(scratch),
        compiler_params=pltpu.CompilerParams(vmem_limit_bytes=limit),
        cost_estimate=cost,
    )


def attend_kernel(
    lengths, queries_in, cache, fresh_in, residual_in, gain_in, mine, theirs,
    stage, wide_rows, mixed, gain_rows, queries, fresh, residual, gain, arrived,
):
    rows = cache.shape[0]
    slots = rows // SLOT_ROWS

    def block_copy(block):
        at = pl.ds(pl.multiple_of(block * (BLOCK * SLOT_ROWS), BLOCK * SLOT_ROWS), BLOCK * SLOT_ROWS)
        return pltpu.make_async_copy(cache.at[at], stage.at[at], arrived.at[block])

    def start(block, carry):
        block_copy(block).start()
        return carry

    def clear(block, carry):
        target = pl.multiple_of(block * (BLOCK * SLOT_PITCH), 8)
        wide_rows[pl.ds(target, BLOCK * SLOT_PITCH), :] = jnp.zeros((BLOCK * SLOT_PITCH, HEAD_SIZE), jnp.float32)
        return carry

    def widen(block, carry):
        block_copy(block).wait()
        source = pl.multiple_of(block * (BLOCK * SLOT_ROWS), BLOCK * SLOT_ROWS)
        target = pl.multiple_of(block * (BLOCK * SLOT_PITCH), 8)
        for slot in range(BLOCK):
            wide_rows[pl.ds(target + slot * SLOT_PITCH, SLOT_ROWS), :] = stage[
                pl.ds(source + slot * SLOT_ROWS, SLOT_ROWS), :
            ].astype(jnp.float32)
        return carry

    blocks = slots // BLOCK
    live_blocks = lax.div(lengths[0, 0] + (BLOCK - 1), BLOCK)
    lax.fori_loop(0, live_blocks, start, 0)
    small = [
        pltpu.make_async_copy(source, target, arrived.at[blocks + index])
        for index, (source, target) in enumerate(
            ((gain_in, gain), (fresh_in, fresh), (queries_in, queries), (residual_in, residual))
        )
    ]
    for copy in small:
        copy.start()
    sizes = [slots // 4, slots // 2, slots]
    fits = [lengths[0, 0] <= size - DECODE_STEPS for size in sizes[:-1]]
    used_blocks = jnp.where(fits[0], sizes[0] // BLOCK, jnp.where(fits[1], sizes[1] // BLOCK, blocks))
    lax.fori_loop(live_blocks, used_blocks, clear, 0)
    lax.fori_loop(0, live_blocks, widen, 0)
    for copy in small:
        copy.wait()
    gain_rows[pl.ds(0, QUERY_HEADS, stride=2), :] = gain[...]
    gain_rows[pl.ds(1, QUERY_HEADS, stride=2), :] = gain[...]
    factor = 1.0 / math.sqrt(HEAD_SIZE)

    def attend(count):
        first_fresh = count - DECODE_STEPS
        for step in range(DECODE_STEPS):
            wide_rows[pl.ds((first_fresh + step) * SLOT_PITCH, SLOT_ROWS), :] = fresh[
                pl.ds(step * SLOT_ROWS, SLOT_ROWS), :
            ].astype(jnp.float32)
        scores = []
        for head in range(KEY_VALUE_HEADS):
            keys = wide_rows[pl.ds(2 * head, count, stride=SLOT_PITCH), :].astype(jnp.bfloat16)
            scores.append(
                lax.dot_general(
                    queries[pl.ds(head * HEAD_ROWS, HEAD_ROWS), :],
                    keys,
                    (((1,), (1,)), ((), ())),
                    preferred_element_type=jnp.float32,
                )
            )
        score = jnp.concatenate(scores, axis=0)
        slot = lax.broadcasted_iota(jnp.int32, score.shape, 1)
        step_of_row = lax.rem(lax.broadcasted_iota(jnp.int32, score.shape, 0), DECODE_STEPS)
        live = (slot < lengths[0, 0]) | ((slot >= first_fresh) & (slot - first_fresh <= step_of_row))
        score = jnp.where(live, score * factor, NEG_FILL)
        weight = jnp.exp(score - jnp.max(score, axis=1, keepdims=True))
        weight = (weight / jnp.sum(weight, axis=1, keepdims=True)).astype(jnp.bfloat16)
        for head in range(KEY_VALUE_HEADS):
            values = wide_rows[pl.ds(2 * head + 1, count, stride=SLOT_PITCH), :].astype(jnp.bfloat16)
            mixed[pl.ds(head * HEAD_ROWS, HEAD_ROWS), :] = jnp.dot(
                weight[head * HEAD_ROWS : (head + 1) * HEAD_ROWS], values, preferred_element_type=jnp.float32
            )

    pl.when(fits[0])(lambda: attend(sizes[0]))
    pl.when(jnp.logical_not(fits[0]) & fits[1])(lambda: attend(sizes[1]))
    pl.when(jnp.logical_not(fits[1]))(lambda: attend(sizes[2]))
    hidden = mixed[...] + residual[...].astype(jnp.float32)
    row_power = jnp.sum(hidden * hidden, axis=1, keepdims=True)
    step_of_row = lax.rem(lax.broadcasted_iota(jnp.int32, row_power.shape, 0), DECODE_STEPS)
    scale = jnp.zeros_like(row_power)
    for step in range(DECODE_STEPS):
        power = jnp.sum(jnp.where(step_of_row == step, row_power, 0.0), axis=0, keepdims=True)
        power = power / (QUERY_HEADS * HEAD_SIZE)
        scale = jnp.where(step_of_row == step, lax.rsqrt(power + 1e-05), scale)
    normed = (hidden * scale * gain_rows[...]).astype(jnp.bfloat16)
    half = normed.shape[0] // 2
    first = lax.axis_index("pair") == 0
    mine[...] = jnp.where(first, normed[:half], normed[half:])
    theirs[...] = jnp.where(first, normed[half:], normed[:half])


def branch_factor(scale, branch):
    guidance = scale[lax.axis_index("wide")]
    return jnp.where(branch == 0, guidance, 1.0 - guidance)


def own_part_kernel(scale, mine, out, factor):
    branch = lax.axis_index("pair")
    out[...] = branch_factor(scale, branch) * mine[...].astype(jnp.float32)
    factor[...] = jnp.full(factor.shape, branch_factor(scale, 1 - branch), jnp.float32)


def combine_kernel(factor, own_part, received, spread):
    other_part = factor[0:1, :] * received[...].astype(jnp.float32)
    guided = (own_part[...] + other_part).astype(jnp.bfloat16)
    spread[...] = jnp.broadcast_to(guided[None], spread.shape)


def project_kernel(rows, weight, other_weight, mine, theirs, wide_rows):
    pairs, per_pair, lanes = rows.shape
    half = pairs // 2
    pitch = per_pair + 1
    for pair in range(pairs):
        wide_rows[pl.ds(pair * pitch, per_pair), :] = rows[pair].astype(jnp.float32)

    def head_rows(head):
        steps = [
            wide_rows[pl.ds(head * DECODE_STEPS + step, pairs, stride=pitch), :] for step in range(DECODE_STEPS)
        ]
        return jnp.concatenate(steps, axis=0).astype(jnp.bfloat16)

    totals = [jnp.zeros((DECODE_STEPS * pairs, weight.shape[1]), jnp.float32)] * 2
    for two in range(per_pair // DECODE_STEPS // 2):
        left = jnp.concatenate([head_rows(2 * two), head_rows(2 * two + 1)], axis=1)
        totals = [
            total + jnp.dot(left, part[pl.ds(two * 2 * lanes, 2 * lanes), :], preferred_element_type=jnp.float32)
            for total, part in zip(totals, (weight, other_weight))
        ]
    total = jnp.concatenate(totals, axis=1)
    low, high = (
        jnp.concatenate(
            [total[step * pairs + part * half : step * pairs + (part + 1) * half] for step in range(DECODE_STEPS)],
            axis=0,
        )
        for part in range(2)
    )
    first = lax.axis_index("pair") == 0
    mine[...] = jnp.where(first, low, high)
    theirs[...] = jnp.where(first, high, low)


def to_lanes(column):
    size = column.shape[0]
    eye = lax.broadcasted_iota(jnp.int32, (size, size), 0) == lax.broadcasted_iota(jnp.int32, (size, size), 1)
    return jnp.sum(jnp.where(eye, column, jnp.zeros_like(column)), axis=0, keepdims=True)


def to_column(lanes):
    size = lanes.shape[1]
    eye = lax.broadcasted_iota(jnp.int32, (size, size), 0) == lax.broadcasted_iota(jnp.int32, (size, size), 1)
    return jnp.sum(jnp.where(eye, lanes, jnp.zeros_like(lanes)), axis=1, keepdims=True)


def allowed_entries(blocks, parity, width):
    count = blocks.shape[1] // 2
    flags = jnp.concatenate(
        [blocks[step, pl.ds(2 * pair + parity, 1), :] for step in range(DECODE_STEPS) for pair in range(count)], axis=0
    )
    block = lax.broadcasted_iota(jnp.int32, (flags.shape[0], width), 1) // BLK
    flag = jnp.zeros(block.shape, jnp.int32)
    for index in range(blocks.shape[2]):
        flag = jnp.where(block == index, flags[:, index : index + 1], flag)
    return flag > 0


def stats_kernel(mine, received, blocks, other_blocks, sampled, guided_out, other_out, stats):
    guided = mine[...] + received[...]
    rows, both = guided.shape
    width = both // 2
    guided_out[...] = guided[:, :width]
    other_out[...] = guided[:, width:]
    position = lax.axis_index("wide")
    parity = position % 2
    allowed = jnp.concatenate(
        [
            jnp.where(parity == 0, *(allowed_entries(part, q, width).astype(jnp.int32) for q in range(2)))
            for part in (blocks, other_blocks)
        ],
        axis=1,
    ) > 0
    top = jnp.max(jnp.where(allowed, guided, NEG_FILL), axis=1, keepdims=True)
    total = jnp.sum(jnp.where(allowed, jnp.exp(guided - top), 0.0), axis=1, keepdims=True)
    count = rows // DECODE_STEPS
    spot = (count, 2 * count)
    of_parity = lax.broadcasted_iota(jnp.int32, spot, 1) == 2 * lax.broadcasted_iota(jnp.int32, spot, 0) + parity
    chosen = jnp.concatenate(
        [
            jnp.sum(jnp.where(of_parity, sampled[pl.ds(step, 1), :], 0), axis=1, keepdims=True)
            for step in range(DECODE_STEPS)
        ],
        axis=0,
    )
    lane = lax.broadcasted_iota(jnp.int32, guided.shape, 1)
    column = jnp.where(lane < width, position * width + lane, (position ^ 1) * width + lane - width)
    picked = jnp.sum(jnp.where(column == chosen, guided, 0.0), axis=1, keepdims=True)
    stats[...] = jnp.broadcast_to(
        jnp.concatenate([to_lanes(top), to_lanes(total), to_lanes(picked)], axis=0)[None], stats.shape
    )


def finish_kernel(guided, received, stats, blocks, logprobs, tokens):
    rows, width = guided.shape
    count = rows // DECODE_STEPS
    chips = stats.shape[0] // 2
    near = lax.axis_index("wide") % 2
    token_rows = [jnp.zeros((1, 2 * count), jnp.float32)] * DECODE_STEPS
    results = []
    for parity in range(2):
        parts = [stats[2 * chip + parity] for chip in range(chips)]
        top = functools.reduce(jnp.maximum, [part[0:1] for part in parts])
        total = sum(part[1:2] * jnp.exp(part[0:1] - top) for part in parts)
        normalizer = top + jnp.log(total)
        token = sum(part[2:3] for part in parts) - normalizer
        values = jnp.where(near == parity, guided[...], received[...])
        results.append(jnp.where(allowed_entries(blocks, parity, width), values - to_column(normalizer), 0.0))
        spot = (count, 2 * count)
        here = lax.broadcasted_iota(jnp.int32, spot, 1) == 2 * lax.broadcasted_iota(jnp.int32, spot, 0) + parity
        for step in range(DECODE_STEPS):
            mine = slice(step * count, (step + 1) * count)
            spread = jnp.sum(jnp.where(here, to_column(token[:, mine]), 0.0), axis=0, keepdims=True)
            token_rows[step] = token_rows[step] + spread
    for step in range(DECODE_STEPS):
        tokens[pl.ds(step, 1), :] = token_rows[step]
        for pair in range(count):
            row = step * count + pair
            for parity, result in enumerate(results):
                logprobs[step, pl.ds(2 * pair + parity, 1), :] = result[row : row + 1]


def slot_rows(array):
    slots = array.shape[0]
    split = array.reshape(slots, 2, KEY_VALUE_HEADS, HEAD_SIZE)
    return split.transpose(0, 2, 1, 3).reshape(slots * SLOT_ROWS, HEAD_SIZE)


def step_rows(array):
    split = array.reshape(DECODE_STEPS, QUERY_HEADS, HEAD_SIZE)
    return split.transpose(1, 0, 2).reshape(QUERY_HEADS * DECODE_STEPS, HEAD_SIZE)


def shards(
    wide,
    queries,
    cache,
    fresh_key_value,
    lengths,
    residual,
    norm_gain,
    vocab_weight,
    guidance,
    allowed_blocks,
    sampled,
):
    steps, half_pairs, blocks_here = allowed_blocks.shape
    width = vocab_weight.shape[1]
    pairs = guidance.shape[0]
    rows = steps * QUERY_HEADS
    cache_rows = slot_rows(cache[0, 0])
    vmem, smem, hbm = in_vmem(), in_smem(), pl.BlockSpec(memory_space=pltpu.HBM)
    half_rows = jax.ShapeDtypeStruct((rows // 2, HEAD_SIZE), jnp.bfloat16)
    chips = wide // 2
    flat = jax.ShapeDtypeStruct((steps * chips // 2, width), jnp.float32)
    flat_two = jax.ShapeDtypeStruct((steps * chips // 2, 2 * width), jnp.float32)

    def other_core(array):
        return lax.ppermute(array, "wide", [(source, source ^ 1) for source in range(wide)])

    def swap(array):
        return lax.ppermute(array, "pair", [(0, 1), (1, 0)])

    mine, theirs = call(
        attend_kernel,
        (pltpu.VMEM(half_rows.shape, half_rows.dtype), pltpu.VMEM(half_rows.shape, half_rows.dtype)),
        [smem] + [hbm] * 5,
        [
            pltpu.VMEM(cache_rows.shape, jnp.bfloat16),
            pltpu.VMEM((cache.shape[2] * SLOT_PITCH, HEAD_SIZE), jnp.float32),
            pltpu.VMEM((rows, HEAD_SIZE), jnp.float32),
            pltpu.VMEM((rows, HEAD_SIZE), jnp.float32),
            pltpu.VMEM((rows, HEAD_SIZE), jnp.bfloat16),
            pltpu.VMEM((steps * SLOT_ROWS, HEAD_SIZE), jnp.bfloat16),
            pltpu.VMEM((rows, HEAD_SIZE), jnp.bfloat16),
            pltpu.VMEM((QUERY_HEADS, HEAD_SIZE), jnp.float32),
            pltpu.SemaphoreType.DMA((cache.shape[2] // BLOCK + 4,)),
        ],
        limit=58 << 20,
    )(
        lengths,
        step_rows(queries[0, 0]),
        cache_rows,
        slot_rows(fresh_key_value[0, 0]),
        step_rows(residual[0, 0]),
        norm_gain.reshape(QUERY_HEADS, HEAD_SIZE),
    )
    received = swap(theirs)
    own_part, factor = call(
        own_part_kernel,
        (jax.ShapeDtypeStruct(half_rows.shape, jnp.float32), jax.ShapeDtypeStruct((8, HEAD_SIZE), jnp.float32)),
        [smem, vmem],
    )(guidance, mine)
    other_weight, other_blocks = other_core(vocab_weight), other_core(allowed_blocks)
    spread = call(combine_kernel, jax.ShapeDtypeStruct((chips,) + half_rows.shape, jnp.bfloat16), [vmem] * 3)(
        factor, own_part, received
    )
    same_core = [list(range(core, wide, 2)) for core in range(2)]
    gathered = lax.all_to_all(spread, "wide", 0, 0, axis_index_groups=same_core, tiled=True)
    mine, theirs = call(
        project_kernel,
        (flat_two, flat_two),
        [vmem] * 3,
        [pltpu.VMEM((chips * (rows // 2 + 1), HEAD_SIZE), jnp.float32)],
    )(gathered, vocab_weight, other_weight)
    guided, other_guided, stats = call(
        stats_kernel,
        (flat, flat, jax.ShapeDtypeStruct((wide, 3, steps * chips // 2), jnp.float32)),
        [vmem] * 5,
    )(mine, swap(theirs), allowed_blocks, other_blocks, sampled)
    other_guided = other_core(other_guided)
    logprobs, tokens = call(
        finish_kernel,
        (
            jax.ShapeDtypeStruct((steps, half_pairs, width), jnp.float32),
            jax.ShapeDtypeStruct((steps, half_pairs), jnp.float32),
        ),
        [vmem] * 4,
    )(guided, other_guided, lax.all_to_all(stats, "wide", 0, 0, tiled=True), allowed_blocks)
    return (logprobs, tokens)


def solution(mesh):
    placed = (
        P("pair", "wide", None, None),
        P("pair", "wide", None, None, None),
        P("pair", "wide", None, None, None),
        P("pair", "wide"),
        P("pair", "wide", None, None),
        P(),
        P("pair", "wide"),
        P(),
        P(None, "pair", "wide"),
        P(None, "pair"),
    )
    return jax.shard_map(
        functools.partial(shards, mesh.shape["wide"]),
        mesh=mesh,
        in_specs=placed,
        out_specs=(P(None, "pair", "wide"), P(None, "pair")),
        check_vma=False,
    )
```

```python
import functools
import math

import jax
import jax.numpy as jnp
from jax import lax
from jax.experimental import pallas as pl
from jax.experimental.pallas import tpu as pltpu
from jax.sharding import PartitionSpec as P

QUERY_HEADS = 64
KEY_VALUE_HEADS = 8
HEAD_SIZE = 128
BLK = 32
DECODE_STEPS = 2
SLOT_ROWS = 2 * KEY_VALUE_HEADS
SLOT_PITCH = SLOT_ROWS + 1
BLOCK = 64
HEAD_ROWS = DECODE_STEPS * (QUERY_HEADS // KEY_VALUE_HEADS)
NEG_FILL = -1e30


def in_vmem():
    return pl.BlockSpec(memory_space=pltpu.VMEM)


def in_smem():
    return pl.BlockSpec(memory_space=pltpu.SMEM)


def call(kernel, out_shape, in_specs, scratch=(), limit=16 << 20, cost=None):
    return pl.pallas_call(
        kernel,
        out_shape=out_shape,
        in_specs=in_specs,
        out_specs=jax.tree.map(lambda _: in_vmem(), out_shape, is_leaf=lambda x: hasattr(x, 'shape')),
        scratch_shapes=list(scratch),
        compiler_params=pltpu.CompilerParams(vmem_limit_bytes=limit),
        cost_estimate=cost,
    )


def attend_kernel(
    lengths, queries_in, cache, fresh_in, residual_in, gain_in, mine, theirs,
    stage, wide_rows, gain_rows, queries, fresh, residual, gain, arrived,
):
    rows = cache.shape[0]
    slots = rows // SLOT_ROWS

    def block_copy(block):
        at = pl.ds(pl.multiple_of(block * (BLOCK * SLOT_ROWS), BLOCK * SLOT_ROWS), BLOCK * SLOT_ROWS)
        return pltpu.make_async_copy(cache.at[at], stage.at[at], arrived.at[block])

    def start(block, carry):
        block_copy(block).start()
        return carry

    def clear(block, carry):
        target = pl.multiple_of(block * (BLOCK * SLOT_PITCH), 8)
        wide_rows[pl.ds(target, BLOCK * SLOT_PITCH), :] = jnp.zeros((BLOCK * SLOT_PITCH, HEAD_SIZE), jnp.float32)
        return carry

    def widen(block, carry):
        block_copy(block).wait()
        source = pl.multiple_of(block * (BLOCK * SLOT_ROWS), BLOCK * SLOT_ROWS)
        target = pl.multiple_of(block * (BLOCK * SLOT_PITCH), 8)
        for slot in range(BLOCK):
            wide_rows[pl.ds(target + slot * SLOT_PITCH, SLOT_ROWS), :] = stage[
                pl.ds(source + slot * SLOT_ROWS, SLOT_ROWS), :
            ].astype(jnp.float32)
        return carry

    blocks = slots // BLOCK
    live_blocks = lax.div(lengths[0, 0] + (BLOCK - 1), BLOCK)
    lax.fori_loop(0, live_blocks, start, 0)
    small = [
        pltpu.make_async_copy(source, target, arrived.at[blocks + index])
        for index, (source, target) in enumerate(
            ((gain_in, gain), (fresh_in, fresh), (queries_in, queries), (residual_in, residual))
        )
    ]
    for copy in small:
        copy.start()
    lax.fori_loop(live_blocks, blocks, clear, 0)
    lax.fori_loop(0, live_blocks, widen, 0)
    for copy in small:
        copy.wait()
    gain_rows[pl.ds(0, QUERY_HEADS, stride=2), :] = gain[...]
    gain_rows[pl.ds(1, QUERY_HEADS, stride=2), :] = gain[...]
    for step in range(DECODE_STEPS):
        wide_rows[pl.ds((slots - DECODE_STEPS + step) * SLOT_PITCH, SLOT_ROWS), :] = fresh[
            pl.ds(step * SLOT_ROWS, SLOT_ROWS), :
        ].astype(jnp.float32)
    factor = 1.0 / math.sqrt(HEAD_SIZE)
    scores = []
    for head in range(KEY_VALUE_HEADS):
        keys = wide_rows[pl.ds(2 * head, slots, stride=SLOT_PITCH), :].astype(jnp.bfloat16)
        scores.append(
            lax.dot_general(
                queries[pl.ds(head * HEAD_ROWS, HEAD_ROWS), :],
                keys,
                (((1,), (1,)), ((), ())),
                preferred_element_type=jnp.float32,
            )
        )
    score = jnp.concatenate(scores, axis=0)
    slot = lax.broadcasted_iota(jnp.int32, score.shape, 1)
    step_of_row = lax.rem(lax.broadcasted_iota(jnp.int32, score.shape, 0), DECODE_STEPS)
    first_fresh = slots - DECODE_STEPS
    live = (slot < lengths[0, 0]) | ((slot >= first_fresh) & (slot - first_fresh <= step_of_row))
    score = jnp.where(live, score * factor, NEG_FILL)
    weight = jnp.exp(score - jnp.max(score, axis=1, keepdims=True))
    weight = (weight / jnp.sum(weight, axis=1, keepdims=True)).astype(jnp.bfloat16)
    mixed = []
    for head in range(KEY_VALUE_HEADS):
        values = wide_rows[pl.ds(2 * head + 1, slots, stride=SLOT_PITCH), :].astype(jnp.bfloat16)
        mixed.append(
            jnp.dot(
                weight[head * HEAD_ROWS : (head + 1) * HEAD_ROWS], values, preferred_element_type=jnp.float32
            )
        )
    hidden = jnp.concatenate(mixed, axis=0) + residual[...].astype(jnp.float32)
    row_power = jnp.sum(hidden * hidden, axis=1, keepdims=True)
    step_of_row = lax.rem(lax.broadcasted_iota(jnp.int32, row_power.shape, 0), DECODE_STEPS)
    scale = jnp.zeros_like(row_power)
    for step in range(DECODE_STEPS):
        power = jnp.sum(jnp.where(step_of_row == step, row_power, 0.0), axis=0, keepdims=True)
        power = power / (QUERY_HEADS * HEAD_SIZE)
        scale = jnp.where(step_of_row == step, lax.rsqrt(power + 1e-05), scale)
    normed = (hidden * scale * gain_rows[pl.ds(0, hidden.shape[0]), :]).astype(jnp.bfloat16)
    half = normed.shape[0] // 2
    first = lax.axis_index("pair") == 0
    mine[...] = jnp.where(first, normed[:half], normed[half:])
    theirs[...] = jnp.where(first, normed[half:], normed[:half])


def branch_factor(scale, branch):
    guidance = scale[lax.axis_index("wide")]
    return jnp.where(branch == 0, guidance, 1.0 - guidance)


def own_part_kernel(scale, mine, out, factor):
    branch = lax.axis_index("pair")
    out[...] = branch_factor(scale, branch) * mine[...].astype(jnp.float32)
    factor[...] = jnp.full(factor.shape, branch_factor(scale, 1 - branch), jnp.float32)


def combine_kernel(factor, own_part, received, spread):
    other_part = factor[0:1, :] * received[...].astype(jnp.float32)
    guided = (own_part[...] + other_part).astype(jnp.bfloat16)
    spread[...] = jnp.broadcast_to(guided[None], spread.shape)


def project_kernel(rows, weight, other_weight, mine, theirs, wide_rows):
    pairs, per_pair, lanes = rows.shape
    half = pairs // 2
    pitch = per_pair + 1
    for pair in range(pairs):
        wide_rows[pl.ds(pair * pitch, per_pair), :] = rows[pair].astype(jnp.float32)

    def head_rows(head):
        steps = [
            wide_rows[pl.ds(head * DECODE_STEPS + step, pairs, stride=pitch), :] for step in range(DECODE_STEPS)
        ]
        return jnp.concatenate(steps, axis=0).astype(jnp.bfloat16)

    totals = [jnp.zeros((DECODE_STEPS * pairs, weight.shape[1]), jnp.float32)] * 2
    for two in range(per_pair // DECODE_STEPS // 2):
        left = jnp.concatenate([head_rows(2 * two), head_rows(2 * two + 1)], axis=1)
        totals = [
            total + jnp.dot(left, part[pl.ds(two * 2 * lanes, 2 * lanes), :], preferred_element_type=jnp.float32)
            for total, part in zip(totals, (weight, other_weight))
        ]
    total = jnp.concatenate(totals, axis=1)
    low, high = (
        jnp.concatenate(
            [total[step * pairs + part * half : step * pairs + (part + 1) * half] for step in range(DECODE_STEPS)],
            axis=0,
        )
        for part in range(2)
    )
    first = lax.axis_index("pair") == 0
    mine[...] = jnp.where(first, low, high)
    theirs[...] = jnp.where(first, high, low)


def to_lanes(column):
    size = column.shape[0]
    eye = lax.broadcasted_iota(jnp.int32, (size, size), 0) == lax.broadcasted_iota(jnp.int32, (size, size), 1)
    return jnp.sum(jnp.where(eye, column, jnp.zeros_like(column)), axis=0, keepdims=True)


def to_column(lanes):
    size = lanes.shape[1]
    eye = lax.broadcasted_iota(jnp.int32, (size, size), 0) == lax.broadcasted_iota(jnp.int32, (size, size), 1)
    return jnp.sum(jnp.where(eye, lanes, jnp.zeros_like(lanes)), axis=1, keepdims=True)


def allowed_entries(blocks, parity, width):
    count = blocks.shape[1] // 2
    flags = jnp.concatenate(
        [blocks[step, pl.ds(2 * pair + parity, 1), :] for step in range(DECODE_STEPS) for pair in range(count)], axis=0
    )
    block = lax.broadcasted_iota(jnp.int32, (flags.shape[0], width), 1) // BLK
    flag = jnp.zeros(block.shape, jnp.int32)
    for index in range(blocks.shape[2]):
        flag = jnp.where(block == index, flags[:, index : index + 1], flag)
    return flag > 0


def stats_kernel(mine, received, blocks, other_blocks, sampled, guided_out, other_out, stats):
    guided = mine[...] + received[...]
    rows, both = guided.shape
    width = both // 2
    guided_out[...] = guided[:, :width]
    other_out[...] = guided[:, width:]
    position = lax.axis_index("wide")
    parity = position % 2
    allowed = jnp.concatenate(
        [
            jnp.where(parity == 0, *(allowed_entries(part, q, width).astype(jnp.int32) for q in range(2)))
            for part in (blocks, other_blocks)
        ],
        axis=1,
    ) > 0
    top = jnp.max(jnp.where(allowed, guided, NEG_FILL), axis=1, keepdims=True)
    total = jnp.sum(jnp.where(allowed, jnp.exp(guided - top), 0.0), axis=1, keepdims=True)
    count = rows // DECODE_STEPS
    spot = (count, 2 * count)
    of_parity = lax.broadcasted_iota(jnp.int32, spot, 1) == 2 * lax.broadcasted_iota(jnp.int32, spot, 0) + parity
    chosen = jnp.concatenate(
        [
            jnp.sum(jnp.where(of_parity, sampled[pl.ds(step, 1), :], 0), axis=1, keepdims=True)
            for step in range(DECODE_STEPS)
        ],
        axis=0,
    )
    lane = lax.broadcasted_iota(jnp.int32, guided.shape, 1)
    column = jnp.where(lane < width, position * width + lane, (position ^ 1) * width + lane - width)
    picked = jnp.sum(jnp.where(column == chosen, guided, 0.0), axis=1, keepdims=True)
    stats[...] = jnp.broadcast_to(
        jnp.concatenate([to_lanes(top), to_lanes(total), to_lanes(picked)], axis=0)[None], stats.shape
    )


def finish_kernel(guided, received, stats, blocks, logprobs, tokens):
    rows, width = guided.shape
    count = rows // DECODE_STEPS
    chips = stats.shape[0] // 2
    near = lax.axis_index("wide") % 2
    token_rows = [jnp.zeros((1, 2 * count), jnp.float32)] * DECODE_STEPS
    results = []
    for parity in range(2):
        parts = [stats[2 * chip + parity] for chip in range(chips)]
        top = functools.reduce(jnp.maximum, [part[0:1] for part in parts])
        total = sum(part[1:2] * jnp.exp(part[0:1] - top) for part in parts)
        normalizer = top + jnp.log(total)
        token = sum(part[2:3] for part in parts) - normalizer
        values = jnp.where(near == parity, guided[...], received[...])
        results.append(jnp.where(allowed_entries(blocks, parity, width), values - to_column(normalizer), 0.0))
        spot = (count, 2 * count)
        here = lax.broadcasted_iota(jnp.int32, spot, 1) == 2 * lax.broadcasted_iota(jnp.int32, spot, 0) + parity
        for step in range(DECODE_STEPS):
            mine = slice(step * count, (step + 1) * count)
            spread = jnp.sum(jnp.where(here, to_column(token[:, mine]), 0.0), axis=0, keepdims=True)
            token_rows[step] = token_rows[step] + spread
    for step in range(DECODE_STEPS):
        tokens[pl.ds(step, 1), :] = token_rows[step]
        for pair in range(count):
            row = step * count + pair
            for parity, result in enumerate(results):
                logprobs[step, pl.ds(2 * pair + parity, 1), :] = result[row : row + 1]


def slot_rows(array):
    slots = array.shape[0]
    split = array.reshape(slots, 2, KEY_VALUE_HEADS, HEAD_SIZE)
    return split.transpose(0, 2, 1, 3).reshape(slots * SLOT_ROWS, HEAD_SIZE)


def step_rows(array):
    split = array.reshape(DECODE_STEPS, QUERY_HEADS, HEAD_SIZE)
    return split.transpose(1, 0, 2).reshape(QUERY_HEADS * DECODE_STEPS, HEAD_SIZE)


def shards(
    wide,
    queries,
    cache,
    fresh_key_value,
    lengths,
    residual,
    norm_gain,
    vocab_weight,
    guidance,
    allowed_blocks,
    sampled,
):
    steps, half_pairs, blocks_here = allowed_blocks.shape
    width = vocab_weight.shape[1]
    pairs = guidance.shape[0]
    rows = steps * QUERY_HEADS
    cache_rows = slot_rows(cache[0, 0])
    vmem, smem, hbm = in_vmem(), in_smem(), pl.BlockSpec(memory_space=pltpu.HBM)
    half_rows = jax.ShapeDtypeStruct((rows // 2, HEAD_SIZE), jnp.bfloat16)
    chips = wide // 2
    flat = jax.ShapeDtypeStruct((steps * chips // 2, width), jnp.float32)
    flat_two = jax.ShapeDtypeStruct((steps * chips // 2, 2 * width), jnp.float32)

    def other_core(array):
        return lax.ppermute(array, "wide", [(source, source ^ 1) for source in range(wide)])

    def swap(array):
        return lax.ppermute(array, "pair", [(0, 1), (1, 0)])

    mine, theirs = call(
        attend_kernel,
        (pltpu.VMEM(half_rows.shape, half_rows.dtype), pltpu.VMEM(half_rows.shape, half_rows.dtype)),
        [smem] + [hbm] * 5,
        [
            pltpu.VMEM(cache_rows.shape, jnp.bfloat16),
            pltpu.VMEM(((cache.shape[2] + 8) * SLOT_PITCH, HEAD_SIZE), jnp.float32),
            pltpu.VMEM((rows + 8, HEAD_SIZE), jnp.float32),
            pltpu.VMEM((rows, HEAD_SIZE), jnp.bfloat16),
            pltpu.VMEM((steps * SLOT_ROWS, HEAD_SIZE), jnp.bfloat16),
            pltpu.VMEM((rows, HEAD_SIZE), jnp.bfloat16),
            pltpu.VMEM((QUERY_HEADS, HEAD_SIZE), jnp.float32),
            pltpu.SemaphoreType.DMA((cache.shape[2] // BLOCK + 4,)),
        ],
        limit=58 << 20,
    )(
        lengths,
        step_rows(queries[0, 0]),
        cache_rows,
        slot_rows(fresh_key_value[0, 0]),
        step_rows(residual[0, 0]),
        norm_gain.reshape(QUERY_HEADS, HEAD_SIZE),
    )
    received = swap(theirs)
    own_part, factor = call(
        own_part_kernel,
        (jax.ShapeDtypeStruct(half_rows.shape, jnp.float32), jax.ShapeDtypeStruct((8, HEAD_SIZE), jnp.float32)),
        [smem, vmem],
    )(guidance, mine)
    other_weight, other_blocks = other_core(vocab_weight), other_core(allowed_blocks)
    spread = call(combine_kernel, jax.ShapeDtypeStruct((chips,) + half_rows.shape, jnp.bfloat16), [vmem] * 3)(
        factor, own_part, received
    )
    same_core = [list(range(core, wide, 2)) for core in range(2)]
    gathered = lax.all_to_all(spread, "wide", 0, 0, axis_index_groups=same_core, tiled=True)
    mine, theirs = call(
        project_kernel,
        (flat_two, flat_two),
        [vmem] * 3,
        [pltpu.VMEM(((chips + 8) * (rows // 2 + 1), HEAD_SIZE), jnp.float32)],
    )(gathered, vocab_weight, other_weight)
    guided, other_guided, stats = call(
        stats_kernel,
        (flat, flat, jax.ShapeDtypeStruct((wide, 3, steps * chips // 2), jnp.float32)),
        [vmem] * 5,
    )(mine, swap(theirs), allowed_blocks, other_blocks, sampled)
    other_guided = other_core(other_guided)
    logprobs, tokens = call(
        finish_kernel,
        (
            jax.ShapeDtypeStruct((steps, half_pairs, width), jnp.float32),
            jax.ShapeDtypeStruct((steps, half_pairs), jnp.float32),
        ),
        [vmem] * 4,
    )(guided, other_guided, lax.all_to_all(stats, "wide", 0, 0, tiled=True), allowed_blocks)
    return (logprobs, tokens)


def solution(mesh):
    placed = (
        P("pair", "wide", None, None),
        P("pair", "wide", None, None, None),
        P("pair", "wide", None, None, None),
        P("pair", "wide"),
        P("pair", "wide", None, None),
        P(),
        P("pair", "wide"),
        P(),
        P(None, "pair", "wide"),
        P(None, "pair"),
    )
    return jax.shard_map(
        functools.partial(shards, mesh.shape["wide"]),
        mesh=mesh,
        in_specs=placed,
        out_specs=(P(None, "pair", "wide"), P(None, "pair")),
        check_vma=False,
    )
```
